1024 devices in a mesh: dp: 32 (over z_hi, x, y), fsdp: 32 (over z_lo, core).
Axes of the slice: x: 4, y: 4, z: 32 (z_hi: 2, z_lo: 16; z = z_hi * 16 + z_lo), core: 2. Of those that a mesh axis runs over, the one named last changes fastest.
Arguments:
- activations: bfloat16 [131072, 2560], P(('dp', 'fsdp')), may hold values from -0.09375 to 0.09375
- value_weight: bfloat16 [2560, 512], P('fsdp'), may hold values from -0.125 to 0.125
- queries: bfloat16 [196608, 2560], P(('dp', 'fsdp')), may hold values from -24 to 24
- key_rows: bfloat16 [196608, 512], P(('dp', 'fsdp')), may hold values from -8 to 8
- context_grad: bfloat16 [196608, 2560], P(('dp', 'fsdp')), may hold values from -6 to 6
- segment: int32 [131072], P(('dp', 'fsdp')), may hold values from 0 to 10, as said below
- send_slot: int32 [131072], P(('dp', 'fsdp')), may hold values from 0 to 191, as said below
Outputs:
- input_grad: bfloat16 [131072, 2560], P(('dp', 'fsdp'))
- weight_grad: bfloat16 [2560, 512], P('fsdp')
The draws below stay inside these ranges and needn't reach their ends.
Inputs may be any that keep to these rules, and one draw needn't show every extreme that they name: A token either keeps send_slot equal to its own position, or its whole response is sent: its tokens go in order to consecutive slots of one section's block, starting at that block's first slot. In each section, of every pair of devices whose dp indices differ by 32 / 2^(s+1) (same fsdp index), exactly one sends exactly one response of 16 to 32 tokens and the other sends none; the pair that holds dp index 0 sends a full 32. `segment`: never falls along one device's tokens; one id is one whole response.
All inputs are finite; a program needn't handle non-finite values.
Results may differ from the reference program's by a relative error of at most 0.015.
Values may be sent and summed in bfloat16 or wider, within the bound.
No kernel may reach another device: no remote copies, remote signals or barrier semaphores. Data moves between devices by JAX's collectives and lax.ppermute only.
A program may use at most 64 MiB of HBM per device.

```python
import math
import jax
import jax.numpy as jnp
from jax import lax

D = 2560
KVH = 4
GROUP = 5
HD = 128
TOK_DEV = 128
SECTIONS = 2
QH = 20
KVW = 512
CAP = 32
BUF = 192
TOKENS = 131072
SLOTS = 196608
N_DP = 32
N_FSDP = 32
DEVICES = 1024


def layout(key):
    keep_pieces = 9
    all_pieces = keep_pieces + 2

    def one_device(device):
        dp_index = device // N_FSDP
        fsdp_index = device % N_FSDP
        sent_lengths = []
        for section in range(2):
            mask = N_DP // 2 ** (section + 1)
            own_bit = dp_index // mask % 2
            pair_id = dp_index - own_bit * mask
            pair_key = jax.random.fold_in(jax.random.fold_in(jax.random.fold_in(key, 21 + section), pair_id), fsdp_index)
            key_side, key_size = jax.random.split(pair_key)
            sender_bit = jax.random.randint(key_side, (), 0, 2)
            length = jnp.where(pair_id == 0, CAP, jax.random.randint(key_size, (), CAP // 2, CAP + 1))
            sent_lengths.append(jnp.where(own_bit == sender_bit, length, 0).astype(jnp.int32))
        device_key = jax.random.fold_in(jax.random.fold_in(key, 13), device)
        key_len, key_shuffle = jax.random.split(device_key)
        kept_total = TOK_DEV - sent_lengths[0] - sent_lengths[1]
        drawn = jax.random.randint(key_len, (keep_pieces,), CAP // 2, 3 * CAP + 1)
        drawn_end = jnp.cumsum(drawn)
        drawn_start = drawn_end - drawn
        kept_len = jnp.minimum(jnp.maximum(kept_total - drawn_start, 0), drawn)
        lengths = jnp.concatenate([kept_len, jnp.stack(sent_lengths)]).astype(jnp.int32)
        targets = jnp.concatenate([jnp.full((keep_pieces,), -1, jnp.int32), jnp.arange(2, dtype=jnp.int32)])
        shuffle = jax.random.permutation(key_shuffle, all_pieces)
        lengths = lengths[shuffle]
        targets = targets[shuffle]
        piece_end = jnp.cumsum(lengths)
        piece_start = piece_end - lengths
        row_ids = jnp.arange(TOK_DEV, dtype=jnp.int32)
        piece_index = jnp.sum((piece_end[None, :] <= row_ids[:, None]).astype(jnp.int32), axis=1)
        rank_piece = jnp.cumsum((lengths > 0).astype(jnp.int32)) - 1
        last_piece = piece_index[TOK_DEV - 1]
        segment_ids = jnp.where(piece_index == last_piece, all_pieces - 1, rank_piece[piece_index])
        target_of = targets[piece_index]
        moved_slot = TOK_DEV + target_of * CAP + row_ids - piece_start[piece_index]
        slot_index = jnp.where(target_of < 0, row_ids, moved_slot)
        return (segment_ids.astype(jnp.int32), slot_index.astype(jnp.int32))
    segment_ids, slot_index = jax.vmap(one_device)(jnp.arange(DEVICES, dtype=jnp.int32))
    return (segment_ids.reshape(TOKENS), slot_index.reshape(TOKENS))


def draw_segment(key, part):
    segment_ids, slot_index = layout(key)
    return segment_ids


def draw_send_slot(key, part):
    segment_ids, slot_index = layout(key)
    return slot_index


def draw_queries(key, part):
    key = jax.random.fold_in(key, 1)
    key_one = jax.random.fold_in(key, 0)
    noise_base = jax.random.normal(key_one, (SLOTS, QH, HD), jnp.float32)
    return jnp.clip(noise_base, -24.0, 24.0).reshape(SLOTS, QH * HD).astype(jnp.bfloat16)


def draw_key_rows(key, part):
    key = jax.random.fold_in(key, 2)
    noise_base = jax.random.normal(key, (SLOTS, KVH, HD), jnp.float32)
    return jnp.clip(noise_base, -8.0, 8.0).reshape(SLOTS, KVH * HD).astype(jnp.bfloat16)


def strengthened(values, own_key, source, target, blocks, factor):
    owner, partner = [(jnp.arange(values.shape[axis_at]) // (values.shape[axis_at] // blocks)).reshape([-1 if axis == axis_at else 1 for axis in range(values.ndim)]) for axis_at in (source, target)]
    chosen = jax.random.permutation(own_key, blocks)[partner]
    strong = (owner == chosen) | (owner == (partner + blocks // 2) % blocks)
    return jnp.where(strong, factor * values, values)


def block_levels(own_key, dims, cuts, least, largest):
    loudness, own = 1.0, jax.random.fold_in(own_key, 6)
    for dim, blocks in cuts:
        draws = jnp.exp(jax.random.uniform(jax.random.fold_in(own, dim), (blocks,), jnp.float32, least / len(cuts), largest / len(cuts)))
        loudness = loudness * jnp.repeat(draws, dims[dim] // blocks).reshape([-1 if axis == dim else 1 for axis in range(len(dims))])
    return loudness


def scatter_about(stream_key, dims, scale, most, shards=(), kind=jnp.bfloat16):
    result = jax.random.normal(stream_key, dims, jnp.float32) * scale
    if len(shards) > 0:
        result = block_levels(stream_key, dims, shards, -0.22, 0.18) * result
    return jnp.clip(result, min=-most, max=most).astype(kind)


def heavy_noise(stream_key, dims, deviation, most, cuts, heavy, kind=jnp.bfloat16):
    values = deviation * jax.random.normal(stream_key, dims, jnp.float32)
    if cuts:
        values = values * block_levels(stream_key, dims, cuts, -0.22, 0.18)
    return jnp.clip(strengthened(values, jax.random.fold_in(stream_key, 3), *heavy), -most, most).astype(kind)


def setup_inputs(seed: int = 0) -> dict:
    key_list = jax.random.split(jax.random.key(seed), 8)
    return {
        "activations": heavy_noise(key_list[0], (TOKENS, D), 0.004, 0.09375, ((0, 1024),), (0, 1, 512, 6.0)),
        "value_weight": scatter_about(key_list[1], (D, KVW), D ** -0.5, 0.125, ((0, 32),)),
        "queries": draw_queries(jax.random.fold_in(key_list[7], 71), 0),
        "key_rows": draw_key_rows(jax.random.fold_in(key_list[7], 71), 0),
        "context_grad": scatter_about(key_list[4], (SLOTS, QH * HD), 1.0, 6.0, ((0, 1024),)),
        "segment": draw_segment(jax.random.fold_in(key_list[7], 71), 0),
        "send_slot": draw_send_slot(jax.random.fold_in(key_list[7], 71), 0),
    }


def attend_block(query_rows, key_rows, context_rows, block_segment):
    count = query_rows.shape[0]
    query_heads = query_rows.astype(jnp.float32).reshape(count, KVH, GROUP, HD)
    key_heads = key_rows.astype(jnp.float32).reshape(count, KVH, HD)
    scores = jnp.einsum('ikgd,jkd->kgij', query_heads, key_heads) / math.sqrt(HD)
    row_ids = jnp.arange(count, dtype=jnp.int32)
    allowed = (block_segment[:, None] == block_segment[None, :]) & (block_segment[:, None] >= 0)
    allowed = allowed & (row_ids[None, :] <= row_ids[:, None])
    allowed = allowed | (row_ids[:, None] == row_ids[None, :])
    masked = jnp.where(allowed, scores, -jnp.inf)
    highest = lax.optimization_barrier(jnp.max(masked, axis=-1, keepdims=True))
    exponent = jnp.where(allowed, jnp.exp(masked - highest), 0.0)
    attn_probs = (exponent / lax.optimization_barrier(jnp.sum(exponent, axis=-1, keepdims=True))).astype(jnp.bfloat16)
    context_heads = context_rows.astype(jnp.float32).reshape(count, KVH, GROUP, HD)
    gradient = jnp.einsum('kgij,ikgd->jkd', attn_probs.astype(jnp.float32), context_heads)
    return gradient.reshape(count, KVH * HD).astype(jnp.bfloat16)

def value_gradient(query_rows, key_rows, context_rows, slot_segment):
    pieces = [attend_block(query_rows[:TOK_DEV], key_rows[:TOK_DEV], context_rows[:TOK_DEV], slot_segment[:TOK_DEV])]
    for section in range(SECTIONS):
        low = TOK_DEV + section * CAP
        pieces.append(attend_block(query_rows[low:low + CAP], key_rows[low:low + CAP], context_rows[low:low + CAP], slot_segment[low:low + CAP]))
    return jnp.concatenate(pieces, axis=0)

def place_labels(labels, targets):
    return jnp.full((BUF,), -1, jnp.int32).at[targets].set(labels)

def take_rows(values, targets):
    return values[targets]

def regroup(own_side):
    dp_ids = jnp.arange(N_DP, dtype=jnp.int32)
    blocks = [own_side[:, :, :TOK_DEV]]
    for section in range(SECTIONS):
        partner = jnp.bitwise_xor(dp_ids, N_DP // 2 ** (section + 1))
        low = TOK_DEV + section * CAP
        blocks.append(own_side[partner][:, :, low:low + CAP])
    return jnp.concatenate(blocks, axis=2)

def reference(activations, value_weight, queries, key_rows, context_grad, segment, send_slot):
    seg_grid = segment.reshape(N_DP, N_FSDP, TOK_DEV)
    slot_grid = send_slot.reshape(N_DP, N_FSDP, TOK_DEV)
    sent_segment = jax.vmap(jax.vmap(place_labels))(seg_grid, slot_grid)
    slot_segment = regroup(sent_segment).reshape(DEVICES, BUF)
    stacked = (queries.reshape(DEVICES, BUF, QH * HD), key_rows.reshape(DEVICES, BUF, KVH * HD), context_grad.reshape(DEVICES, BUF, QH * HD), slot_segment)
    balanced = lax.map(lambda members: value_gradient(*members), stacked)
    returned = regroup(balanced.reshape(N_DP, N_FSDP, BUF, KVH * HD))
    row_grads = jax.vmap(jax.vmap(take_rows))(returned, slot_grid).reshape(DEVICES, TOK_DEV, KVH * HD)
    inputs = activations.reshape(DEVICES, TOK_DEV, D)

    def accumulate(running, members):
        rows_in, grads_in = members
        partial_sum = jnp.dot(rows_in.T, grads_in, preferred_element_type=jnp.float32)
        input_rows = jnp.dot(grads_in, value_weight.T, preferred_element_type=jnp.float32).astype(jnp.bfloat16)
        return (running + partial_sum, input_rows)
    grad_total, input_rows = lax.scan(accumulate, jnp.zeros((D, KVH * HD), jnp.float32), (inputs, row_grads))
    return (input_rows.reshape(TOKENS, D), grad_total.astype(jnp.bfloat16))
```

```python
import functools
import math

import jax
import jax.numpy as jnp
from jax import lax
from jax.experimental import pallas as pl
from jax.experimental.pallas import tpu as pltpu
from jax.sharding import PartitionSpec as P

KVH = 4
GROUP = 5
HD = 128
SECTIONS = 2
PLANE = 16
DEPTH = 16
ROWS = 24
CUTS = 4
BOTH = ("dp", "fsdp")
BF16 = jnp.bfloat16
F32 = jnp.float32


def swapped(block, axis, distance):
    route = [(low, low ^ distance) for low in range(lax.axis_size(axis))]
    return lax.ppermute(block, axis, route)


def after(value, *others):
    return lax.optimization_barrier((value, *others))[0]


def attend_part(q_ref, k_ref, c_ref, low, count, allowed):
    rows = slice(low, low + count)
    query = jnp.concatenate([q_ref[rows, g * HD : (g + 1) * HD] for g in range(GROUP)], axis=0)
    context = jnp.concatenate([c_ref[rows, g * HD : (g + 1) * HD] for g in range(GROUP)], axis=0)
    scores = lax.dot_general(
        k_ref[rows, :], query, (((1,), (1,)), ((), ())), preferred_element_type=F32
    ) * (1.0 / math.sqrt(HD))
    bias = jnp.where(allowed, 0.0, -jnp.inf)
    masked = scores + jnp.concatenate([bias] * GROUP, axis=1)
    exponent = jnp.exp(masked - jnp.max(masked, axis=0, keepdims=True))
    probs = exponent * (1.0 / jnp.sum(exponent, axis=0, keepdims=True))
    return jnp.dot(probs.astype(BF16), context, preferred_element_type=F32).astype(BF16)


def attend_kernel(tok, block, col_ref, row_ref, q_ref, k_ref, c_ref, out_ref):
    for low, count in ((0, tok), (tok, SECTIONS * block)):
        col = col_ref[low : low + count, :]
        row = row_ref[:, low : low + count]
        j = lax.broadcasted_iota(jnp.int32, (count, count), 0)
        i = lax.broadcasted_iota(jnp.int32, (count, count), 1)
        same = (col == row) & (row >= 0) & (j <= i)
        if low:
            same = same & ((j < block) == (i < block))
        out_ref[low : low + count, :] = attend_part(q_ref, k_ref, c_ref, low, count, same | (i == j))


def attend(queries, key_rows, context_grad, ids, tok, block):
    slots = queries.shape[0]
    wide = pl.BlockSpec((slots, GROUP * HD), lambda h: (0, h))
    thin = pl.BlockSpec((slots, HD), lambda h: (0, h))
    return pl.pallas_call(
        functools.partial(attend_kernel, tok, block),
        grid=(KVH,),
        in_specs=[
            pl.BlockSpec((slots, 1), lambda h: (0, 0)),
            pl.BlockSpec((1, slots), lambda h: (0, 0)),
            wide,
            thin,
            wide,
        ],
        out_specs=thin,
        out_shape=jax.ShapeDtypeStruct((slots, KVH * HD), BF16),
        name="attend",
    )(ids.reshape(slots, 1), ids.reshape(1, slots), queries, key_rows, context_grad)


def gradient_kernel(core_ref, slot_ref, main_ref, first_ref, second_ref, act_ref, rows_ref, keep_ref, send_ref, whole):
    tok = slot_ref.shape[0]

    @pl.when(pl.program_id(0) == 0)
    def _():
        held = jnp.concatenate([main_ref[...], first_ref[...], second_ref[...]], axis=0)
        slots = lax.broadcasted_iota(jnp.int32, (tok, held.shape[0]), 1)
        chosen = (slot_ref[...] == slots).astype(F32).astype(BF16)
        rows_ref[...] = jnp.dot(chosen, held, preferred_element_type=F32).astype(BF16)

    whole[...] = lax.dot_general(
        act_ref[...], rows_ref[...], (((0,), (0,)), ((), ())), preferred_element_type=F32
    )
    core = core_ref[0]
    shard = whole.shape[0] // (2 * keep_ref.shape[1])
    for target, parity in ((keep_ref, core), (send_ref, 1 - core)):
        for z in range(keep_ref.shape[1]):
            for cut in range(CUTS):
                size = min(ROWS, shard - cut * ROWS)
                start = pl.multiple_of(z * 2 * shard + parity * shard + cut * ROWS, 8)
                part = whole[pl.ds(start, size), :]
                if size < ROWS:
                    part = jnp.concatenate([part, jnp.zeros((ROWS - size, part.shape[1]), F32)], axis=0)
                for k in range(CUTS):
                    target[cut * CUTS + k, z] = part[:, k * HD : (k + 1) * HD].astype(BF16)


def gradient_pieces(core, send_slot, main, first, second, activations):
    tok, features = activations.shape
    width = main.shape[1]
    steps = 4
    held = pl.BlockSpec((tok, width), lambda m, *_: (0, 0))
    back = pl.BlockSpec(first.shape, lambda m, *_: (0, 0))
    pieces = pl.BlockSpec((CUTS * CUTS, DEPTH // steps, ROWS, HD), lambda m, *_: (0, m, 0, 0))
    shape = jax.ShapeDtypeStruct((CUTS * CUTS, DEPTH, ROWS, HD), BF16)
    return pl.pallas_call(
        gradient_kernel,
        grid_spec=pltpu.PrefetchScalarGridSpec(
            num_scalar_prefetch=1,
            grid=(steps,),
            in_specs=[
                pl.BlockSpec((tok, 1), lambda m, *_: (0, 0)),
                held,
                back,
                back,
                pl.BlockSpec((tok, features // steps), lambda m, *_: (0, m)),
            ],
            out_specs=[held, pieces, pieces],
            scratch_shapes=[pltpu.VMEM((features // steps, width), F32)],
        ),
        out_shape=[jax.ShapeDtypeStruct((tok, width), BF16), shape, shape],
        compiler_params=pltpu.CompilerParams(vmem_limit_bytes=24 * 2**20),
        name="gradient_pieces",
    )(core, send_slot.reshape(tok, 1), main, first, second, activations)


def project_kernel(core_ref, rows_ref, own_ref, other_ref, out_ref, whole):
    core = core_ref[0]
    shard = whole.shape[0] // (2 * own_ref.shape[1])
    for source, parity in ((own_ref, core), (other_ref, 1 - core)):
        for z in range(own_ref.shape[1]):
            for cut in range(CUTS):
                size = min(ROWS, shard - cut * ROWS)
                start = pl.multiple_of(z * 2 * shard + parity * shard + cut * ROWS, 8)
                for k in range(CUTS):
                    part = source[cut * CUTS + k, z].astype(F32)
                    whole[pl.ds(start, size), k * HD : (k + 1) * HD] = part[:size]
    out_ref[...] = lax.dot_general(
        rows_ref[...], whole[...].astype(BF16), (((1,), (1,)), ((), ())), preferred_element_type=F32
    ).astype(BF16)


def project_back(core, row_grads, own, other):
    tok, width = row_grads.shape
    steps = 4
    features = 2 * DEPTH * 80
    pieces = pl.BlockSpec((CUTS * CUTS, DEPTH // steps, ROWS, HD), lambda m, *_: (0, m, 0, 0))
    return pl.pallas_call(
        project_kernel,
        grid_spec=pltpu.PrefetchScalarGridSpec(
            num_scalar_prefetch=1,
            grid=(steps,),
            in_specs=[pl.BlockSpec((tok, width), lambda m, *_: (0, 0)), pieces, pieces],
            out_specs=pl.BlockSpec((tok, features // steps), lambda m, *_: (0, m)),
            scratch_shapes=[pltpu.VMEM((features // steps, width), F32)],
        ),
        out_shape=jax.ShapeDtypeStruct((tok, features), BF16),
        compiler_params=pltpu.CompilerParams(vmem_limit_bytes=24 * 2**20),
        name="project_back",
    )(core, row_grads, own, other)


def plane_exchange(pieces):
    groups = [list(range(half * PLANE, (half + 1) * PLANE)) for half in range(2)]
    return lax.all_to_all(pieces, "dp", 0, 0, axis_index_groups=groups)


def plane_gather(piece):
    return plane_exchange(jnp.broadcast_to(piece[None], (PLANE, *piece.shape)))


def depth_gather(piece):
    groups = [[2 * z + core for z in range(DEPTH)] for core in range(2)]
    return lax.all_to_all(
        jnp.broadcast_to(piece[None], (DEPTH, *piece.shape)), "fsdp", 0, 0, axis_index_groups=groups
    )


def depth_exchange(pieces):
    count = 2 * DEPTH
    groups = [
        [(half * PLANE + at) * count + 2 * z + core for half in range(2) for z in range(DEPTH)]
        for at in range(PLANE)
        for core in range(2)
    ]
    return lax.all_to_all(
        jnp.concatenate([pieces, pieces], axis=0), BOTH, 0, 0, axis_index_groups=groups
    )


def total(parts):
    return jnp.sum(parts.astype(F32), axis=0).astype(BF16)


def cut_up(shard):
    padded = jnp.pad(shard, ((0, CUTS * ROWS - shard.shape[0]), (0, 0)))
    return padded.reshape(CUTS, ROWS, CUTS, HD).transpose(0, 2, 1, 3).reshape(CUTS * CUTS, ROWS, HD)


def put_together(pieces, rows):
    whole = pieces.reshape(CUTS, CUTS, ROWS, HD).transpose(0, 2, 1, 3)
    return whole.reshape(CUTS * ROWS, CUTS * HD)[:rows]


def local(activations, value_weight, queries, key_rows, context_grad, segment, send_slot):
    tok = activations.shape[0]
    block = (queries.shape[0] - tok) // SECTIONS
    half = lax.axis_size("dp") // 2
    place = lax.axis_index("dp") % PLANE
    core = (lax.axis_index("fsdp") % 2).astype(jnp.int32).reshape(1)

    slots = tok + jnp.arange(SECTIONS * block, dtype=jnp.int32)
    taken = send_slot[None, :] == slots[:, None]
    sent = jnp.max(jnp.where(taken, segment[None, :], -1), axis=1)
    got = [
        swapped(sent[s * block : (s + 1) * block], "dp", half >> s) for s in range(SECTIONS)
    ]

    piece = lax.dynamic_index_in_dim(cut_up(value_weight), place, 0, keepdims=False)
    depth_weight = depth_gather(after(piece, sent))

    ids = after(jnp.concatenate([segment, *got]), depth_weight)
    slot_grads = attend(queries, key_rows, context_grad, ids, tok, block)
    returned = [
        swapped(slot_grads[tok + s * block : tok + (s + 1) * block], "dp", half >> s)
        for s in range(SECTIONS)
    ]

    own_weight = plane_gather(after(depth_weight, slot_grads))
    first, second, own_weight = lax.optimization_barrier((*returned, own_weight))
    other_weight = swapped(own_weight, "fsdp", 1)

    row_grads, keep, send = gradient_pieces(core, send_slot, slot_grads[:tok], first, second, activations)
    came = swapped(send, "fsdp", 1)
    input_grad = project_back(core, row_grads, own_weight, other_weight)

    plane_part = total(plane_exchange((keep.astype(F32) + came.astype(F32)).astype(BF16)))
    depth_part = total(depth_exchange(plane_part))
    weight_grad = put_together(plane_gather(depth_part), value_weight.shape[0])
    return (input_grad, weight_grad)


def solution(mesh):
    rows = P(("dp", "fsdp"), None)
    flat = P(("dp", "fsdp"))
    return jax.shard_map(
        local,
        mesh=mesh,
        in_specs=(rows, P("fsdp", None), rows, rows, rows, flat, flat),
        out_specs=(rows, P("fsdp", None)),
        check_vma=False,
    )
```

```python
import functools
import math

import jax
import jax.numpy as jnp
from jax import lax
from jax.experimental import pallas as pl
from jax.experimental.pallas import tpu as pltpu
from jax.sharding import PartitionSpec as P

KVH = 4
GROUP = 5
HD = 128
SECTIONS = 2
LEAST = 16
PLANE = 16
DEPTH = 16
CUTS = 4
ROWS = 24
BOTH = ("dp", "fsdp")
BF16 = jnp.bfloat16
F32 = jnp.float32
WIDTH = KVH * HD
FEATURES = KVH * GROUP * HD
SUMS = FEATURES
PROBS = SUMS + 2 * WIDTH
MESSAGE = PROBS + 2 * KVH * HD
SCALE = 1.0 / math.sqrt(HD)
ON_COLUMNS = (((1,), (1,)), ((), ()))


def swapped(block, axis, distance):
    route = [(low, low ^ distance) for low in range(lax.axis_size(axis))]
    return lax.ppermute(block, axis, route)


def softmax_down(scores, allowed):
    masked = jnp.where(allowed, scores * SCALE, -jnp.inf)
    exponent = jnp.exp(masked - jnp.max(masked, axis=0, keepdims=True))
    return (exponent * (1.0 / jnp.sum(exponent, axis=0, keepdims=True))).astype(BF16)


def iota(shape, dim):
    return lax.broadcasted_iota(jnp.int32, shape, dim)


def message_kernel(block, q_ref, k_ref, c_ref, *out_refs):
    for section, out_ref in enumerate(out_refs):
        low = section * block
        copies_ref = None
        if section == 0:
            copies_ref, out_ref = out_ref, out_ref.at[0]
        out_ref[:, :FEATURES] = c_ref[low + LEAST : low + block, :]
        pad = jnp.zeros((HD - GROUP * LEAST, HD), BF16)
        for h in range(KVH):

            def stacked(ref, start):
                heads = [ref[start : start + LEAST, (h * GROUP + g) * HD : (h * GROUP + g + 1) * HD] for g in range(GROUP)]
                return jnp.concatenate([*heads, pad], axis=0)

            keys = k_ref[low : low + block, h * HD : (h + 1) * HD]
            scores = lax.dot_general(keys, stacked(q_ref, low + LEAST), ON_COLUMNS, preferred_element_type=F32)
            allowed = iota((block, HD), 0) <= iota((block, HD), 1) % LEAST + LEAST
            probs = softmax_down(scores, allowed)
            at = PROBS + 2 * h * HD
            out_ref[:, at : at + HD] = probs[:LEAST]
            out_ref[:, at + HD : at + 2 * HD] = probs[LEAST:]

            scores = lax.dot_general(keys[:LEAST], stacked(q_ref, low), ON_COLUMNS, preferred_element_type=F32)
            allowed = iota((LEAST, HD), 0) <= iota((LEAST, HD), 1) % LEAST
            probs = softmax_down(scores, allowed)
            sums = jnp.dot(probs, stacked(c_ref, low), preferred_element_type=F32)
            coarse = sums.astype(BF16)
            at = SUMS + h * HD
            out_ref[:, at : at + HD] = coarse
            out_ref[:, at + WIDTH : at + WIDTH + HD] = (sums - coarse.astype(F32)).astype(BF16)
        if copies_ref is not None:
            copies_ref[1] = copies_ref[0]


def messages(queries, key_rows, context_grad, tok, block):
    both = SECTIONS * block
    last = tok // both
    specs = [pl.BlockSpec((both, x.shape[1]), lambda i: (last, 0)) for x in (queries, key_rows, context_grad)]
    shape = (block - LEAST, MESSAGE)
    return pl.pallas_call(
        functools.partial(message_kernel, block),
        grid=(1,),
        in_specs=specs,
        out_specs=[pl.BlockSpec((2, *shape), lambda i: (0, 0, 0)), pl.BlockSpec(shape, lambda i: (0, 0))],
        out_shape=[jax.ShapeDtypeStruct((2, *shape), BF16), jax.ShapeDtypeStruct(shape, BF16)],
        compiler_params=pltpu.CompilerParams(vmem_limit_bytes=24 * 2**20),
        name="messages",
    )(queries, key_rows, context_grad)


def sent_block(slot, message_ref, low, block):
    inside = (slot >= low) & (slot < low + block)
    count = jnp.sum(inside.astype(jnp.int32), axis=0, keepdims=True)
    pad = jnp.zeros((HD - GROUP * LEAST, HD), BF16)
    heads = []
    for h in range(KVH):
        at = PROBS + 2 * h * HD
        probs = jnp.concatenate([message_ref[:, at : at + HD], message_ref[:, at + HD : at + 2 * HD]], axis=0)
        held = iota(probs.shape, 1) % LEAST + LEAST < count
        probs = jnp.where(held, probs.astype(F32), 0.0).astype(BF16)
        rows = [message_ref[:, (h * GROUP + g) * HD : (h * GROUP + g + 1) * HD] for g in range(GROUP)]
        late = jnp.dot(probs, jnp.concatenate([*rows, pad], axis=0), preferred_element_type=F32)
        at = SUMS + h * HD
        early = message_ref[:, at : at + HD].astype(F32) + message_ref[:, at + WIDTH : at + WIDTH + HD].astype(F32)
        heads.append(late + jnp.concatenate([early, jnp.zeros((block - LEAST, HD), F32)], axis=0))
    return jnp.concatenate(heads, axis=1).astype(BF16)


def attend_kernel(col_ref, row_ref, q_ref, k_ref, c_ref, behind_ref, out_ref):
    del behind_ref
    tok = q_ref.shape[0]
    query = jnp.concatenate([q_ref[:, g * HD : (g + 1) * HD] for g in range(GROUP)], axis=0)
    context = jnp.concatenate([c_ref[:, g * HD : (g + 1) * HD] for g in range(GROUP)], axis=0)
    allowed = (col_ref[...] == row_ref[...]) & (iota((tok, tok), 0) <= iota((tok, tok), 1))
    bias = jnp.where(allowed, 0.0, -jnp.inf)
    scores = lax.dot_general(k_ref[...], query, ON_COLUMNS, preferred_element_type=F32) * SCALE
    masked = scores + jnp.concatenate([bias] * GROUP, axis=1)
    exponent = jnp.exp(masked - jnp.max(masked, axis=0, keepdims=True))
    probs = (exponent * (1.0 / jnp.sum(exponent, axis=0, keepdims=True))).astype(BF16)
    out_ref[...] = jnp.dot(probs, context, preferred_element_type=F32).astype(BF16)


def attend(queries, key_rows, context_grad, segment, behind):
    tok = segment.shape[0]
    wide = pl.BlockSpec((tok, GROUP * HD), lambda h: (0, h))
    thin = pl.BlockSpec((tok, HD), lambda h: (0, h))
    return pl.pallas_call(
        attend_kernel,
        grid=(KVH,),
        in_specs=[
            pl.BlockSpec((tok, 1), lambda h: (0, 0)),
            pl.BlockSpec((1, tok), lambda h: (0, 0)),
            wide,
            thin,
            wide,
            pl.BlockSpec(memory_space=pl.ANY),
        ],
        out_specs=thin,
        out_shape=jax.ShapeDtypeStruct((tok, WIDTH), BF16),
        name="attend",
    )(segment.reshape(tok, 1), segment.reshape(1, tok), queries, key_rows, context_grad, behind)


def gradient_kernel(block, core_ref, half_ref, slot_ref, main_ref, first_ref, second_ref, act_ref, rows_ref, keep_ref, send_ref, whole):
    tok = slot_ref.shape[0]

    @pl.when(pl.program_id(0) == 0)
    def _():
        slot = slot_ref[...]
        refs = (first_ref.at[1 - half_ref[0]], second_ref)
        parts = [sent_block(slot, ref, tok + s * block, block) for s, ref in enumerate(refs)]
        held = jnp.concatenate([main_ref[...], *parts], axis=0)
        chosen = (slot == iota((tok, held.shape[0]), 1)).astype(F32).astype(BF16)
        rows_ref[...] = jnp.dot(chosen, held, preferred_element_type=F32).astype(BF16)

    whole[...] = lax.dot_general(
        act_ref[...], rows_ref[...], (((0,), (0,)), ((), ())), preferred_element_type=F32
    )
    core = core_ref[0]
    pairs = keep_ref.shape[1]
    shard = whole.shape[0] // (4 * pairs)
    upper = iota((8, WIDTH), 0) < 4
    for target, parity in ((keep_ref, core), (send_ref, 1 - core)):
        for pair in range(pairs):

            def rows(odd, start, size):
                at = (4 * pair + 2 * odd + parity) * shard + start
                return whole[pl.ds(pl.multiple_of(at, 8), size), :]

            for cut in range(CUTS):
                split = 16 * CUTS + 8 * (cut // 2)
                even, odd = rows(0, split, 8), pltpu.roll(rows(1, split, 8), 4, 0)
                mixed = jnp.where(upper, even, odd) if cut % 2 == 0 else jnp.where(upper, odd, even)
                piece = jnp.concatenate([rows(0, 16 * cut, 16), rows(1, 16 * cut, 16), mixed], axis=0).astype(BF16)
                for k in range(CUTS):
                    target[cut * CUTS + k, pair] = piece[:, k * HD : (k + 1) * HD]


def gradient_pieces(core, half, send_slot, main, first, second, activations, block):
    tok, features = activations.shape
    steps = 4
    held = pl.BlockSpec((tok, WIDTH), lambda m, *_: (0, 0))
    message = [pl.BlockSpec(x.shape, lambda m, *_, rank=x.ndim: (0,) * rank) for x in (first, second)]
    pieces = pl.BlockSpec((CUTS * CUTS, DEPTH // 2 // steps, 40, HD), lambda m, *_: (0, m, 0, 0))
    shape = jax.ShapeDtypeStruct((CUTS * CUTS, DEPTH // 2, 40, HD), BF16)
    return pl.pallas_call(
        functools.partial(gradient_kernel, block),
        grid_spec=pltpu.PrefetchScalarGridSpec(
            num_scalar_prefetch=2,
            grid=(steps,),
            in_specs=[
                pl.BlockSpec((tok, 1), lambda m, *_: (0, 0)),
                held,
                *message,
                pl.BlockSpec((tok, features // steps), lambda m, *_: (0, m)),
            ],
            out_specs=[held, pieces, pieces],
            scratch_shapes=[pltpu.VMEM((features // steps, WIDTH), F32)],
        ),
        out_shape=[jax.ShapeDtypeStruct((tok, WIDTH), BF16), shape, shape],
        compiler_params=pltpu.CompilerParams(vmem_limit_bytes=24 * 2**20),
        name="gradient_pieces",
    )(core, half, send_slot.reshape(tok, 1), main, first, second, activations)


def plane_sum_kernel(odd_ref, parts_ref, keep_ref, send_ref, whole):
    pairs, rows, _ = whole.shape
    for pair in range(pairs):
        whole[pair] = jnp.sum(parts_ref[:, pair * rows : (pair + 1) * rows, :].astype(F32), axis=0)
    odd = odd_ref[0]
    for target, parity in ((keep_ref, odd), (send_ref, 1 - odd)):
        for pair in range(whole.shape[0]):
            own = whole[pair, pl.ds(pl.multiple_of(parity * 16, 8), 16), :]
            target[pair] = jnp.concatenate([own, whole[pair, 32:40, :]], axis=0).astype(BF16)


def plane_sum(odd, parts, pairs, rows):
    count, _, lanes = parts.shape
    out = pl.BlockSpec((pairs, ROWS, lanes), lambda i, *_: (0, 0, 0))
    return pl.pallas_call(
        plane_sum_kernel,
        grid_spec=pltpu.PrefetchScalarGridSpec(
            num_scalar_prefetch=1,
            grid=(1,),
            in_specs=[pl.BlockSpec((count, pairs * rows, lanes), lambda i, *_: (0, 0, 0))],
            out_specs=[out, out],
            scratch_shapes=[pltpu.VMEM((pairs, rows, lanes), F32)],
        ),
        out_shape=[jax.ShapeDtypeStruct((pairs, ROWS, lanes), BF16)] * 2,
        compiler_params=pltpu.CompilerParams(vmem_limit_bytes=24 * 2**20),
        name="plane_sum",
    )(odd, parts)


def depth_sum_kernel(parts_ref, out_ref):
    total = jnp.sum(parts_ref[...].astype(F32), axis=0).astype(BF16)
    for at in range(out_ref.shape[0]):
        out_ref[at] = total


def depth_sum(parts):
    return pl.pallas_call(
        depth_sum_kernel,
        out_shape=jax.ShapeDtypeStruct((PLANE, *parts.shape[1:]), BF16),
        name="depth_sum",
    )(parts)


def join_kernel(odd_ref, pieces_ref, out_ref):
    odd = odd_ref[0]
    upper = iota((8, HD), 0) < 4
    for k in range(CUTS):
        lanes = slice(k * HD, (k + 1) * HD)
        tiles = []
        for cut in range(CUTS):
            out_ref[16 * cut : 16 * cut + 16, lanes] = pieces_ref[cut * CUTS + k, :16, :]
            tiles.append(pieces_ref[cut * CUTS + k, 16:, :].astype(F32))
        last = []
        for low, high in ((tiles[0], tiles[1]), (tiles[2], tiles[3])):
            from_odd = pltpu.roll(jnp.where(upper, high, low), 4, 0)
            last.append(jnp.where(odd == 1, from_odd, jnp.where(upper, low, high)))
        out_ref[16 * CUTS :, lanes] = jnp.concatenate(last, axis=0).astype(BF16)


def join(odd, pieces, rows):
    return pl.pallas_call(
        join_kernel,
        grid_spec=pltpu.PrefetchScalarGridSpec(
            num_scalar_prefetch=1,
            grid=(1,),
            in_specs=[pl.BlockSpec(pieces.shape, lambda i, *_: (0, 0, 0))],
            out_specs=pl.BlockSpec((rows, WIDTH), lambda i, *_: (0, 0)),
        ),
        out_shape=jax.ShapeDtypeStruct((rows, WIDTH), BF16),
        name="join",
    )(odd, pieces)


def project_kernel(core_ref, odd_ref, pair_ref, rows_ref, *refs):
    *source_refs, out_ref, whole = refs
    core, odd, swap = core_ref[0], odd_ref[0], pair_ref[0] % 2
    pairs = source_refs[0].shape[1]
    shard = whole.shape[0] // (4 * pairs)
    places = [(a, b) for b in (core, 1 - core) for a in (odd, 1 - odd)]
    for source, (z_parity, core_parity) in zip(source_refs, places, strict=True):
        for pair in range(pairs):
            for cut in range(CUTS):
                size = min(ROWS, shard - cut * ROWS)
                at = (4 * pair + 2 * z_parity + core_parity) * shard + cut * ROWS
                for k in range(CUTS):
                    part = source[cut * CUTS + k, pair ^ swap].astype(F32)
                    whole[pl.ds(pl.multiple_of(at, 8), size), k * HD : (k + 1) * HD] = part[:size]
    out_ref[...] = lax.dot_general(
        rows_ref[...], whole[...].astype(BF16), ON_COLUMNS, preferred_element_type=F32
    ).astype(BF16)


def project_back(core, odd, pair, row_grads, sources, features):
    tok, width = row_grads.shape
    steps = 4
    pieces = pl.BlockSpec((CUTS * CUTS, DEPTH // 2 // steps, ROWS, HD), lambda m, c, o, p: (0, m ^ (p[0] // 2), 0, 0))
    return pl.pallas_call(
        project_kernel,
        grid_spec=pltpu.PrefetchScalarGridSpec(
            num_scalar_prefetch=3,
            grid=(steps,),
            in_specs=[pl.BlockSpec((tok, width), lambda m, *_: (0, 0))] + [pieces] * len(sources),
            out_specs=pl.BlockSpec((tok, features // steps), lambda m, *_: (0, m)),
            scratch_shapes=[pltpu.VMEM((features // steps, width), F32)],
        ),
        out_shape=jax.ShapeDtypeStruct((tok, features), BF16),
        compiler_params=pltpu.CompilerParams(vmem_limit_bytes=24 * 2**20),
        name="project_back",
    )(core, odd, pair, row_grads, *sources)


def plane_exchange(pieces):
    groups = [list(range(half * PLANE, (half + 1) * PLANE)) for half in range(2)]
    return lax.all_to_all(pieces, "dp", 0, 0, axis_index_groups=groups)


def depth_gather(piece):
    pieces = piece[None]
    for bit in range(1, DEPTH.bit_length() - 1):
        pieces = jnp.concatenate([pieces, swapped(pieces, "fsdp", 2 << bit)], axis=0)
    return pieces.reshape(DEPTH // 2 * ROWS, HD)


def halves_exchange(copies):
    groups = [[at, at + PLANE] for at in range(PLANE)]
    return lax.all_to_all(copies, "dp", 0, 0, axis_index_groups=groups)


def depth_exchange(pieces):
    count = 2 * DEPTH
    groups = [
        [(half * PLANE + at) * count + 2 * z + core for half in range(2) for z in range(odd, DEPTH, 2)]
        for at in range(PLANE)
        for odd in range(2)
        for core in range(2)
    ]
    return lax.all_to_all(pieces, BOTH, 0, 0, axis_index_groups=groups)


def added(one, two):
    return (one.astype(F32) + two.astype(F32)).astype(BF16)


def cut_up(shard):
    padded = jnp.pad(shard, ((0, CUTS * ROWS - shard.shape[0]), (0, 0)))
    return padded.reshape(CUTS, ROWS, CUTS, HD).transpose(0, 2, 1, 3).reshape(CUTS * CUTS, ROWS, HD)


def local(activations, value_weight, queries, key_rows, context_grad, segment, send_slot):
    tok, features = activations.shape
    block = (queries.shape[0] - tok) // SECTIONS
    half = lax.axis_size("dp") // 2
    place = lax.axis_index("dp") % PLANE
    core, odd, pair, upper = (
        x.astype(jnp.int32).reshape(1)
        for x in (
            lax.axis_index("fsdp") % 2,
            lax.axis_index("fsdp") // 2 % 2,
            lax.axis_index("fsdp") // 4,
            lax.axis_index("dp") // half,
        )
    )

    piece = lax.dynamic_index_in_dim(cut_up(value_weight), place, 0, keepdims=False)
    first, second = messages(queries, key_rows, context_grad, tok, block)
    first = halves_exchange(first)
    second = swapped(second, "dp", half // 2)
    depth_weight = depth_gather(piece)
    main = attend(queries, key_rows, context_grad, segment, depth_weight)

    row_grads, keep, send = gradient_pieces(core, upper, send_slot, main, first, second, activations, block)
    came = swapped(send, "fsdp", 1)
    _, pairs, rows, _ = keep.shape
    gradient = added(keep, came).reshape(PLANE, pairs * rows, HD)
    weight = jnp.broadcast_to(depth_weight[None], (PLANE, *depth_weight.shape))
    parts = plane_exchange(jnp.concatenate([gradient, weight], axis=1))

    keep, send = plane_sum(odd, parts, pairs, rows)
    came = swapped(send, "fsdp", 2)
    depth_part, parts = lax.optimization_barrier((added(keep, came), parts))
    depth_parts = depth_exchange(jnp.concatenate([depth_part, depth_part], axis=0))

    weight = parts[:, pairs * rows :].reshape(CUTS * CUTS, DEPTH // 2, ROWS, HD)
    weights = [weight, swapped(weight, "fsdp", 2)]
    weights += [swapped(x, "fsdp", 1) for x in weights]
    finished = plane_exchange(depth_sum(depth_parts))
    input_grad = project_back(core, odd, pair, row_grads, weights, features)
    finished, input_grad = lax.optimization_barrier((finished, input_grad))
    weight_grad = join(odd, finished, value_weight.shape[0])
    return (input_grad, weight_grad)


def solution(mesh):
    rows = P(("dp", "fsdp"), None)
    flat = P(("dp", "fsdp"))
    return jax.shard_map(
        local,
        mesh=mesh,
        in_specs=(rows, P("fsdp", None), rows, rows, rows, flat, flat),
        out_specs=(rows, P("fsdp", None)),
        check_vma=False,
    )
```

```python
import functools
import math

import jax
import jax.numpy as jnp
from jax import lax
from jax.experimental import pallas as pl
from jax.experimental.pallas import tpu as pltpu
from jax.sharding import PartitionSpec as P

KVH = 4
GROUP = 5
HD = 128
SECTIONS = 2
LEAST = 16
PLANE = 16
DEPTH = 16
CUTS = 4
ROWS = 24
BOTH = ("dp", "fsdp")
BF16 = jnp.bfloat16
F32 = jnp.float32
WIDTH = KVH * HD
FEATURES = KVH * GROUP * HD
SUMS = FEATURES
PROBS = SUMS + 2 * WIDTH
MESSAGE = PROBS + 2 * KVH * HD
SCALE = 1.0 / math.sqrt(HD)
ON_COLUMNS = (((1,), (1,)), ((), ()))


def swapped(block, axis, distance):
    route = [(low, low ^ distance) for low in range(lax.axis_size(axis))]
    return lax.ppermute(block, axis, route)


def softmax_down(scores, allowed):
    masked = jnp.where(allowed, scores * SCALE, -jnp.inf)
    exponent = jnp.exp(masked - jnp.max(masked, axis=0, keepdims=True))
    return (exponent * (1.0 / jnp.sum(exponent, axis=0, keepdims=True))).astype(BF16)


def iota(shape, dim):
    return lax.broadcasted_iota(jnp.int32, shape, dim)


def message_kernel(block, q_ref, k_ref, c_ref, *out_refs):
    for section, out_ref in enumerate(out_refs):
        low = section * block
        out_ref[:, :FEATURES] = c_ref[low + LEAST : low + block, :]
        pad = jnp.zeros((HD - GROUP * LEAST, HD), BF16)
        for h in range(KVH):

            def stacked(ref, start):
                heads = [ref[start : start + LEAST, (h * GROUP + g) * HD : (h * GROUP + g + 1) * HD] for g in range(GROUP)]
                return jnp.concatenate([*heads, pad], axis=0)

            keys = k_ref[low : low + block, h * HD : (h + 1) * HD]
            scores = lax.dot_general(keys, stacked(q_ref, low + LEAST), ON_COLUMNS, preferred_element_type=F32)
            allowed = iota((block, HD), 0) <= iota((block, HD), 1) % LEAST + LEAST
            probs = softmax_down(scores, allowed)
            at = PROBS + 2 * h * HD
            out_ref[:, at : at + HD] = probs[:LEAST]
            out_ref[:, at + HD : at + 2 * HD] = probs[LEAST:]

            scores = lax.dot_general(keys[:LEAST], stacked(q_ref, low), ON_COLUMNS, preferred_element_type=F32)
            allowed = iota((LEAST, HD), 0) <= iota((LEAST, HD), 1) % LEAST
            probs = softmax_down(scores, allowed)
            sums = jnp.dot(probs, stacked(c_ref, low), preferred_element_type=F32)
            coarse = sums.astype(BF16)
            at = SUMS + h * HD
            out_ref[:, at : at + HD] = coarse
            out_ref[:, at + WIDTH : at + WIDTH + HD] = (sums - coarse.astype(F32)).astype(BF16)


def messages(queries, key_rows, context_grad, tok, block):
    both = SECTIONS * block
    last = tok // both
    specs = [pl.BlockSpec((both, x.shape[1]), lambda i: (last, 0)) for x in (queries, key_rows, context_grad)]
    shape = (block - LEAST, MESSAGE)
    return pl.pallas_call(
        functools.partial(message_kernel, block),
        grid=(1,),
        in_specs=specs,
        out_specs=[pl.BlockSpec(shape, lambda i: (0, 0))] * SECTIONS,
        out_shape=[jax.ShapeDtypeStruct(shape, BF16)] * SECTIONS,
        compiler_params=pltpu.CompilerParams(vmem_limit_bytes=56 * 2**20),
        name="messages",
    )(queries, key_rows, context_grad)


def sent_block(slot, message_ref, low, block):
    inside = (slot >= low) & (slot < low + block)
    count = jnp.sum(inside.astype(jnp.int32), axis=0, keepdims=True)
    pad = jnp.zeros((HD - GROUP * LEAST, HD), BF16)
    heads = []
    for h in range(KVH):
        at = PROBS + 2 * h * HD
        probs = jnp.concatenate([message_ref[:, at : at + HD], message_ref[:, at + HD : at + 2 * HD]], axis=0)
        held = iota(probs.shape, 1) % LEAST + LEAST < count
        probs = jnp.where(held, probs.astype(F32), 0.0).astype(BF16)
        rows = [message_ref[:, (h * GROUP + g) * HD : (h * GROUP + g + 1) * HD] for g in range(GROUP)]
        late = jnp.dot(probs, jnp.concatenate([*rows, pad], axis=0), preferred_element_type=F32)
        at = SUMS + h * HD
        early = message_ref[:, at : at + HD].astype(F32) + message_ref[:, at + WIDTH : at + WIDTH + HD].astype(F32)
        heads.append(late + jnp.concatenate([early, jnp.zeros((block - LEAST, HD), F32)], axis=0))
    return jnp.concatenate(heads, axis=1).astype(BF16)


def attend_kernel(col_ref, row_ref, q_ref, k_ref, c_ref, out_ref):
    tok = q_ref.shape[0]
    query = jnp.concatenate([q_ref[:, g * HD : (g + 1) * HD] for g in range(GROUP)], axis=0)
    context = jnp.concatenate([c_ref[:, g * HD : (g + 1) * HD] for g in range(GROUP)], axis=0)
    allowed = (col_ref[...] == row_ref[...]) & (iota((tok, tok), 0) <= iota((tok, tok), 1))
    bias = jnp.where(allowed, 0.0, -jnp.inf)
    scores = lax.dot_general(k_ref[...], query, ON_COLUMNS, preferred_element_type=F32) * SCALE
    masked = scores + jnp.concatenate([bias] * GROUP, axis=1)
    exponent = jnp.exp(masked - jnp.max(masked, axis=0, keepdims=True))
    probs = (exponent * (1.0 / jnp.sum(exponent, axis=0, keepdims=True))).astype(BF16)
    out_ref[...] = jnp.dot(probs, context, preferred_element_type=F32).astype(BF16)


def attend(queries, key_rows, context_grad, segment):
    tok = segment.shape[0]
    wide = pl.BlockSpec((tok, GROUP * HD), lambda h: (0, h))
    thin = pl.BlockSpec((tok, HD), lambda h: (0, h))
    return pl.pallas_call(
        attend_kernel,
        grid=(KVH,),
        in_specs=[
            pl.BlockSpec((tok, 1), lambda h: (0, 0)),
            pl.BlockSpec((1, tok), lambda h: (0, 0)),
            wide,
            thin,
            wide,
        ],
        out_specs=thin,
        out_shape=jax.ShapeDtypeStruct((tok, WIDTH), BF16),
        name="attend",
    )(segment.reshape(tok, 1), segment.reshape(1, tok), queries, key_rows, context_grad)


def gradient_kernel(block, core_ref, slot_ref, main_ref, first_ref, second_ref, act_ref, behind_ref, rows_ref, keep_ref, send_ref, whole):
    del behind_ref
    tok = slot_ref.shape[0]

    @pl.when(pl.program_id(0) == 0)
    def _():
        slot = slot_ref[...]
        parts = [sent_block(slot, ref, tok + s * block, block) for s, ref in enumerate((first_ref, second_ref))]
        held = jnp.concatenate([main_ref[...], *parts], axis=0)
        chosen = (slot == iota((tok, held.shape[0]), 1)).astype(F32).astype(BF16)
        rows_ref[...] = jnp.dot(chosen, held, preferred_element_type=F32).astype(BF16)

    whole[...] = lax.dot_general(
        act_ref[...], rows_ref[...], (((0,), (0,)), ((), ())), preferred_element_type=F32
    )
    core = core_ref[0]
    pairs = keep_ref.shape[1]
    shard = whole.shape[0] // (4 * pairs)
    upper = iota((8, WIDTH), 0) < 4
    for target, parity in ((keep_ref, core), (send_ref, 1 - core)):
        for pair in range(pairs):

            def rows(odd, start, size):
                at = (4 * pair + 2 * odd + parity) * shard + start
                return whole[pl.ds(pl.multiple_of(at, 8), size), :]

            for cut in range(CUTS):
                split = 16 * CUTS + 8 * (cut // 2)
                even, odd = rows(0, split, 8), pltpu.roll(rows(1, split, 8), 4, 0)
                mixed = jnp.where(upper, even, odd) if cut % 2 == 0 else jnp.where(upper, odd, even)
                piece = jnp.concatenate([rows(0, 16 * cut, 16), rows(1, 16 * cut, 16), mixed], axis=0).astype(BF16)
                for k in range(CUTS):
                    target[cut * CUTS + k, pair] = piece[:, k * HD : (k + 1) * HD]


def gradient_pieces(core, send_slot, main, first, second, activations, behind, block):
    tok, features = activations.shape
    steps = 4
    held = pl.BlockSpec((tok, WIDTH), lambda m, *_: (0, 0))
    message = pl.BlockSpec(first.shape, lambda m, *_: (0, 0))
    pieces = pl.BlockSpec((CUTS * CUTS, DEPTH // 2 // steps, 40, HD), lambda m, *_: (0, m, 0, 0))
    shape = jax.ShapeDtypeStruct((CUTS * CUTS, DEPTH // 2, 40, HD), BF16)
    return pl.pallas_call(
        functools.partial(gradient_kernel, block),
        grid_spec=pltpu.PrefetchScalarGridSpec(
            num_scalar_prefetch=1,
            grid=(steps,),
            in_specs=[
                pl.BlockSpec((tok, 1), lambda m, *_: (0, 0)),
                held,
                message,
                message,
                pl.BlockSpec((tok, features // steps), lambda m, *_: (0, m)),
                pl.BlockSpec(memory_space=pl.ANY),
            ],
            out_specs=[held, pieces, pieces],
            scratch_shapes=[pltpu.VMEM((features // steps, WIDTH), F32)],
        ),
        out_shape=[jax.ShapeDtypeStruct((tok, WIDTH), BF16), shape, shape],
        compiler_params=pltpu.CompilerParams(vmem_limit_bytes=24 * 2**20),
        name="gradient_pieces",
    )(core, send_slot.reshape(tok, 1), main, first, second, activations, behind)


def plane_sum_kernel(odd_ref, parts_ref, keep_ref, send_ref, whole):
    pairs, rows, _ = whole.shape
    for pair in range(pairs):
        whole[pair] = jnp.sum(parts_ref[:, pair * rows : (pair + 1) * rows, :].astype(F32), axis=0)
    odd = odd_ref[0]
    for target, parity in ((keep_ref, odd), (send_ref, 1 - odd)):
        for pair in range(whole.shape[0]):
            own = whole[pair, pl.ds(pl.multiple_of(parity * 16, 8), 16), :]
            target[pair] = jnp.concatenate([own, whole[pair, 32:40, :]], axis=0).astype(BF16)


def plane_sum(odd, parts, pairs, rows):
    count, _, lanes = parts.shape
    out = pl.BlockSpec((pairs, ROWS, lanes), lambda i, *_: (0, 0, 0))
    return pl.pallas_call(
        plane_sum_kernel,
        grid_spec=pltpu.PrefetchScalarGridSpec(
            num_scalar_prefetch=1,
            grid=(1,),
            in_specs=[pl.BlockSpec((count, pairs * rows, lanes), lambda i, *_: (0, 0, 0))],
            out_specs=[out, out],
            scratch_shapes=[pltpu.VMEM((pairs, rows, lanes), F32)],
        ),
        out_shape=[jax.ShapeDtypeStruct((pairs, ROWS, lanes), BF16)] * 2,
        compiler_params=pltpu.CompilerParams(vmem_limit_bytes=24 * 2**20),
        name="plane_sum",
    )(odd, parts)


def depth_sum_kernel(parts_ref, out_ref):
    total = jnp.sum(parts_ref[...].astype(F32), axis=0).astype(BF16)
    for at in range(out_ref.shape[0]):
        out_ref[at] = total


def depth_sum(parts):
    return pl.pallas_call(
        depth_sum_kernel,
        out_shape=jax.ShapeDtypeStruct((PLANE, *parts.shape[1:]), BF16),
        name="depth_sum",
    )(parts)


def join_kernel(odd_ref, pieces_ref, out_ref):
    odd = odd_ref[0]
    upper = iota((8, HD), 0) < 4
    for k in range(CUTS):
        lanes = slice(k * HD, (k + 1) * HD)
        tiles = []
        for cut in range(CUTS):
            out_ref[16 * cut : 16 * cut + 16, lanes] = pieces_ref[cut * CUTS + k, :16, :]
            tiles.append(pieces_ref[cut * CUTS + k, 16:, :].astype(F32))
        last = []
        for low, high in ((tiles[0], tiles[1]), (tiles[2], tiles[3])):
            from_odd = pltpu.roll(jnp.where(upper, high, low), 4, 0)
            last.append(jnp.where(odd == 1, from_odd, jnp.where(upper, low, high)))
        out_ref[16 * CUTS :, lanes] = jnp.concatenate(last, axis=0).astype(BF16)


def join(odd, pieces, rows):
    return pl.pallas_call(
        join_kernel,
        grid_spec=pltpu.PrefetchScalarGridSpec(
            num_scalar_prefetch=1,
            grid=(1,),
            in_specs=[pl.BlockSpec(pieces.shape, lambda i, *_: (0, 0, 0))],
            out_specs=pl.BlockSpec((rows, WIDTH), lambda i, *_: (0, 0)),
        ),
        out_shape=jax.ShapeDtypeStruct((rows, WIDTH), BF16),
        name="join",
    )(odd, pieces)


def project_kernel(core_ref, rows_ref, own_ref, other_ref, out_ref, whole):
    core = core_ref[0]
    shard = whole.shape[0] // (2 * own_ref.shape[1])
    for source, parity in ((own_ref, core), (other_ref, 1 - core)):
        for z in range(own_ref.shape[1]):
            for cut in range(CUTS):
                size = min(ROWS, shard - cut * ROWS)
                start = pl.multiple_of(z * 2 * shard + parity * shard + cut * ROWS, 8)
                for k in range(CUTS):
                    part = source[cut * CUTS + k, z].astype(F32)
                    whole[pl.ds(start, size), k * HD : (k + 1) * HD] = part[:size]
    out_ref[...] = lax.dot_general(
        rows_ref[...], whole[...].astype(BF16), ON_COLUMNS, preferred_element_type=F32
    ).astype(BF16)


def project_back(core, row_grads, own, other, features):
    tok, width = row_grads.shape
    steps = 4
    pieces = pl.BlockSpec((CUTS * CUTS, DEPTH // steps, ROWS, HD), lambda m, *_: (0, m, 0, 0))
    return pl.pallas_call(
        project_kernel,
        grid_spec=pltpu.PrefetchScalarGridSpec(
            num_scalar_prefetch=1,
            grid=(steps,),
            in_specs=[pl.BlockSpec((tok, width), lambda m, *_: (0, 0)), pieces, pieces],
            out_specs=pl.BlockSpec((tok, features // steps), lambda m, *_: (0, m)),
            scratch_shapes=[pltpu.VMEM((features // steps, width), F32)],
        ),
        out_shape=jax.ShapeDtypeStruct((tok, features), BF16),
        compiler_params=pltpu.CompilerParams(vmem_limit_bytes=24 * 2**20),
        name="project_back",
    )(core, row_grads, own, other)


def plane_exchange(pieces):
    groups = [list(range(half * PLANE, (half + 1) * PLANE)) for half in range(2)]
    return lax.all_to_all(pieces, "dp", 0, 0, axis_index_groups=groups)


def depth_gather(piece):
    groups = [[2 * z + core for z in range(DEPTH)] for core in range(2)]
    copies = jnp.broadcast_to(piece[None], (DEPTH, *piece.shape))
    return lax.all_to_all(copies, "fsdp", 0, 0, axis_index_groups=groups)


def plane_gather(pieces):
    rounds = 1 + lax.axis_index("dp") // lax.axis_size("dp")
    copies = jnp.broadcast_to(pieces[None], (PLANE, *pieces.shape))
    return lax.fori_loop(0, rounds, lambda _, held: plane_exchange(held), copies)


def depth_exchange(pieces):
    count = 2 * DEPTH
    groups = [
        [(half * PLANE + at) * count + 2 * z + core for half in range(2) for z in range(odd, DEPTH, 2)]
        for at in range(PLANE)
        for odd in range(2)
        for core in range(2)
    ]
    return lax.all_to_all(pieces, BOTH, 0, 0, axis_index_groups=groups)


def added(one, two):
    return (one.astype(F32) + two.astype(F32)).astype(BF16)


def cut_up(shard):
    padded = jnp.pad(shard, ((0, CUTS * ROWS - shard.shape[0]), (0, 0)))
    return padded.reshape(CUTS, ROWS, CUTS, HD).transpose(0, 2, 1, 3).reshape(CUTS * CUTS, ROWS, HD)


def local(activations, value_weight, queries, key_rows, context_grad, segment, send_slot):
    tok, features = activations.shape
    block = (queries.shape[0] - tok) // SECTIONS
    half = lax.axis_size("dp") // 2
    place = lax.axis_index("dp") % PLANE
    core = (lax.axis_index("fsdp") % 2).astype(jnp.int32).reshape(1)
    odd = (lax.axis_index("fsdp") // 2 % 2).astype(jnp.int32).reshape(1)

    piece = lax.dynamic_index_in_dim(cut_up(value_weight), place, 0, keepdims=False)
    first, second = messages(queries, key_rows, context_grad, tok, block)
    first = swapped(first, "dp", half)
    second = swapped(second, "dp", half // 2)
    own_weight = plane_gather(depth_gather(piece))
    main = attend(queries, key_rows, context_grad, segment)
    main, own_weight = lax.optimization_barrier((main, own_weight))

    row_grads, keep, send = gradient_pieces(core, send_slot, main, first, second, activations, own_weight, block)
    came = swapped(send, "fsdp", 1)
    _, pairs, rows, _ = keep.shape
    parts = plane_exchange(added(keep, came).reshape(PLANE, pairs * rows, HD))
    other_weight = swapped(own_weight, "fsdp", 1)

    keep, send = plane_sum(odd, parts, pairs, rows)
    came = swapped(send, "fsdp", 2)
    depth_part = added(keep, came)
    depth_parts = depth_exchange(jnp.concatenate([depth_part, depth_part], axis=0))
    input_grad = project_back(core, row_grads, own_weight, other_weight, features)
    depth_parts, input_grad = lax.optimization_barrier((depth_parts, input_grad))
    finished = plane_exchange(depth_sum(depth_parts))
    weight_grad = join(odd, finished, value_weight.shape[0])
    return (input_grad, weight_grad)


def solution(mesh):
    rows = P(("dp", "fsdp"), None)
    flat = P(("dp", "fsdp"))
    return jax.shard_map(
        local,
        mesh=mesh,
        in_specs=(rows, P("fsdp", None), rows, rows, rows, flat, flat),
        out_specs=(rows, P("fsdp", None)),
        check_vma=False,
    )
```

```python
import functools
import math

import jax
import jax.numpy as jnp
from jax import lax
from jax.experimental import pallas as pl
from jax.experimental.pallas import tpu as pltpu
from jax.sharding import PartitionSpec as P

KVH = 4
GROUP = 5
HD = 128
SECTIONS = 2
LEAST = 16
PLANE = 16
DEPTH = 16
CUTS = 4
ROWS = 24
BOTH = ("dp", "fsdp")
BF16 = jnp.bfloat16
F32 = jnp.float32
WIDTH = KVH * HD
FEATURES = KVH * GROUP * HD
SUMS = FEATURES
PROBS = SUMS + 2 * WIDTH
MESSAGE = PROBS + 2 * KVH * HD
SCALE = 1.0 / math.sqrt(HD)
ON_COLUMNS = (((1,), (1,)), ((), ()))


def swapped(block, axis, distance):
    route = [(low, low ^ distance) for low in range(lax.axis_size(axis))]
    return lax.ppermute(block, axis, route)


def softmax_down(scores, allowed):
    masked = jnp.where(allowed, scores * SCALE, -jnp.inf)
    exponent = jnp.exp(masked - jnp.max(masked, axis=0, keepdims=True))
    return (exponent * (1.0 / jnp.sum(exponent, axis=0, keepdims=True))).astype(BF16)


def iota(shape, dim):
    return lax.broadcasted_iota(jnp.int32, shape, dim)


def message_kernel(block, q_ref, k_ref, c_ref, *out_refs):
    for section, out_ref in enumerate(out_refs):
        low = section * block
        out_ref[:, :FEATURES] = c_ref[low + LEAST : low + block, :]
        pad = jnp.zeros((HD - GROUP * LEAST, HD), BF16)
        for h in range(KVH):

            def stacked(ref, start):
                heads = [ref[start : start + LEAST, (h * GROUP + g) * HD : (h * GROUP + g + 1) * HD] for g in range(GROUP)]
                return jnp.concatenate([*heads, pad], axis=0)

            keys = k_ref[low : low + block, h * HD : (h + 1) * HD]
            scores = lax.dot_general(keys, stacked(q_ref, low + LEAST), ON_COLUMNS, preferred_element_type=F32)
            allowed = iota((block, HD), 0) <= iota((block, HD), 1) % LEAST + LEAST
            probs = softmax_down(scores, allowed)
            at = PROBS + 2 * h * HD
            out_ref[:, at : at + HD] = probs[:LEAST]
            out_ref[:, at + HD : at + 2 * HD] = probs[LEAST:]

            scores = lax.dot_general(keys[:LEAST], stacked(q_ref, low), ON_COLUMNS, preferred_element_type=F32)
            allowed = iota((LEAST, HD), 0) <= iota((LEAST, HD), 1) % LEAST
            probs = softmax_down(scores, allowed)
            sums = jnp.dot(probs, stacked(c_ref, low), preferred_element_type=F32)
            coarse = sums.astype(BF16)
            at = SUMS + h * HD
            out_ref[:, at : at + HD] = coarse
            out_ref[:, at + WIDTH : at + WIDTH + HD] = (sums - coarse.astype(F32)).astype(BF16)


def messages(queries, key_rows, context_grad, tok, block):
    both = SECTIONS * block
    last = tok // both
    specs = [pl.BlockSpec((both, x.shape[1]), lambda i: (last, 0)) for x in (queries, key_rows, context_grad)]
    shape = (block - LEAST, MESSAGE)
    return pl.pallas_call(
        functools.partial(message_kernel, block),
        grid=(1,),
        in_specs=specs,
        out_specs=[pl.BlockSpec(shape, lambda i: (0, 0))] * SECTIONS,
        out_shape=[jax.ShapeDtypeStruct(shape, BF16)] * SECTIONS,
        compiler_params=pltpu.CompilerParams(vmem_limit_bytes=56 * 2**20),
        name="messages",
    )(queries, key_rows, context_grad)


def sent_block(slot, message_ref, low, block):
    inside = (slot >= low) & (slot < low + block)
    count = jnp.sum(inside.astype(jnp.int32), axis=0, keepdims=True)
    pad = jnp.zeros((HD - GROUP * LEAST, HD), BF16)
    heads = []
    for h in range(KVH):
        at = PROBS + 2 * h * HD
        probs = jnp.concatenate([message_ref[:, at : at + HD], message_ref[:, at + HD : at + 2 * HD]], axis=0)
        held = iota(probs.shape, 1) % LEAST + LEAST < count
        probs = jnp.where(held, probs.astype(F32), 0.0).astype(BF16)
        rows = [message_ref[:, (h * GROUP + g) * HD : (h * GROUP + g + 1) * HD] for g in range(GROUP)]
        late = jnp.dot(probs, jnp.concatenate([*rows, pad], axis=0), preferred_element_type=F32)
        at = SUMS + h * HD
        early = message_ref[:, at : at + HD].astype(F32) + message_ref[:, at + WIDTH : at + WIDTH + HD].astype(F32)
        heads.append(late + jnp.concatenate([early, jnp.zeros((block - LEAST, HD), F32)], axis=0))
    return jnp.concatenate(heads, axis=1).astype(BF16)


def attend_kernel(col_ref, row_ref, q_ref, k_ref, c_ref, behind_ref, out_ref):
    del behind_ref
    tok = q_ref.shape[0]
    query = jnp.concatenate([q_ref[:, g * HD : (g + 1) * HD] for g in range(GROUP)], axis=0)
    context = jnp.concatenate([c_ref[:, g * HD : (g + 1) * HD] for g in range(GROUP)], axis=0)
    allowed = (col_ref[...] == row_ref[...]) & (iota((tok, tok), 0) <= iota((tok, tok), 1))
    bias = jnp.where(allowed, 0.0, -jnp.inf)
    scores = lax.dot_general(k_ref[...], query, ON_COLUMNS, preferred_element_type=F32) * SCALE
    masked = scores + jnp.concatenate([bias] * GROUP, axis=1)
    exponent = jnp.exp(masked - jnp.max(masked, axis=0, keepdims=True))
    probs = (exponent * (1.0 / jnp.sum(exponent, axis=0, keepdims=True))).astype(BF16)
    out_ref[...] = jnp.dot(probs, context, preferred_element_type=F32).astype(BF16)


def attend(queries, key_rows, context_grad, segment, behind):
    tok = segment.shape[0]
    wide = pl.BlockSpec((tok, GROUP * HD), lambda h: (0, h))
    thin = pl.BlockSpec((tok, HD), lambda h: (0, h))
    return pl.pallas_call(
        attend_kernel,
        grid=(KVH,),
        in_specs=[
            pl.BlockSpec((tok, 1), lambda h: (0, 0)),
            pl.BlockSpec((1, tok), lambda h: (0, 0)),
            wide,
            thin,
            wide,
            pl.BlockSpec(memory_space=pl.ANY),
        ],
        out_specs=thin,
        out_shape=jax.ShapeDtypeStruct((tok, WIDTH), BF16),
        name="attend",
    )(segment.reshape(tok, 1), segment.reshape(1, tok), queries, key_rows, context_grad, behind)


def gradient_kernel(block, core_ref, slot_ref, main_ref, first_ref, second_ref, act_ref, behind_ref, rows_ref, keep_ref, send_ref, whole):
    del behind_ref
    tok = slot_ref.shape[0]

    @pl.when(pl.program_id(0) == 0)
    def _():
        slot = slot_ref[...]
        parts = [sent_block(slot, ref, tok + s * block, block) for s, ref in enumerate((first_ref, second_ref))]
        held = jnp.concatenate([main_ref[...], *parts], axis=0)
        chosen = (slot == iota((tok, held.shape[0]), 1)).astype(F32).astype(BF16)
        rows_ref[...] = jnp.dot(chosen, held, preferred_element_type=F32).astype(BF16)

    whole[...] = lax.dot_general(
        act_ref[...], rows_ref[...], (((0,), (0,)), ((), ())), preferred_element_type=F32
    )
    core = core_ref[0]
    pairs = keep_ref.shape[1]
    shard = whole.shape[0] // (4 * pairs)
    upper = iota((8, WIDTH), 0) < 4
    for target, parity in ((keep_ref, core), (send_ref, 1 - core)):
        for pair in range(pairs):

            def rows(odd, start, size):
                at = (4 * pair + 2 * odd + parity) * shard + start
                return whole[pl.ds(pl.multiple_of(at, 8), size), :]

            for cut in range(CUTS):
                split = 16 * CUTS + 8 * (cut // 2)
                even, odd = rows(0, split, 8), pltpu.roll(rows(1, split, 8), 4, 0)
                mixed = jnp.where(upper, even, odd) if cut % 2 == 0 else jnp.where(upper, odd, even)
                piece = jnp.concatenate([rows(0, 16 * cut, 16), rows(1, 16 * cut, 16), mixed], axis=0).astype(BF16)
                for k in range(CUTS):
                    target[cut * CUTS + k, pair] = piece[:, k * HD : (k + 1) * HD]


def gradient_pieces(core, send_slot, main, first, second, activations, behind, block):
    tok, features = activations.shape
    steps = 4
    held = pl.BlockSpec((tok, WIDTH), lambda m, *_: (0, 0))
    message = pl.BlockSpec(first.shape, lambda m, *_: (0, 0))
    pieces = pl.BlockSpec((CUTS * CUTS, DEPTH // 2 // steps, 40, HD), lambda m, *_: (0, m, 0, 0))
    shape = jax.ShapeDtypeStruct((CUTS * CUTS, DEPTH // 2, 40, HD), BF16)
    return pl.pallas_call(
        functools.partial(gradient_kernel, block),
        grid_spec=pltpu.PrefetchScalarGridSpec(
            num_scalar_prefetch=1,
            grid=(steps,),
            in_specs=[
                pl.BlockSpec((tok, 1), lambda m, *_: (0, 0)),
                held,
                message,
                message,
                pl.BlockSpec((tok, features // steps), lambda m, *_: (0, m)),
                pl.BlockSpec(memory_space=pl.ANY),
            ],
            out_specs=[held, pieces, pieces],
            scratch_shapes=[pltpu.VMEM((features // steps, WIDTH), F32)],
        ),
        out_shape=[jax.ShapeDtypeStruct((tok, WIDTH), BF16), shape, shape],
        compiler_params=pltpu.CompilerParams(vmem_limit_bytes=24 * 2**20),
        name="gradient_pieces",
    )(core, send_slot.reshape(tok, 1), main, first, second, activations, behind)


def plane_sum_kernel(odd_ref, parts_ref, keep_ref, send_ref, whole):
    pairs, rows, _ = whole.shape
    for pair in range(pairs):
        whole[pair] = jnp.sum(parts_ref[:, pair * rows : (pair + 1) * rows, :].astype(F32), axis=0)
    odd = odd_ref[0]
    for target, parity in ((keep_ref, odd), (send_ref, 1 - odd)):
        for pair in range(whole.shape[0]):
            own = whole[pair, pl.ds(pl.multiple_of(parity * 16, 8), 16), :]
            target[pair] = jnp.concatenate([own, whole[pair, 32:40, :]], axis=0).astype(BF16)


def plane_sum(odd, parts, pairs, rows):
    count, _, lanes = parts.shape
    out = pl.BlockSpec((pairs, ROWS, lanes), lambda i, *_: (0, 0, 0))
    return pl.pallas_call(
        plane_sum_kernel,
        grid_spec=pltpu.PrefetchScalarGridSpec(
            num_scalar_prefetch=1,
            grid=(1,),
            in_specs=[pl.BlockSpec((count, pairs * rows, lanes), lambda i, *_: (0, 0, 0))],
            out_specs=[out, out],
            scratch_shapes=[pltpu.VMEM((pairs, rows, lanes), F32)],
        ),
        out_shape=[jax.ShapeDtypeStruct((pairs, ROWS, lanes), BF16)] * 2,
        compiler_params=pltpu.CompilerParams(vmem_limit_bytes=24 * 2**20),
        name="plane_sum",
    )(odd, parts)


def depth_sum_kernel(parts_ref, out_ref):
    total = jnp.sum(parts_ref[...].astype(F32), axis=0).astype(BF16)
    for at in range(out_ref.shape[0]):
        out_ref[at] = total


def depth_sum(parts):
    return pl.pallas_call(
        depth_sum_kernel,
        out_shape=jax.ShapeDtypeStruct((PLANE, *parts.shape[1:]), BF16),
        name="depth_sum",
    )(parts)


def join_kernel(odd_ref, pieces_ref, out_ref):
    odd = odd_ref[0]
    upper = iota((8, HD), 0) < 4
    for k in range(CUTS):
        lanes = slice(k * HD, (k + 1) * HD)
        tiles = []
        for cut in range(CUTS):
            out_ref[16 * cut : 16 * cut + 16, lanes] = pieces_ref[cut * CUTS + k, :16, :]
            tiles.append(pieces_ref[cut * CUTS + k, 16:, :].astype(F32))
        last = []
        for low, high in ((tiles[0], tiles[1]), (tiles[2], tiles[3])):
            from_odd = pltpu.roll(jnp.where(upper, high, low), 4, 0)
            last.append(jnp.where(odd == 1, from_odd, jnp.where(upper, low, high)))
        out_ref[16 * CUTS :, lanes] = jnp.concatenate(last, axis=0).astype(BF16)


def join(odd, pieces, rows):
    return pl.pallas_call(
        join_kernel,
        grid_spec=pltpu.PrefetchScalarGridSpec(
            num_scalar_prefetch=1,
            grid=(1,),
            in_specs=[pl.BlockSpec(pieces.shape, lambda i, *_: (0, 0, 0))],
            out_specs=pl.BlockSpec((rows, WIDTH), lambda i, *_: (0, 0)),
        ),
        out_shape=jax.ShapeDtypeStruct((rows, WIDTH), BF16),
        name="join",
    )(odd, pieces)


def cut_out(shard, place):
    cut, k = place // CUTS, place % CUTS
    rows = lax.dynamic_slice(shard, (16 * cut, HD * k), (16, HD))
    tile = lax.dynamic_slice(shard, (16 * CUTS + 8 * (cut // 2), HD * k), (8, HD))
    return jnp.concatenate([rows, tile], axis=0)


def spread_kernel(place_ref, pieces_ref, out_ref, paired):
    count = pieces_ref.shape[0]

    @pl.when(pl.program_id(0) == 0)
    def _():
        flip = place_ref[0] // CUTS % 2
        upper = iota((8, HD), 0) // 4 == flip
        for z in range(0, count, 2):
            even, odd = ((z + i + count // 2) % count for i in range(2))
            turned = pltpu.roll(pieces_ref[odd, 16:, :].astype(F32), 4, 0)
            mixed = jnp.where(upper, pieces_ref[even, 16:, :].astype(F32), turned)
            part = [pieces_ref[even, :16, :].astype(F32), pieces_ref[odd, :16, :].astype(F32), mixed]
            paired[20 * z : 20 * z + 40, :] = jnp.concatenate(part, axis=0)

    for at in range(out_ref.shape[0]):
        out_ref[at] = paired[...].astype(BF16)


def spread(place, pieces):
    steps = 4
    rows = pieces.shape[0] * 20
    return pl.pallas_call(
        spread_kernel,
        grid_spec=pltpu.PrefetchScalarGridSpec(
            num_scalar_prefetch=1,
            grid=(steps,),
            in_specs=[pl.BlockSpec(pieces.shape, lambda m, *_: (0, 0, 0))],
            out_specs=pl.BlockSpec((PLANE // steps, rows, HD), lambda m, *_: (m, 0, 0)),
            scratch_shapes=[pltpu.VMEM((rows, HD), F32)],
        ),
        out_shape=jax.ShapeDtypeStruct((PLANE, rows, HD), BF16),
        compiler_params=pltpu.CompilerParams(vmem_limit_bytes=24 * 2**20),
        name="spread",
    )(place, pieces)


def project_kernel(core_ref, rows_ref, own_ref, other_ref, out_ref, whole):
    core = core_ref[0]
    pairs = own_ref.shape[1] // 40
    shard = whole.shape[0] // (4 * pairs)
    upper = iota((8, HD), 0) < 4
    for source, parity in ((own_ref, core), (other_ref, 1 - core)):
        for pair in range(pairs):

            def put(odd, start, k, value):
                at = pl.multiple_of((4 * pair + 2 * odd + parity) * shard + start, 16)
                whole[pl.ds(at, 16), k * HD : (k + 1) * HD] = value

            for k in range(CUTS):
                tiles = []
                for cut in range(CUTS):
                    piece = source[cut * CUTS + k, 40 * pair : 40 * pair + 32, :]
                    put(0, 16 * cut, k, piece[:16])
                    put(1, 16 * cut, k, piece[16:])
                    tiles.append(source[cut * CUTS + k, 40 * pair + 32 : 40 * pair + 40, :].astype(F32))
                evens = [jnp.where(upper, tiles[i], tiles[i + 1]) for i in (0, 2)]
                odds = [pltpu.roll(jnp.where(upper, tiles[i + 1], tiles[i]), 4, 0) for i in (0, 2)]
                put(0, 16 * CUTS, k, jnp.concatenate(evens, axis=0).astype(BF16))
                put(1, 16 * CUTS, k, jnp.concatenate(odds, axis=0).astype(BF16))
    out_ref[...] = lax.dot_general(
        rows_ref[...], whole[...], ON_COLUMNS, preferred_element_type=F32
    ).astype(BF16)


def project_back(core, row_grads, own, other, features):
    tok, width = row_grads.shape
    steps = 4
    pieces = pl.BlockSpec((PLANE, own.shape[1] // steps, HD), lambda m, *_: (0, m, 0))
    return pl.pallas_call(
        project_kernel,
        grid_spec=pltpu.PrefetchScalarGridSpec(
            num_scalar_prefetch=1,
            grid=(steps,),
            in_specs=[pl.BlockSpec((tok, width), lambda m, *_: (0, 0)), pieces, pieces],
            out_specs=pl.BlockSpec((tok, features // steps), lambda m, *_: (0, m)),
            scratch_shapes=[pltpu.VMEM((features // steps, width), BF16)],
        ),
        out_shape=jax.ShapeDtypeStruct((tok, features), BF16),
        compiler_params=pltpu.CompilerParams(vmem_limit_bytes=24 * 2**20),
        name="project_back",
    )(core, row_grads, own, other)


def plane_exchange(pieces):
    groups = [list(range(half * PLANE, (half + 1) * PLANE)) for half in range(2)]
    return lax.all_to_all(pieces, "dp", 0, 0, axis_index_groups=groups)


def depth_gather(piece):
    groups = [[2 * ((z + DEPTH // 2) % DEPTH) + core for z in range(DEPTH)] for core in range(2)]
    copies = jnp.broadcast_to(piece[None], (DEPTH, *piece.shape))
    return lax.all_to_all(copies, "fsdp", 0, 0, axis_index_groups=groups)


def depth_exchange(pieces):
    count = 2 * DEPTH
    groups = [
        [(half * PLANE + at) * count + 2 * z + core for half in range(2) for z in range(odd, DEPTH, 2)]
        for at in range(PLANE)
        for odd in range(2)
        for core in range(2)
    ]
    return lax.all_to_all(pieces, BOTH, 0, 0, axis_index_groups=groups)


def added(one, two):
    return (one.astype(F32) + two.astype(F32)).astype(BF16)


def local(activations, value_weight, queries, key_rows, context_grad, segment, send_slot):
    tok, features = activations.shape
    block = (queries.shape[0] - tok) // SECTIONS
    half = lax.axis_size("dp") // 2
    place = lax.axis_index("dp") % PLANE
    core = (lax.axis_index("fsdp") % 2).astype(jnp.int32).reshape(1)
    odd = (lax.axis_index("fsdp") // 2 % 2).astype(jnp.int32).reshape(1)

    first, second = messages(queries, key_rows, context_grad, tok, block)
    first = swapped(first, "dp", half)
    copies = spread(place.astype(jnp.int32).reshape(1), depth_gather(cut_out(value_weight, place)))

    def beside(held):
        copies, second, _ = held
        main = attend(queries, key_rows, context_grad, segment, second)
        return plane_exchange(copies), swapped(second, "dp", half // 2), main

    held = (copies, second, jnp.zeros((tok, WIDTH), BF16))
    own_weight, second, main = lax.cond(lax.axis_index("dp") < lax.axis_size("dp"), beside, lambda held: held, held)
    main, own_weight = lax.optimization_barrier((main, own_weight))

    row_grads, keep, send = gradient_pieces(core, send_slot, main, first, second, activations, own_weight, block)
    came = swapped(send, "fsdp", 1)
    _, pairs, rows, _ = keep.shape
    parts = plane_exchange(added(keep, came).reshape(PLANE, pairs * rows, HD))
    other_weight = swapped(own_weight, "fsdp", 1)

    keep, send = plane_sum(odd, parts, pairs, rows)
    came = swapped(send, "fsdp", 2)
    depth_part = added(keep, came)
    depth_parts = depth_exchange(jnp.concatenate([depth_part, depth_part], axis=0))
    input_grad = project_back(core, row_grads, own_weight, other_weight, features)
    depth_parts, input_grad = lax.optimization_barrier((depth_parts, input_grad))
    finished = plane_exchange(depth_sum(depth_parts))
    weight_grad = join(odd, finished, value_weight.shape[0])
    return (input_grad, weight_grad)


def solution(mesh):
    rows = P(("dp", "fsdp"), None)
    flat = P(("dp", "fsdp"))
    return jax.shard_map(
        local,
        mesh=mesh,
        in_specs=(rows, P("fsdp", None), rows, rows, rows, flat, flat),
        out_specs=(rows, P("fsdp", None)),
        check_vma=False,
    )
```

```python
import functools
import math

import jax
import jax.numpy as jnp
from jax import lax
from jax.experimental import pallas as pl
from jax.experimental.pallas import tpu as pltpu
from jax.sharding import PartitionSpec as P

KVH = 4
GROUP = 5
HD = 128
SECTIONS = 2
LEAST = 16
PLANE = 16
DEPTH = 16
CUTS = 4
ROWS = 24
BOTH = ("dp", "fsdp")
BF16 = jnp.bfloat16
F32 = jnp.float32
WIDTH = KVH * HD
FEATURES = KVH * GROUP * HD
LATE = GROUP * LEAST
SUMS = FEATURES
PROBS = SUMS + WIDTH
MESSAGE = PROBS + 2 * KVH * LATE
SCALE = 1.0 / math.sqrt(HD)
ON_COLUMNS = (((1,), (1,)), ((), ()))


def swapped(block, axis, distance):
    route = [(low, low ^ distance) for low in range(lax.axis_size(axis))]
    return lax.ppermute(block, axis, route)


def softmax_down(scores, allowed):
    masked = jnp.where(allowed, scores * SCALE, -jnp.inf)
    exponent = jnp.exp(masked - jnp.max(masked, axis=0, keepdims=True))
    return exponent * (1.0 / jnp.sum(exponent, axis=0, keepdims=True))


def iota(shape, dim):
    return lax.broadcasted_iota(jnp.int32, shape, dim)


def message_kernel(block, q_ref, k_ref, c_ref, *out_refs):
    for section, out_ref in enumerate(out_refs):
        low = section * block
        out_ref[:, :FEATURES] = c_ref[low + LEAST : low + block, :]
        pad = jnp.zeros((HD - LATE, HD), BF16)
        late = []
        for h in range(KVH):

            def stacked(ref, start):
                heads = [ref[start : start + LEAST, (h * GROUP + g) * HD : (h * GROUP + g + 1) * HD] for g in range(GROUP)]
                return jnp.concatenate([*heads, pad], axis=0)

            keys = k_ref[low : low + block, h * HD : (h + 1) * HD]
            scores = lax.dot_general(keys, stacked(q_ref, low + LEAST), ON_COLUMNS, preferred_element_type=F32)
            allowed = iota((block, HD), 0) <= iota((block, HD), 1) % LEAST + LEAST
            late.append(softmax_down(scores, allowed)[:, :LATE])

            scores = lax.dot_general(keys[:LEAST], stacked(q_ref, low), ON_COLUMNS, preferred_element_type=F32)
            allowed = iota((LEAST, HD), 0) <= iota((LEAST, HD), 1) % LEAST
            probs = softmax_down(scores, allowed).astype(BF16)
            sums = jnp.dot(probs, stacked(c_ref, low), preferred_element_type=F32)
            out_ref[:, SUMS + h * HD : SUMS + (h + 1) * HD] = sums.astype(BF16)
        late = [x[start : start + LEAST] for start in range(0, block, LEAST) for x in late]
        out_ref[:, PROBS:] = jnp.concatenate(late, axis=1).astype(BF16)


def messages(queries, key_rows, context_grad, tok, block):
    both = SECTIONS * block
    last = tok // both
    specs = [pl.BlockSpec((both, x.shape[1]), lambda i: (last, 0)) for x in (queries, key_rows, context_grad)]
    shape = (block - LEAST, MESSAGE)
    return pl.pallas_call(
        functools.partial(message_kernel, block),
        grid=(1,),
        in_specs=specs,
        out_specs=[pl.BlockSpec(shape, lambda i: (0, 0))] * SECTIONS,
        out_shape=[jax.ShapeDtypeStruct(shape, BF16)] * SECTIONS,
        compiler_params=pltpu.CompilerParams(vmem_limit_bytes=24 * 2**20),
        name="messages",
    )(queries, key_rows, context_grad)


def sent_block(slot, message_ref, low, block):
    inside = (slot >= low) & (slot < low + block)
    count = jnp.sum(inside.astype(jnp.int32), axis=0, keepdims=True)
    held = iota((block, HD), 1) % LEAST + LEAST < count
    pad = jnp.zeros((HD - LATE, HD), BF16)
    late = message_ref[:, PROBS:].astype(F32)
    heads = []
    for h in range(KVH):
        parts = [late[:, (half * KVH + h) * LATE : (half * KVH + h + 1) * LATE] for half in range(block // LEAST)]
        probs = jnp.concatenate(parts, axis=0)
        probs = jnp.concatenate([probs, jnp.zeros((block, HD - LATE), F32)], axis=1)
        probs = jnp.where(held, probs, 0.0).astype(BF16)
        rows = [message_ref[:, (h * GROUP + g) * HD : (h * GROUP + g + 1) * HD] for g in range(GROUP)]
        sums = jnp.dot(probs, jnp.concatenate([*rows, pad], axis=0), preferred_element_type=F32)
        early = message_ref[:, SUMS + h * HD : SUMS + (h + 1) * HD].astype(F32)
        heads.append(sums + jnp.concatenate([early, jnp.zeros((block - LEAST, HD), F32)], axis=0))
    return jnp.concatenate(heads, axis=1).astype(BF16)


def attend_kernel(col_ref, row_ref, q_ref, k_ref, c_ref, behind_ref, out_ref):
    del behind_ref
    tok = q_ref.shape[0]
    query = jnp.concatenate([q_ref[:, g * HD : (g + 1) * HD] for g in range(GROUP)], axis=0)
    context = jnp.concatenate([c_ref[:, g * HD : (g + 1) * HD] for g in range(GROUP)], axis=0)
    allowed = (col_ref[...] == row_ref[...]) & (iota((tok, tok), 0) <= iota((tok, tok), 1))
    bias = jnp.where(allowed, 0.0, -jnp.inf)
    scores = lax.dot_general(k_ref[...], query, ON_COLUMNS, preferred_element_type=F32) * SCALE
    masked = scores + jnp.concatenate([bias] * GROUP, axis=1)
    exponent = jnp.exp(masked - jnp.max(masked, axis=0, keepdims=True))
    probs = (exponent * (1.0 / jnp.sum(exponent, axis=0, keepdims=True))).astype(BF16)
    out_ref[...] = jnp.dot(probs, context, preferred_element_type=F32).astype(BF16)


def attend(queries, key_rows, context_grad, segment, behind):
    tok = segment.shape[0]
    wide = pl.BlockSpec((tok, GROUP * HD), lambda h: (0, h))
    thin = pl.BlockSpec((tok, HD), lambda h: (0, h))
    return pl.pallas_call(
        attend_kernel,
        grid=(KVH,),
        in_specs=[
            pl.BlockSpec((tok, 1), lambda h: (0, 0)),
            pl.BlockSpec((1, tok), lambda h: (0, 0)),
            wide,
            thin,
            wide,
            pl.BlockSpec(memory_space=pl.ANY),
        ],
        out_specs=thin,
        out_shape=jax.ShapeDtypeStruct((tok, WIDTH), BF16),
        name="attend",
    )(segment.reshape(tok, 1), segment.reshape(1, tok), queries, key_rows, context_grad, behind)


def rows_kernel(block, slot_ref, main_ref, first_ref, second_ref, out_ref):
    slot = slot_ref[...]
    tok = slot.shape[0]
    parts = [sent_block(slot, ref, tok + s * block, block) for s, ref in enumerate((first_ref, second_ref))]
    held = jnp.concatenate([main_ref[...], *parts], axis=0)
    chosen = (slot == iota((tok, held.shape[0]), 1)).astype(F32).astype(BF16)
    out_ref[...] = jnp.dot(chosen, held, preferred_element_type=F32).astype(BF16)


def own_rows(send_slot, main, first, second, block):
    tok = main.shape[0]
    operands = (send_slot.reshape(tok, 1), main, first, second)
    return pl.pallas_call(
        functools.partial(rows_kernel, block),
        grid=(1,),
        in_specs=[pl.BlockSpec(x.shape, lambda i: (0, 0)) for x in operands],
        out_specs=pl.BlockSpec(main.shape, lambda i: (0, 0)),
        out_shape=jax.ShapeDtypeStruct(main.shape, BF16),
        compiler_params=pltpu.CompilerParams(vmem_limit_bytes=24 * 2**20),
        name="own_rows",
    )(*operands)


def gradient_kernel(core_ref, rows_ref, other_rows_ref, act_ref, other_act_ref, out_ref, whole):
    whole[...] = lax.dot_general(
        jnp.concatenate([act_ref[...], other_act_ref[...]], axis=0),
        jnp.concatenate([rows_ref[...], other_rows_ref[...]], axis=0),
        (((0,), (0,)), ((), ())),
        preferred_element_type=F32,
    )
    core = core_ref[0]
    pairs = out_ref.shape[1] // 40
    shard = whole.shape[0] // (4 * pairs)
    upper = iota((8, WIDTH), 0) < 4
    for pair in range(pairs):

        def rows(odd, start, size):
            at = (4 * pair + 2 * odd + core) * shard + start
            return whole[pl.ds(pl.multiple_of(at, 8), size), :]

        for cut in range(CUTS):
            split = 16 * CUTS + 8 * (cut // 2)
            even, odd = rows(0, split, 8), pltpu.roll(rows(1, split, 8), 4, 0)
            mixed = jnp.where(upper, even, odd) if cut % 2 == 0 else jnp.where(upper, odd, even)
            piece = jnp.concatenate([rows(0, 16 * cut, 16), rows(1, 16 * cut, 16), mixed], axis=0).astype(BF16)
            for k in range(CUTS):
                out_ref[cut * CUTS + k, 40 * pair : 40 * pair + 40, :] = piece[:, k * HD : (k + 1) * HD]


def gradient_pieces(core, rows, other_rows, activations, other_activations):
    tok, features = activations.shape
    steps = 4
    held = pl.BlockSpec((tok, WIDTH), lambda m, *_: (0, 0))
    columns = pl.BlockSpec((tok, features // steps), lambda m, *_: (0, m))
    return pl.pallas_call(
        gradient_kernel,
        grid_spec=pltpu.PrefetchScalarGridSpec(
            num_scalar_prefetch=1,
            grid=(steps,),
            in_specs=[held, held, columns, columns],
            out_specs=pl.BlockSpec((CUTS * CUTS, 20 * DEPTH // steps, HD), lambda m, *_: (0, m, 0)),
            scratch_shapes=[pltpu.VMEM((features // steps, WIDTH), F32)],
        ),
        out_shape=jax.ShapeDtypeStruct((CUTS * CUTS, 20 * DEPTH, HD), BF16),
        compiler_params=pltpu.CompilerParams(vmem_limit_bytes=24 * 2**20),
        name="gradient_pieces",
    )(core, rows, other_rows, activations, other_activations)


def plane_sum_kernel(odd_ref, parts_ref, keep_ref, send_ref, whole):
    pairs, rows, _ = whole.shape
    for pair in range(pairs):
        whole[pair] = jnp.sum(parts_ref[:, pair * rows : (pair + 1) * rows, :].astype(F32), axis=0)
    odd = odd_ref[0]
    for target, parity in ((keep_ref, odd), (send_ref, 1 - odd)):
        for pair in range(whole.shape[0]):
            own = whole[pair, pl.ds(pl.multiple_of(parity * 16, 8), 16), :]
            target[pair] = jnp.concatenate([own, whole[pair, 32:40, :]], axis=0).astype(BF16)


def plane_sum(odd, parts):
    count, rows, lanes = parts.shape
    pairs, rows = rows // 40, 40
    out = pl.BlockSpec((pairs, ROWS, lanes), lambda i, *_: (0, 0, 0))
    return pl.pallas_call(
        plane_sum_kernel,
        grid_spec=pltpu.PrefetchScalarGridSpec(
            num_scalar_prefetch=1,
            grid=(1,),
            in_specs=[pl.BlockSpec((count, pairs * rows, lanes), lambda i, *_: (0, 0, 0))],
            out_specs=[out, out],
            scratch_shapes=[pltpu.VMEM((pairs, rows, lanes), F32)],
        ),
        out_shape=[jax.ShapeDtypeStruct((pairs, ROWS, lanes), BF16)] * 2,
        compiler_params=pltpu.CompilerParams(vmem_limit_bytes=24 * 2**20),
        name="plane_sum",
    )(odd, parts)


def join_kernel(odd_ref, pieces_ref, out_ref):
    odd = odd_ref[0]
    upper = iota((8, HD), 0) < 4
    for k in range(CUTS):
        lanes = slice(k * HD, (k + 1) * HD)
        tiles = []
        for cut in range(CUTS):
            out_ref[16 * cut : 16 * cut + 16, lanes] = pieces_ref[cut * CUTS + k, :16, :]
            tiles.append(pieces_ref[cut * CUTS + k, 16:, :].astype(F32))
        last = []
        for low, high in ((tiles[0], tiles[1]), (tiles[2], tiles[3])):
            from_odd = pltpu.roll(jnp.where(upper, high, low), 4, 0)
            last.append(jnp.where(odd == 1, from_odd, jnp.where(upper, low, high)))
        out_ref[16 * CUTS :, lanes] = jnp.concatenate(last, axis=0).astype(BF16)


def join(odd, pieces, rows):
    return pl.pallas_call(
        join_kernel,
        grid_spec=pltpu.PrefetchScalarGridSpec(
            num_scalar_prefetch=1,
            grid=(1,),
            in_specs=[pl.BlockSpec(pieces.shape, lambda i, *_: (0, 0, 0))],
            out_specs=pl.BlockSpec((rows, WIDTH), lambda i, *_: (0, 0)),
        ),
        out_shape=jax.ShapeDtypeStruct((rows, WIDTH), BF16),
        name="join",
    )(odd, pieces)


def cut_out(shard, place):
    cut, k = place // CUTS, place % CUTS
    rows = lax.dynamic_slice(shard, (16 * cut, HD * k), (16, HD))
    tile = lax.dynamic_slice(shard, (16 * CUTS + 8 * (cut // 2), HD * k), (8, HD))
    return jnp.concatenate([rows, tile], axis=0)


def spread_kernel(place_ref, pieces_ref, out_ref, paired):
    count = pieces_ref.shape[0]

    @pl.when(pl.program_id(0) == 0)
    def _():
        flip = place_ref[0] // CUTS % 2
        upper = iota((8, HD), 0) // 4 == flip
        for z in range(0, count, 2):
            even, odd = ((z + i + count // 2) % count for i in range(2))
            turned = pltpu.roll(pieces_ref[odd, 16:, :].astype(F32), 4, 0)
            mixed = jnp.where(upper, pieces_ref[even, 16:, :].astype(F32), turned)
            part = [pieces_ref[even, :16, :].astype(F32), pieces_ref[odd, :16, :].astype(F32), mixed]
            paired[20 * z : 20 * z + 40, :] = jnp.concatenate(part, axis=0)

    for at in range(out_ref.shape[0]):
        out_ref[at] = paired[...].astype(BF16)


def spread(place, pieces):
    steps = 4
    rows = pieces.shape[0] * 20
    return pl.pallas_call(
        spread_kernel,
        grid_spec=pltpu.PrefetchScalarGridSpec(
            num_scalar_prefetch=1,
            grid=(steps,),
            in_specs=[pl.BlockSpec(pieces.shape, lambda m, *_: (0, 0, 0))],
            out_specs=pl.BlockSpec((PLANE // steps, rows, HD), lambda m, *_: (m, 0, 0)),
            scratch_shapes=[pltpu.VMEM((rows, HD), F32)],
        ),
        out_shape=jax.ShapeDtypeStruct((PLANE, rows, HD), BF16),
        compiler_params=pltpu.CompilerParams(vmem_limit_bytes=24 * 2**20),
        name="spread",
    )(place, pieces)


def project_kernel(core_ref, rows_ref, own_ref, other_ref, out_ref, whole):
    core = core_ref[0]
    pairs = own_ref.shape[1] // 40
    shard = whole.shape[0] // (4 * pairs)
    upper = iota((8, HD), 0) < 4
    for source, parity in ((own_ref, core), (other_ref, 1 - core)):
        for pair in range(pairs):

            def put(odd, start, k, value):
                at = pl.multiple_of((4 * pair + 2 * odd + parity) * shard + start, 16)
                whole[pl.ds(at, 16), k * HD : (k + 1) * HD] = value

            for k in range(CUTS):
                tiles = []
                for cut in range(CUTS):
                    piece = source[cut * CUTS + k, 40 * pair : 40 * pair + 32, :]
                    put(0, 16 * cut, k, piece[:16])
                    put(1, 16 * cut, k, piece[16:])
                    tiles.append(source[cut * CUTS + k, 40 * pair + 32 : 40 * pair + 40, :].astype(F32))
                evens = [jnp.where(upper, tiles[i], tiles[i + 1]) for i in (0, 2)]
                odds = [pltpu.roll(jnp.where(upper, tiles[i + 1], tiles[i]), 4, 0) for i in (0, 2)]
                put(0, 16 * CUTS, k, jnp.concatenate(evens, axis=0).astype(BF16))
                put(1, 16 * CUTS, k, jnp.concatenate(odds, axis=0).astype(BF16))
    out_ref[...] = lax.dot_general(
        rows_ref[...], whole[...], ON_COLUMNS, preferred_element_type=F32
    ).astype(BF16)


def project_back(core, row_grads, own, other, features):
    tok, width = row_grads.shape
    steps = 4
    pieces = pl.BlockSpec((PLANE, own.shape[1] // steps, HD), lambda m, *_: (0, m, 0))
    return pl.pallas_call(
        project_kernel,
        grid_spec=pltpu.PrefetchScalarGridSpec(
            num_scalar_prefetch=1,
            grid=(steps,),
            in_specs=[pl.BlockSpec((tok, width), lambda m, *_: (0, 0)), pieces, pieces],
            out_specs=pl.BlockSpec((tok, features // steps), lambda m, *_: (0, m)),
            scratch_shapes=[pltpu.VMEM((features // steps, width), BF16)],
        ),
        out_shape=jax.ShapeDtypeStruct((tok, features), BF16),
        compiler_params=pltpu.CompilerParams(vmem_limit_bytes=24 * 2**20),
        name="project_back",
    )(core, row_grads, own, other)


def plane_exchange(pieces):
    groups = [list(range(half * PLANE, (half + 1) * PLANE)) for half in range(2)]
    return lax.all_to_all(pieces, "dp", 0, 0, axis_index_groups=groups)


def depth_gather(piece):
    groups = [[2 * ((z + DEPTH // 2) % DEPTH) + core for z in range(DEPTH)] for core in range(2)]
    copies = jnp.broadcast_to(piece[None], (DEPTH, *piece.shape))
    return lax.all_to_all(copies, "fsdp", 0, 0, axis_index_groups=groups)


def depth_exchange(pieces):
    count = 2 * DEPTH
    groups = [
        [(half * PLANE + at) * count + 2 * z + core for half in range(2) for z in range(odd, DEPTH, 2)]
        for at in range(PLANE)
        for odd in range(2)
        for core in range(2)
    ]
    return lax.all_to_all(pieces, BOTH, 0, 0, axis_index_groups=groups)


def added(one, two):
    return (one.astype(F32) + two.astype(F32)).astype(BF16)


def local(activations, value_weight, queries, key_rows, context_grad, segment, send_slot):
    tok, features = activations.shape
    block = (queries.shape[0] - tok) // SECTIONS
    half = lax.axis_size("dp") // 2
    place = lax.axis_index("dp") % PLANE
    core = (lax.axis_index("fsdp") % 2).astype(jnp.int32).reshape(1)
    odd = (lax.axis_index("fsdp") // 2 % 2).astype(jnp.int32).reshape(1)

    first, second = messages(queries, key_rows, context_grad, tok, block)
    first = swapped(first, "dp", half)
    copies = spread(place.astype(jnp.int32).reshape(1), depth_gather(cut_out(value_weight, place)))

    def beside(held):
        copies, second, _, act = held
        main = attend(queries, key_rows, context_grad, segment, second)
        return plane_exchange(copies), swapped(second, "dp", half // 2), main, swapped(act, "fsdp", 1)

    held = (copies, second, jnp.zeros((tok, WIDTH), BF16), activations)
    own_weight, second, main, other_act = lax.cond(
        lax.axis_index("dp") < lax.axis_size("dp"), beside, lambda held: held, held
    )
    main, own_weight = lax.optimization_barrier((main, own_weight))

    row_grads = own_rows(send_slot, main, first, second, block)
    other_rows = swapped(row_grads, "fsdp", 1)
    parts = plane_exchange(gradient_pieces(core, row_grads, other_rows, activations, other_act))
    other_weight = swapped(own_weight, "fsdp", 1)

    keep, send = plane_sum(odd, parts)
    came = swapped(send, "fsdp", 2)
    depth_part = added(keep, came)
    depth_parts = depth_exchange(jnp.concatenate([depth_part, depth_part], axis=0))
    input_grad = project_back(core, row_grads, own_weight, other_weight, features)
    depth_parts, input_grad = lax.optimization_barrier((depth_parts, input_grad))
    finished = jnp.sum(depth_parts.astype(F32), axis=0).astype(BF16)
    finished = plane_exchange(jnp.broadcast_to(finished[None], (PLANE, *finished.shape)))
    weight_grad = join(odd, finished, value_weight.shape[0])
    return (input_grad, weight_grad)


def solution(mesh):
    rows = P(("dp", "fsdp"), None)
    flat = P(("dp", "fsdp"))
    return jax.shard_map(
        local,
        mesh=mesh,
        in_specs=(rows, P("fsdp", None), rows, rows, rows, flat, flat),
        out_specs=(rows, P("fsdp", None)),
        check_vma=False,
    )
```

```python
import functools
import math

import jax
import jax.numpy as jnp
from jax import lax
from jax.experimental import pallas as pl
from jax.experimental.pallas import tpu as pltpu
from jax.sharding import PartitionSpec as P

KVH = 4
GROUP = 5
HD = 128
SECTIONS = 2
LEAST = 16
PLANE = 16
DEPTH = 16
CUTS = 4
ROWS = 24
BOTH = ("dp", "fsdp")
BF16 = jnp.bfloat16
F32 = jnp.float32
WIDTH = KVH * HD
FEATURES = KVH * GROUP * HD
LATE = GROUP * LEAST
SUMS = FEATURES
PROBS = SUMS + WIDTH
MESSAGE = PROBS + 2 * KVH * LATE
SCALE = 1.0 / math.sqrt(HD)
ON_COLUMNS = (((1,), (1,)), ((), ()))


def swapped(block, axis, distance):
    route = [(low, low ^ distance) for low in range(lax.axis_size(axis))]
    return lax.ppermute(block, axis, route)


def softmax_down(scores, allowed):
    masked = jnp.where(allowed, scores * SCALE, -jnp.inf)
    exponent = jnp.exp(masked - jnp.max(masked, axis=0, keepdims=True))
    return exponent * (1.0 / jnp.sum(exponent, axis=0, keepdims=True))


def iota(shape, dim):
    return lax.broadcasted_iota(jnp.int32, shape, dim)


def message_kernel(block, q_ref, k_ref, c_ref, *out_refs):
    for section, out_ref in enumerate(out_refs):
        low = section * block
        out_ref[:, :FEATURES] = c_ref[low + LEAST : low + block, :]
        pad = jnp.zeros((HD - LATE, HD), BF16)
        late = []
        for h in range(KVH):

            def stacked(ref, start):
                heads = [ref[start : start + LEAST, (h * GROUP + g) * HD : (h * GROUP + g + 1) * HD] for g in range(GROUP)]
                return jnp.concatenate([*heads, pad], axis=0)

            keys = k_ref[low : low + block, h * HD : (h + 1) * HD]
            scores = lax.dot_general(keys, stacked(q_ref, low + LEAST), ON_COLUMNS, preferred_element_type=F32)
            allowed = iota((block, HD), 0) <= iota((block, HD), 1) % LEAST + LEAST
            late.append(softmax_down(scores, allowed)[:, :LATE])

            scores = lax.dot_general(keys[:LEAST], stacked(q_ref, low), ON_COLUMNS, preferred_element_type=F32)
            allowed = iota((LEAST, HD), 0) <= iota((LEAST, HD), 1) % LEAST
            probs = softmax_down(scores, allowed).astype(BF16)
            sums = jnp.dot(probs, stacked(c_ref, low), preferred_element_type=F32)
            out_ref[:, SUMS + h * HD : SUMS + (h + 1) * HD] = sums.astype(BF16)
        late = [x[start : start + LEAST] for start in range(0, block, LEAST) for x in late]
        out_ref[:, PROBS:] = jnp.concatenate(late, axis=1).astype(BF16)


def messages(queries, key_rows, context_grad, tok, block):
    both = SECTIONS * block
    last = tok // both
    specs = [pl.BlockSpec((both, x.shape[1]), lambda i: (last, 0)) for x in (queries, key_rows, context_grad)]
    shape = (block - LEAST, MESSAGE)
    return pl.pallas_call(
        functools.partial(message_kernel, block),
        grid=(1,),
        in_specs=specs,
        out_specs=[pl.BlockSpec(shape, lambda i: (0, 0))] * SECTIONS,
        out_shape=[jax.ShapeDtypeStruct(shape, BF16)] * SECTIONS,
        compiler_params=pltpu.CompilerParams(vmem_limit_bytes=24 * 2**20),
        name="messages",
    )(queries, key_rows, context_grad)


def sent_block(slot, message_ref, low, block):
    inside = (slot >= low) & (slot < low + block)
    count = jnp.sum(inside.astype(jnp.int32), axis=0, keepdims=True)
    held = iota((block, HD), 1) % LEAST + LEAST < count
    pad = jnp.zeros((HD - LATE, HD), BF16)
    late = message_ref[:, PROBS:].astype(F32)
    heads = []
    for h in range(KVH):
        parts = [late[:, (half * KVH + h) * LATE : (half * KVH + h + 1) * LATE] for half in range(block // LEAST)]
        probs = jnp.concatenate(parts, axis=0)
        probs = jnp.concatenate([probs, jnp.zeros((block, HD - LATE), F32)], axis=1)
        probs = jnp.where(held, probs, 0.0).astype(BF16)
        rows = [message_ref[:, (h * GROUP + g) * HD : (h * GROUP + g + 1) * HD] for g in range(GROUP)]
        sums = jnp.dot(probs, jnp.concatenate([*rows, pad], axis=0), preferred_element_type=F32)
        early = message_ref[:, SUMS + h * HD : SUMS + (h + 1) * HD].astype(F32)
        heads.append(sums + jnp.concatenate([early, jnp.zeros((block - LEAST, HD), F32)], axis=0))
    return jnp.concatenate(heads, axis=1).astype(BF16)


def attend_kernel(col_ref, row_ref, q_ref, k_ref, c_ref, out_ref):
    tok = q_ref.shape[0]
    query = jnp.concatenate([q_ref[:, g * HD : (g + 1) * HD] for g in range(GROUP)], axis=0)
    context = jnp.concatenate([c_ref[:, g * HD : (g + 1) * HD] for g in range(GROUP)], axis=0)
    allowed = (col_ref[...] == row_ref[...]) & (iota((tok, tok), 0) <= iota((tok, tok), 1))
    bias = jnp.where(allowed, 0.0, -jnp.inf)
    scores = lax.dot_general(k_ref[...], query, ON_COLUMNS, preferred_element_type=F32) * SCALE
    masked = scores + jnp.concatenate([bias] * GROUP, axis=1)
    exponent = jnp.exp(masked - jnp.max(masked, axis=0, keepdims=True))
    probs = (exponent * (1.0 / jnp.sum(exponent, axis=0, keepdims=True))).astype(BF16)
    out_ref[...] = jnp.dot(probs, context, preferred_element_type=F32).astype(BF16)


def attend(queries, key_rows, context_grad, segment):
    tok = segment.shape[0]
    wide = pl.BlockSpec((tok, GROUP * HD), lambda h: (0, h))
    thin = pl.BlockSpec((tok, HD), lambda h: (0, h))
    return pl.pallas_call(
        attend_kernel,
        grid=(KVH,),
        in_specs=[
            pl.BlockSpec((tok, 1), lambda h: (0, 0)),
            pl.BlockSpec((1, tok), lambda h: (0, 0)),
            wide,
            thin,
            wide,
        ],
        out_specs=thin,
        out_shape=jax.ShapeDtypeStruct((tok, WIDTH), BF16),
        name="attend",
    )(segment.reshape(tok, 1), segment.reshape(1, tok), queries, key_rows, context_grad)


def rows_kernel(block, slot_ref, main_ref, first_ref, second_ref, out_ref):
    slot = slot_ref[...]
    tok = slot.shape[0]
    parts = [sent_block(slot, ref, tok + s * block, block) for s, ref in enumerate((first_ref, second_ref))]
    held = jnp.concatenate([main_ref[...], *parts], axis=0)
    chosen = (slot == iota((tok, held.shape[0]), 1)).astype(F32).astype(BF16)
    out_ref[...] = jnp.dot(chosen, held, preferred_element_type=F32).astype(BF16)


def own_rows(send_slot, main, first, second, block):
    tok = main.shape[0]
    operands = (send_slot.reshape(tok, 1), main, first, second)
    return pl.pallas_call(
        functools.partial(rows_kernel, block),
        grid=(1,),
        in_specs=[pl.BlockSpec(x.shape, lambda i: (0, 0)) for x in operands],
        out_specs=pl.BlockSpec(main.shape, lambda i: (0, 0)),
        out_shape=jax.ShapeDtypeStruct(main.shape, BF16),
        compiler_params=pltpu.CompilerParams(vmem_limit_bytes=24 * 2**20),
        name="own_rows",
    )(*operands)


def gradient_kernel(core_ref, rows_ref, other_rows_ref, act_ref, other_act_ref, out_ref, whole):
    whole[...] = lax.dot_general(
        jnp.concatenate([act_ref[...], other_act_ref[...]], axis=0),
        jnp.concatenate([rows_ref[...], other_rows_ref[...]], axis=0),
        (((0,), (0,)), ((), ())),
        preferred_element_type=F32,
    )
    core = core_ref[0]
    pairs = out_ref.shape[1] // 40
    shard = whole.shape[0] // (4 * pairs)
    upper = iota((8, WIDTH), 0) < 4
    for pair in range(pairs):

        def rows(odd, start, size):
            at = (4 * pair + 2 * odd + core) * shard + start
            return whole[pl.ds(pl.multiple_of(at, 8), size), :]

        for cut in range(CUTS):
            split = 16 * CUTS + 8 * (cut // 2)
            even, odd = rows(0, split, 8), pltpu.roll(rows(1, split, 8), 4, 0)
            mixed = jnp.where(upper, even, odd) if cut % 2 == 0 else jnp.where(upper, odd, even)
            piece = jnp.concatenate([rows(0, 16 * cut, 16), rows(1, 16 * cut, 16), mixed], axis=0).astype(BF16)
            for k in range(CUTS):
                out_ref[cut * CUTS + k, 40 * pair : 40 * pair + 40, :] = piece[:, k * HD : (k + 1) * HD]


def gradient_pieces(core, rows, other_rows, activations, other_activations):
    tok, features = activations.shape
    steps = 2
    held = pl.BlockSpec((tok, WIDTH), lambda m, *_: (0, 0))
    columns = pl.BlockSpec((tok, features // steps), lambda m, *_: (0, m))
    return pl.pallas_call(
        gradient_kernel,
        grid_spec=pltpu.PrefetchScalarGridSpec(
            num_scalar_prefetch=1,
            grid=(steps,),
            in_specs=[held, held, columns, columns],
            out_specs=pl.BlockSpec((CUTS * CUTS, 20 * DEPTH // steps, HD), lambda m, *_: (0, m, 0)),
            scratch_shapes=[pltpu.VMEM((features // steps, WIDTH), F32)],
        ),
        out_shape=jax.ShapeDtypeStruct((CUTS * CUTS, 20 * DEPTH, HD), BF16),
        compiler_params=pltpu.CompilerParams(vmem_limit_bytes=24 * 2**20),
        name="gradient_pieces",
    )(core, rows, other_rows, activations, other_activations)


def plane_sum_kernel(odd_ref, parts_ref, keep_ref, send_ref, whole):
    pairs, rows, _ = whole.shape
    for pair in range(pairs):
        whole[pair] = jnp.sum(parts_ref[:, pair * rows : (pair + 1) * rows, :].astype(F32), axis=0)
    odd = odd_ref[0]
    for target, parity in ((keep_ref, odd), (send_ref, 1 - odd)):
        for pair in range(whole.shape[0]):
            own = whole[pair, pl.ds(pl.multiple_of(parity * 16, 8), 16), :]
            target[pair] = jnp.concatenate([own, whole[pair, 32:40, :]], axis=0).astype(BF16)


def plane_sum(odd, parts):
    count, rows, lanes = parts.shape
    pairs, rows = rows // 40, 40
    out = pl.BlockSpec((pairs, ROWS, lanes), lambda i, *_: (0, 0, 0))
    return pl.pallas_call(
        plane_sum_kernel,
        grid_spec=pltpu.PrefetchScalarGridSpec(
            num_scalar_prefetch=1,
            grid=(1,),
            in_specs=[pl.BlockSpec((count, pairs * rows, lanes), lambda i, *_: (0, 0, 0))],
            out_specs=[out, out],
            scratch_shapes=[pltpu.VMEM((pairs, rows, lanes), F32)],
        ),
        out_shape=[jax.ShapeDtypeStruct((pairs, ROWS, lanes), BF16)] * 2,
        compiler_params=pltpu.CompilerParams(vmem_limit_bytes=24 * 2**20),
        name="plane_sum",
    )(odd, parts)


def join_kernel(odd_ref, pieces_ref, out_ref):
    odd = odd_ref[0]
    upper = iota((8, HD), 0) < 4
    for k in range(CUTS):
        lanes = slice(k * HD, (k + 1) * HD)
        tiles = []
        for cut in range(CUTS):
            out_ref[16 * cut : 16 * cut + 16, lanes] = pieces_ref[cut * CUTS + k, :16, :]
            tiles.append(pieces_ref[cut * CUTS + k, 16:, :].astype(F32))
        last = []
        for low, high in ((tiles[0], tiles[1]), (tiles[2], tiles[3])):
            from_odd = pltpu.roll(jnp.where(upper, high, low), 4, 0)
            last.append(jnp.where(odd == 1, from_odd, jnp.where(upper, low, high)))
        out_ref[16 * CUTS :, lanes] = jnp.concatenate(last, axis=0).astype(BF16)


def join(odd, pieces, rows):
    return pl.pallas_call(
        join_kernel,
        grid_spec=pltpu.PrefetchScalarGridSpec(
            num_scalar_prefetch=1,
            grid=(1,),
            in_specs=[pl.BlockSpec(pieces.shape, lambda i, *_: (0, 0, 0))],
            out_specs=pl.BlockSpec((rows, WIDTH), lambda i, *_: (0, 0)),
        ),
        out_shape=jax.ShapeDtypeStruct((rows, WIDTH), BF16),
        name="join",
    )(odd, pieces)


def cut_kernel(place_ref, rows_ref, tile_ref, out_ref):
    del place_ref
    for at in range(out_ref.shape[0]):
        out_ref[at, :16, :] = rows_ref[...]
        out_ref[at, 16:, :] = tile_ref[...]


def cut_out(shard, place):
    return pl.pallas_call(
        cut_kernel,
        grid_spec=pltpu.PrefetchScalarGridSpec(
            num_scalar_prefetch=1,
            grid=(1,),
            in_specs=[
                pl.BlockSpec((16, HD), lambda i, p: (p[0] // CUTS, p[0] % CUTS)),
                pl.BlockSpec((8, HD), lambda i, p: (2 * CUTS + p[0] // (2 * CUTS), p[0] % CUTS)),
            ],
            out_specs=pl.BlockSpec((DEPTH, ROWS, HD), lambda i, p: (0, 0, 0)),
        ),
        out_shape=jax.ShapeDtypeStruct((DEPTH, ROWS, HD), BF16),
        name="cut_out",
    )(place, shard, shard)


def spread_kernel(place_ref, pieces_ref, out_ref, paired):
    count = pieces_ref.shape[0]

    @pl.when(pl.program_id(0) == 0)
    def _():
        flip = place_ref[0] // CUTS % 2
        upper = iota((8, HD), 0) // 4 == flip
        for z in range(0, count, 2):
            even, odd = ((z + i + count // 2) % count for i in range(2))
            turned = pltpu.roll(pieces_ref[odd, 16:, :].astype(F32), 4, 0)
            mixed = jnp.where(upper, pieces_ref[even, 16:, :].astype(F32), turned)
            part = [pieces_ref[even, :16, :].astype(F32), pieces_ref[odd, :16, :].astype(F32), mixed]
            paired[20 * z : 20 * z + 40, :] = jnp.concatenate(part, axis=0)

    for at in range(out_ref.shape[0]):
        out_ref[at] = paired[...].astype(BF16)


def spread(place, pieces):
    steps = 4
    rows = pieces.shape[0] * 20
    return pl.pallas_call(
        spread_kernel,
        grid_spec=pltpu.PrefetchScalarGridSpec(
            num_scalar_prefetch=1,
            grid=(steps,),
            in_specs=[pl.BlockSpec(pieces.shape, lambda m, *_: (0, 0, 0))],
            out_specs=pl.BlockSpec((PLANE // steps, rows, HD), lambda m, *_: (m, 0, 0)),
            scratch_shapes=[pltpu.VMEM((rows, HD), F32)],
        ),
        out_shape=jax.ShapeDtypeStruct((PLANE, rows, HD), BF16),
        compiler_params=pltpu.CompilerParams(vmem_limit_bytes=24 * 2**20),
        name="spread",
    )(place, pieces)


def project_kernel(core_ref, rows_ref, own_ref, other_ref, out_ref, whole):
    core = core_ref[0]
    pairs = own_ref.shape[1] // 40
    shard = whole.shape[0] // (4 * pairs)
    upper = iota((8, HD), 0) < 4
    for source, parity in ((own_ref, core), (other_ref, 1 - core)):
        for pair in range(pairs):

            def put(odd, start, k, value):
                at = pl.multiple_of((4 * pair + 2 * odd + parity) * shard + start, 16)
                whole[pl.ds(at, 16), k * HD : (k + 1) * HD] = value

            for k in range(CUTS):
                tiles = []
                for cut in range(CUTS):
                    piece = source[cut * CUTS + k, 40 * pair : 40 * pair + 32, :]
                    put(0, 16 * cut, k, piece[:16])
                    put(1, 16 * cut, k, piece[16:])
                    tiles.append(source[cut * CUTS + k, 40 * pair + 32 : 40 * pair + 40, :].astype(F32))
                evens = [jnp.where(upper, tiles[i], tiles[i + 1]) for i in (0, 2)]
                odds = [pltpu.roll(jnp.where(upper, tiles[i + 1], tiles[i]), 4, 0) for i in (0, 2)]
                put(0, 16 * CUTS, k, jnp.concatenate(evens, axis=0).astype(BF16))
                put(1, 16 * CUTS, k, jnp.concatenate(odds, axis=0).astype(BF16))
    out_ref[...] = lax.dot_general(
        rows_ref[...], whole[...], ON_COLUMNS, preferred_element_type=F32
    ).astype(BF16)


def project_back(core, row_grads, own, other, features):
    tok, width = row_grads.shape
    steps = 4
    pieces = pl.BlockSpec((PLANE, own.shape[1] // steps, HD), lambda m, *_: (0, m, 0))
    return pl.pallas_call(
        project_kernel,
        grid_spec=pltpu.PrefetchScalarGridSpec(
            num_scalar_prefetch=1,
            grid=(steps,),
            in_specs=[pl.BlockSpec((tok, width), lambda m, *_: (0, 0)), pieces, pieces],
            out_specs=pl.BlockSpec((tok, features // steps), lambda m, *_: (0, m)),
            scratch_shapes=[pltpu.VMEM((features // steps, width), BF16)],
        ),
        out_shape=jax.ShapeDtypeStruct((tok, features), BF16),
        compiler_params=pltpu.CompilerParams(vmem_limit_bytes=24 * 2**20),
        name="project_back",
    )(core, row_grads, own, other)


def plane_exchange(pieces):
    groups = [list(range(half * PLANE, (half + 1) * PLANE)) for half in range(2)]
    return lax.all_to_all(pieces, "dp", 0, 0, axis_index_groups=groups)


def depth_gather(copies):
    groups = [[2 * ((z + DEPTH // 2) % DEPTH) + core for z in range(DEPTH)] for core in range(2)]
    return lax.all_to_all(copies, "fsdp", 0, 0, axis_index_groups=groups)


def depth_exchange(pieces):
    count = 2 * DEPTH
    groups = [
        [(half * PLANE + at) * count + 2 * z + core for half in range(2) for z in range(odd, DEPTH, 2)]
        for at in range(PLANE)
        for odd in range(2)
        for core in range(2)
    ]
    return lax.all_to_all(pieces, BOTH, 0, 0, axis_index_groups=groups)


def added(one, two):
    return (one.astype(F32) + two.astype(F32)).astype(BF16)


def local(activations, value_weight, queries, key_rows, context_grad, segment, send_slot):
    tok, features = activations.shape
    block = (queries.shape[0] - tok) // SECTIONS
    half = lax.axis_size("dp") // 2
    place = (lax.axis_index("dp") % PLANE).astype(jnp.int32).reshape(1)
    core = (lax.axis_index("fsdp") % 2).astype(jnp.int32).reshape(1)
    odd = (lax.axis_index("fsdp") // 2 % 2).astype(jnp.int32).reshape(1)

    first, second = messages(queries, key_rows, context_grad, tok, block)
    first = swapped(first, "dp", half)
    second = swapped(second, "dp", half // 2)
    copies = spread(place, depth_gather(cut_out(value_weight, place)))

    def beside(held):
        copies, _, act = held
        return plane_exchange(copies), attend(queries, key_rows, context_grad, segment), swapped(act, "fsdp", 1)

    held = (copies, jnp.zeros((tok, WIDTH), BF16), activations)
    own_weight, main, other_act = lax.cond(
        lax.axis_index("dp") < lax.axis_size("dp"), beside, lambda held: held, held
    )
    main, own_weight = lax.optimization_barrier((main, own_weight))

    row_grads = own_rows(send_slot, main, first, second, block)
    other_rows = swapped(row_grads, "fsdp", 1)
    parts = plane_exchange(gradient_pieces(core, row_grads, other_rows, activations, other_act))
    other_weight = swapped(own_weight, "fsdp", 1)

    keep, send = plane_sum(odd, parts)
    came = swapped(send, "fsdp", 2)
    depth_part = added(keep, came)
    depth_parts = depth_exchange(jnp.concatenate([depth_part, depth_part], axis=0))
    input_grad = project_back(core, row_grads, own_weight, other_weight, features)
    depth_parts, input_grad = lax.optimization_barrier((depth_parts, input_grad))
    finished = jnp.sum(depth_parts.astype(F32), axis=0).astype(BF16)
    finished = plane_exchange(jnp.broadcast_to(finished[None], (PLANE, *finished.shape)))
    weight_grad = join(odd, finished, value_weight.shape[0])
    return (input_grad, weight_grad)


def solution(mesh):
    rows = P(("dp", "fsdp"), None)
    flat = P(("dp", "fsdp"))
    return jax.shard_map(
        local,
        mesh=mesh,
        in_specs=(rows, P("fsdp", None), rows, rows, rows, flat, flat),
        out_specs=(rows, P("fsdp", None)),
        check_vma=False,
    )
```

```python
import functools
import math

import jax
import jax.numpy as jnp
from jax import lax
from jax.experimental import pallas as pl
from jax.experimental.pallas import tpu as pltpu
from jax.sharding import PartitionSpec as P

KVH = 4
GROUP = 5
HD = 128
SECTIONS = 2
LEAST = 16
PLANE = 16
DEPTH = 16
CUTS = 4
ROWS = 24
BOTH = ("dp", "fsdp")
BF16 = jnp.bfloat16
F32 = jnp.float32
WIDTH = KVH * HD
FEATURES = KVH * GROUP * HD
LATE = GROUP * LEAST
SUMS = FEATURES
PROBS = SUMS + WIDTH
MESSAGE = PROBS + 2 * KVH * LATE
SCALE = 1.0 / math.sqrt(HD)
ON_COLUMNS = (((1,), (1,)), ((), ()))


def swapped(block, axis, distance):
    route = [(low, low ^ distance) for low in range(lax.axis_size(axis))]
    return lax.ppermute(block, axis, route)


def softmax_down(scores, allowed):
    masked = jnp.where(allowed, scores * SCALE, -jnp.inf)
    exponent = jnp.exp(masked - jnp.max(masked, axis=0, keepdims=True))
    return exponent * (1.0 / jnp.sum(exponent, axis=0, keepdims=True))


def iota(shape, dim):
    return lax.broadcasted_iota(jnp.int32, shape, dim)


def message_kernel(block, q_ref, k_ref, c_ref, *out_refs):
    for section, out_ref in enumerate(out_refs):
        low = section * block
        out_ref[:, :FEATURES] = c_ref[low + LEAST : low + block, :]
        pad = jnp.zeros((HD - LATE, HD), BF16)
        late = []
        for h in range(KVH):

            def stacked(ref, start):
                heads = [ref[start : start + LEAST, (h * GROUP + g) * HD : (h * GROUP + g + 1) * HD] for g in range(GROUP)]
                return jnp.concatenate([*heads, pad], axis=0)

            keys = k_ref[low : low + block, h * HD : (h + 1) * HD]
            scores = lax.dot_general(keys, stacked(q_ref, low + LEAST), ON_COLUMNS, preferred_element_type=F32)
            allowed = iota((block, HD), 0) <= iota((block, HD), 1) % LEAST + LEAST
            late.append(softmax_down(scores, allowed)[:, :LATE])

            scores = lax.dot_general(keys[:LEAST], stacked(q_ref, low), ON_COLUMNS, preferred_element_type=F32)
            allowed = iota((LEAST, HD), 0) <= iota((LEAST, HD), 1) % LEAST
            probs = softmax_down(scores, allowed).astype(BF16)
            sums = jnp.dot(probs, stacked(c_ref, low), preferred_element_type=F32)
            out_ref[:, SUMS + h * HD : SUMS + (h + 1) * HD] = sums.astype(BF16)
        late = [x[start : start + LEAST] for start in range(0, block, LEAST) for x in late]
        out_ref[:, PROBS:] = jnp.concatenate(late, axis=1).astype(BF16)


def messages(queries, key_rows, context_grad, tok, block):
    both = SECTIONS * block
    last = tok // both
    specs = [pl.BlockSpec((both, x.shape[1]), lambda i: (last, 0)) for x in (queries, key_rows, context_grad)]
    shape = (block - LEAST, MESSAGE)
    return pl.pallas_call(
        functools.partial(message_kernel, block),
        grid=(1,),
        in_specs=specs,
        out_specs=[pl.BlockSpec(shape, lambda i: (0, 0))] * SECTIONS,
        out_shape=[jax.ShapeDtypeStruct(shape, BF16)] * SECTIONS,
        compiler_params=pltpu.CompilerParams(vmem_limit_bytes=24 * 2**20),
        name="messages",
    )(queries, key_rows, context_grad)


def sent_block(slot, message_ref, low, block):
    inside = (slot >= low) & (slot < low + block)
    count = jnp.sum(inside.astype(jnp.int32), axis=0, keepdims=True)
    held = iota((block, HD), 1) % LEAST + LEAST < count
    pad = jnp.zeros((HD - LATE, HD), BF16)
    late = message_ref[:, PROBS:].astype(F32)
    heads = []
    for h in range(KVH):
        parts = [late[:, (half * KVH + h) * LATE : (half * KVH + h + 1) * LATE] for half in range(block // LEAST)]
        probs = jnp.concatenate(parts, axis=0)
        probs = jnp.concatenate([probs, jnp.zeros((block, HD - LATE), F32)], axis=1)
        probs = jnp.where(held, probs, 0.0).astype(BF16)
        rows = [message_ref[:, (h * GROUP + g) * HD : (h * GROUP + g + 1) * HD] for g in range(GROUP)]
        sums = jnp.dot(probs, jnp.concatenate([*rows, pad], axis=0), preferred_element_type=F32)
        early = message_ref[:, SUMS + h * HD : SUMS + (h + 1) * HD].astype(F32)
        heads.append(sums + jnp.concatenate([early, jnp.zeros((block - LEAST, HD), F32)], axis=0))
    return jnp.concatenate(heads, axis=1).astype(BF16)


def attend_kernel(col_ref, row_ref, q_ref, k_ref, c_ref, out_ref):
    tok = q_ref.shape[0]
    query = jnp.concatenate([q_ref[:, g * HD : (g + 1) * HD] for g in range(GROUP)], axis=0)
    context = jnp.concatenate([c_ref[:, g * HD : (g + 1) * HD] for g in range(GROUP)], axis=0)
    allowed = (col_ref[...] == row_ref[...]) & (iota((tok, tok), 0) <= iota((tok, tok), 1))
    bias = jnp.where(allowed, 0.0, -jnp.inf)
    scores = lax.dot_general(k_ref[...], query, ON_COLUMNS, preferred_element_type=F32) * SCALE
    masked = scores + jnp.concatenate([bias] * GROUP, axis=1)
    exponent = jnp.exp(masked - jnp.max(masked, axis=0, keepdims=True))
    probs = (exponent * (1.0 / jnp.sum(exponent, axis=0, keepdims=True))).astype(BF16)
    out_ref[...] = jnp.dot(probs, context, preferred_element_type=F32).astype(BF16)


def attend(queries, key_rows, context_grad, segment):
    tok = segment.shape[0]
    wide = pl.BlockSpec((tok, GROUP * HD), lambda h: (0, h))
    thin = pl.BlockSpec((tok, HD), lambda h: (0, h))
    return pl.pallas_call(
        attend_kernel,
        grid=(KVH,),
        in_specs=[
            pl.BlockSpec((tok, 1), lambda h: (0, 0)),
            pl.BlockSpec((1, tok), lambda h: (0, 0)),
            wide,
            thin,
            wide,
        ],
        out_specs=thin,
        out_shape=jax.ShapeDtypeStruct((tok, WIDTH), BF16),
        name="attend",
    )(segment.reshape(tok, 1), segment.reshape(1, tok), queries, key_rows, context_grad)


def rows_kernel(block, slot_ref, main_ref, first_ref, second_ref, out_ref):
    slot = slot_ref[...]
    tok = slot.shape[0]
    parts = [sent_block(slot, ref, tok + s * block, block) for s, ref in enumerate((first_ref, second_ref))]
    held = jnp.concatenate([main_ref[...], *parts], axis=0)
    chosen = (slot == iota((tok, held.shape[0]), 1)).astype(F32).astype(BF16)
    out_ref[...] = jnp.dot(chosen, held, preferred_element_type=F32).astype(BF16)


def own_rows(send_slot, main, first, second, block):
    tok = main.shape[0]
    operands = (send_slot.reshape(tok, 1), main, first, second)
    return pl.pallas_call(
        functools.partial(rows_kernel, block),
        grid=(1,),
        in_specs=[pl.BlockSpec(x.shape, lambda i: (0, 0)) for x in operands],
        out_specs=pl.BlockSpec(main.shape, lambda i: (0, 0)),
        out_shape=jax.ShapeDtypeStruct(main.shape, BF16),
        compiler_params=pltpu.CompilerParams(vmem_limit_bytes=24 * 2**20),
        name="own_rows",
    )(*operands)


def gradient_kernel(core_ref, rows_ref, other_rows_ref, act_ref, other_act_ref, out_ref, whole):
    whole[...] = lax.dot_general(
        jnp.concatenate([act_ref[...], other_act_ref[...]], axis=0),
        jnp.concatenate([rows_ref[...], other_rows_ref[...]], axis=0),
        (((0,), (0,)), ((), ())),
        preferred_element_type=F32,
    )
    core = core_ref[0]
    pairs = out_ref.shape[1] // 40
    shard = whole.shape[0] // (4 * pairs)
    upper = iota((8, WIDTH), 0) < 4
    for pair in range(pairs):

        def rows(odd, start, size):
            at = (4 * pair + 2 * odd + core) * shard + start
            return whole[pl.ds(pl.multiple_of(at, 8), size), :]

        for cut in range(CUTS):
            split = 16 * CUTS + 8 * (cut // 2)
            even, odd = rows(0, split, 8), pltpu.roll(rows(1, split, 8), 4, 0)
            mixed = jnp.where(upper, even, odd) if cut % 2 == 0 else jnp.where(upper, odd, even)
            piece = jnp.concatenate([rows(0, 16 * cut, 16), rows(1, 16 * cut, 16), mixed], axis=0).astype(BF16)
            for k in range(CUTS):
                out_ref[cut * CUTS + k, 40 * pair : 40 * pair + 40, :] = piece[:, k * HD : (k + 1) * HD]


def gradient_pieces(core, rows, other_rows, activations, other_activations):
    tok, features = activations.shape
    steps = 2
    held = pl.BlockSpec((tok, WIDTH), lambda m, *_: (0, 0))
    columns = pl.BlockSpec((tok, features // steps), lambda m, *_: (0, m))
    return pl.pallas_call(
        gradient_kernel,
        grid_spec=pltpu.PrefetchScalarGridSpec(
            num_scalar_prefetch=1,
            grid=(steps,),
            in_specs=[held, held, columns, columns],
            out_specs=pl.BlockSpec((CUTS * CUTS, 20 * DEPTH // steps, HD), lambda m, *_: (0, m, 0)),
            scratch_shapes=[pltpu.VMEM((features // steps, WIDTH), F32)],
        ),
        out_shape=jax.ShapeDtypeStruct((CUTS * CUTS, 20 * DEPTH, HD), BF16),
        compiler_params=pltpu.CompilerParams(vmem_limit_bytes=24 * 2**20),
        name="gradient_pieces",
    )(core, rows, other_rows, activations, other_activations)


def plane_sum_kernel(odd_ref, parts_ref, keep_ref, send_ref, whole):
    pairs, rows, _ = whole.shape
    for pair in range(pairs):
        whole[pair] = jnp.sum(parts_ref[:, pair * rows : (pair + 1) * rows, :].astype(F32), axis=0)
    odd = odd_ref[0]
    for target, parity in ((keep_ref, odd), (send_ref, 1 - odd)):
        for pair in range(whole.shape[0]):
            own = whole[pair, pl.ds(pl.multiple_of(parity * 16, 8), 16), :]
            target[pair] = jnp.concatenate([own, whole[pair, 32:40, :]], axis=0).astype(BF16)


def plane_sum(odd, parts):
    count, rows, lanes = parts.shape
    pairs, rows = rows // 40, 40
    out = pl.BlockSpec((pairs, ROWS, lanes), lambda i, *_: (0, 0, 0))
    return pl.pallas_call(
        plane_sum_kernel,
        grid_spec=pltpu.PrefetchScalarGridSpec(
            num_scalar_prefetch=1,
            grid=(1,),
            in_specs=[pl.BlockSpec((count, pairs * rows, lanes), lambda i, *_: (0, 0, 0))],
            out_specs=[out, out],
            scratch_shapes=[pltpu.VMEM((pairs, rows, lanes), F32)],
        ),
        out_shape=[jax.ShapeDtypeStruct((pairs, ROWS, lanes), BF16)] * 2,
        compiler_params=pltpu.CompilerParams(vmem_limit_bytes=24 * 2**20),
        name="plane_sum",
    )(odd, parts)


def join_kernel(odd_ref, pieces_ref, out_ref):
    odd = odd_ref[0]
    upper = iota((8, HD), 0) < 4
    for k in range(CUTS):
        lanes = slice(k * HD, (k + 1) * HD)
        tiles = []
        for cut in range(CUTS):
            out_ref[16 * cut : 16 * cut + 16, lanes] = pieces_ref[cut * CUTS + k, :16, :]
            tiles.append(pieces_ref[cut * CUTS + k, 16:, :].astype(F32))
        last = []
        for low, high in ((tiles[0], tiles[1]), (tiles[2], tiles[3])):
            from_odd = pltpu.roll(jnp.where(upper, high, low), 4, 0)
            last.append(jnp.where(odd == 1, from_odd, jnp.where(upper, low, high)))
        out_ref[16 * CUTS :, lanes] = jnp.concatenate(last, axis=0).astype(BF16)


def join(odd, pieces, rows):
    return pl.pallas_call(
        join_kernel,
        grid_spec=pltpu.PrefetchScalarGridSpec(
            num_scalar_prefetch=1,
            grid=(1,),
            in_specs=[pl.BlockSpec(pieces.shape, lambda i, *_: (0, 0, 0))],
            out_specs=pl.BlockSpec((rows, WIDTH), lambda i, *_: (0, 0)),
        ),
        out_shape=jax.ShapeDtypeStruct((rows, WIDTH), BF16),
        name="join",
    )(odd, pieces)


def cut_kernel(place_ref, rows_ref, tile_ref, out_ref):
    del place_ref
    for at in range(out_ref.shape[0]):
        out_ref[at, :16, :] = rows_ref[...]
        out_ref[at, 16:, :] = tile_ref[...]


def cut_out(shard, place):
    return pl.pallas_call(
        cut_kernel,
        grid_spec=pltpu.PrefetchScalarGridSpec(
            num_scalar_prefetch=1,
            grid=(1,),
            in_specs=[
                pl.BlockSpec((16, HD), lambda i, p: (p[0] // CUTS, p[0] % CUTS)),
                pl.BlockSpec((8, HD), lambda i, p: (2 * CUTS + p[0] // (2 * CUTS), p[0] % CUTS)),
            ],
            out_specs=pl.BlockSpec((DEPTH, ROWS, HD), lambda i, p: (0, 0, 0)),
        ),
        out_shape=jax.ShapeDtypeStruct((DEPTH, ROWS, HD), BF16),
        name="cut_out",
    )(place, shard, shard)


def spread_kernel(place_ref, pieces_ref, out_ref, paired):
    count = pieces_ref.shape[0]

    @pl.when(pl.program_id(0) == 0)
    def _():
        flip = place_ref[0] // CUTS % 2
        upper = iota((8, HD), 0) // 4 == flip
        for z in range(0, count, 2):
            even, odd = ((z + i + count // 2) % count for i in range(2))
            turned = pltpu.roll(pieces_ref[odd, 16:, :].astype(F32), 4, 0)
            mixed = jnp.where(upper, pieces_ref[even, 16:, :].astype(F32), turned)
            part = [pieces_ref[even, :16, :].astype(F32), pieces_ref[odd, :16, :].astype(F32), mixed]
            paired[20 * z : 20 * z + 40, :] = jnp.concatenate(part, axis=0)

    for at in range(out_ref.shape[0]):
        out_ref[at] = paired[...].astype(BF16)


def spread(place, pieces):
    steps = 4
    rows = pieces.shape[0] * 20
    return pl.pallas_call(
        spread_kernel,
        grid_spec=pltpu.PrefetchScalarGridSpec(
            num_scalar_prefetch=1,
            grid=(steps,),
            in_specs=[pl.BlockSpec(pieces.shape, lambda m, *_: (0, 0, 0))],
            out_specs=pl.BlockSpec((PLANE // steps, rows, HD), lambda m, *_: (m, 0, 0)),
            scratch_shapes=[pltpu.VMEM((rows, HD), F32)],
        ),
        out_shape=jax.ShapeDtypeStruct((PLANE, rows, HD), BF16),
        compiler_params=pltpu.CompilerParams(vmem_limit_bytes=24 * 2**20),
        name="spread",
    )(place, pieces)


def project_kernel(core_ref, rows_ref, own_ref, other_ref, out_ref, whole):
    core = core_ref[0]
    pairs = own_ref.shape[1] // 40
    shard = whole.shape[0] // (4 * pairs)
    upper = iota((8, HD), 0) < 4
    for source, parity in ((own_ref, core), (other_ref, 1 - core)):
        for pair in range(pairs):

            def put(odd, start, k, value):
                at = pl.multiple_of((4 * pair + 2 * odd + parity) * shard + start, 16)
                whole[pl.ds(at, 16), k * HD : (k + 1) * HD] = value

            for k in range(CUTS):
                tiles = []
                for cut in range(CUTS):
                    piece = source[cut * CUTS + k, 40 * pair : 40 * pair + 32, :]
                    put(0, 16 * cut, k, piece[:16])
                    put(1, 16 * cut, k, piece[16:])
                    tiles.append(source[cut * CUTS + k, 40 * pair + 32 : 40 * pair + 40, :].astype(F32))
                evens = [jnp.where(upper, tiles[i], tiles[i + 1]) for i in (0, 2)]
                odds = [pltpu.roll(jnp.where(upper, tiles[i + 1], tiles[i]), 4, 0) for i in (0, 2)]
                put(0, 16 * CUTS, k, jnp.concatenate(evens, axis=0).astype(BF16))
                put(1, 16 * CUTS, k, jnp.concatenate(odds, axis=0).astype(BF16))
    out_ref[...] = lax.dot_general(
        rows_ref[...], whole[...], ON_COLUMNS, preferred_element_type=F32
    ).astype(BF16)


def project_back(core, row_grads, own, other, features):
    tok, width = row_grads.shape
    steps = 4
    pieces = pl.BlockSpec((PLANE, own.shape[1] // steps, HD), lambda m, *_: (0, m, 0))
    return pl.pallas_call(
        project_kernel,
        grid_spec=pltpu.PrefetchScalarGridSpec(
            num_scalar_prefetch=1,
            grid=(steps,),
            in_specs=[pl.BlockSpec((tok, width), lambda m, *_: (0, 0)), pieces, pieces],
            out_specs=pl.BlockSpec((tok, features // steps), lambda m, *_: (0, m)),
            scratch_shapes=[pltpu.VMEM((features // steps, width), BF16)],
        ),
        out_shape=jax.ShapeDtypeStruct((tok, features), BF16),
        compiler_params=pltpu.CompilerParams(vmem_limit_bytes=24 * 2**20),
        name="project_back",
    )(core, row_grads, own, other)


def plane_exchange(pieces):
    groups = [list(range(half * PLANE, (half + 1) * PLANE)) for half in range(2)]
    return lax.all_to_all(pieces, "dp", 0, 0, axis_index_groups=groups)


def depth_gather(copies):
    groups = [[2 * ((z + DEPTH // 2) % DEPTH) + core for z in range(DEPTH)] for core in range(2)]
    return lax.all_to_all(copies, "fsdp", 0, 0, axis_index_groups=groups)


def depth_exchange(pieces):
    count = 2 * DEPTH
    groups = [
        [(half * PLANE + at) * count + 2 * z + core for half in (1, 0) for z in range(odd, DEPTH, 2)]
        for at in range(PLANE)
        for odd in range(2)
        for core in range(2)
    ]
    return lax.all_to_all(pieces, BOTH, 0, 0, axis_index_groups=groups)


def added(one, two):
    return (one.astype(F32) + two.astype(F32)).astype(BF16)


def local(activations, value_weight, queries, key_rows, context_grad, segment, send_slot):
    tok, features = activations.shape
    block = (queries.shape[0] - tok) // SECTIONS
    half = lax.axis_size("dp") // 2
    place = (lax.axis_index("dp") % PLANE).astype(jnp.int32).reshape(1)
    core = (lax.axis_index("fsdp") % 2).astype(jnp.int32).reshape(1)
    odd = (lax.axis_index("fsdp") // 2 % 2).astype(jnp.int32).reshape(1)

    first, second = messages(queries, key_rows, context_grad, tok, block)
    first = swapped(first, "dp", half)
    second = swapped(second, "dp", half // 2)
    copies = spread(place, depth_gather(cut_out(value_weight, place)))

    def beside(held):
        copies, _, act = held
        return plane_exchange(copies), attend(queries, key_rows, context_grad, segment), swapped(act, "fsdp", 1)

    held = (copies, jnp.zeros((tok, WIDTH), BF16), activations)
    own_weight, main, other_act = lax.cond(
        lax.axis_index("dp") < lax.axis_size("dp"), beside, lambda held: held, held
    )
    main, own_weight = lax.optimization_barrier((main, own_weight))

    row_grads = own_rows(send_slot, main, first, second, block)
    other_rows = swapped(row_grads, "fsdp", 1)
    parts = plane_exchange(gradient_pieces(core, row_grads, other_rows, activations, other_act))
    other_weight = swapped(own_weight, "fsdp", 1)

    keep, send = plane_sum(odd, parts)
    came = swapped(send, "fsdp", 2)
    depth_part = added(keep, came)
    depth_parts = depth_exchange(jnp.concatenate([depth_part, depth_part], axis=0))
    input_grad = project_back(core, row_grads, own_weight, other_weight, features)
    depth_parts, input_grad = lax.optimization_barrier((depth_parts, input_grad))
    finished = jnp.sum(depth_parts.astype(F32), axis=0).astype(BF16)
    finished = plane_exchange(jnp.broadcast_to(finished[None], (PLANE, *finished.shape)))
    weight_grad = join(odd, finished, value_weight.shape[0])
    return (input_grad, weight_grad)


def solution(mesh):
    rows = P(("dp", "fsdp"), None)
    flat = P(("dp", "fsdp"))
    return jax.shard_map(
        local,
        mesh=mesh,
        in_specs=(rows, P("fsdp", None), rows, rows, rows, flat, flat),
        out_specs=(rows, P("fsdp", None)),
        check_vma=False,
    )
```

```python
import functools
import math

import jax
import jax.numpy as jnp
from jax import lax
from jax.experimental import pallas as pl
from jax.experimental.pallas import tpu as pltpu
from jax.sharding import PartitionSpec as P

KVH = 4
GROUP = 5
HD = 128
SECTIONS = 2
LEAST = 16
PLANE = 16
DEPTH = 16
CUTS = 4
ROWS = 24
BOTH = ("dp", "fsdp")
BF16 = jnp.bfloat16
F32 = jnp.float32
WIDTH = KVH * HD
FEATURES = KVH * GROUP * HD
LATE = GROUP * LEAST
SUMS = FEATURES
PROBS = SUMS + WIDTH
MESSAGE = PROBS + 2 * KVH * LATE
SCALE = 1.0 / math.sqrt(HD)
ON_COLUMNS = (((1,), (1,)), ((), ()))


def swapped(block, axis, distance):
    route = [(low, low ^ distance) for low in range(lax.axis_size(axis))]
    return lax.ppermute(block, axis, route)


def softmax_down(scores, allowed):
    masked = jnp.where(allowed, scores * SCALE, -jnp.inf)
    exponent = jnp.exp(masked - jnp.max(masked, axis=0, keepdims=True))
    return exponent * (1.0 / jnp.sum(exponent, axis=0, keepdims=True))


def iota(shape, dim):
    return lax.broadcasted_iota(jnp.int32, shape, dim)


def message_kernel(block, q_ref, k_ref, c_ref, *out_refs):
    for section, out_ref in enumerate(out_refs):
        low = section * block
        out_ref[:, :FEATURES] = c_ref[low + LEAST : low + block, :]
        pad = jnp.zeros((HD - LATE, HD), BF16)
        late = []
        for h in range(KVH):

            def stacked(ref, start):
                heads = [ref[start : start + LEAST, (h * GROUP + g) * HD : (h * GROUP + g + 1) * HD] for g in range(GROUP)]
                return jnp.concatenate([*heads, pad], axis=0)

            keys = k_ref[low : low + block, h * HD : (h + 1) * HD]
            scores = lax.dot_general(keys, stacked(q_ref, low + LEAST), ON_COLUMNS, preferred_element_type=F32)
            allowed = iota((block, HD), 0) <= iota((block, HD), 1) % LEAST + LEAST
            late.append(softmax_down(scores, allowed)[:, :LATE])

            scores = lax.dot_general(keys[:LEAST], stacked(q_ref, low), ON_COLUMNS, preferred_element_type=F32)
            allowed = iota((LEAST, HD), 0) <= iota((LEAST, HD), 1) % LEAST
            probs = softmax_down(scores, allowed).astype(BF16)
            sums = jnp.dot(probs, stacked(c_ref, low), preferred_element_type=F32)
            out_ref[:, SUMS + h * HD : SUMS + (h + 1) * HD] = sums.astype(BF16)
        late = [x[start : start + LEAST] for start in range(0, block, LEAST) for x in late]
        out_ref[:, PROBS:] = jnp.concatenate(late, axis=1).astype(BF16)


def messages(queries, key_rows, context_grad, tok, block):
    both = SECTIONS * block
    last = tok // both
    specs = [pl.BlockSpec((both, x.shape[1]), lambda i: (last, 0)) for x in (queries, key_rows, context_grad)]
    shape = (block - LEAST, MESSAGE)
    return pl.pallas_call(
        functools.partial(message_kernel, block),
        grid=(1,),
        in_specs=specs,
        out_specs=[pl.BlockSpec(shape, lambda i: (0, 0))] * SECTIONS,
        out_shape=[jax.ShapeDtypeStruct(shape, BF16)] * SECTIONS,
        compiler_params=pltpu.CompilerParams(vmem_limit_bytes=24 * 2**20),
        name="messages",
    )(queries, key_rows, context_grad)


def sent_block(slot, message_ref, low, block):
    inside = (slot >= low) & (slot < low + block)
    count = jnp.sum(inside.astype(jnp.int32), axis=0, keepdims=True)
    held = iota((block, HD), 1) % LEAST + LEAST < count
    pad = jnp.zeros((HD - LATE, HD), BF16)
    late = message_ref[:, PROBS:].astype(F32)
    heads = []
    for h in range(KVH):
        parts = [late[:, (half * KVH + h) * LATE : (half * KVH + h + 1) * LATE] for half in range(block // LEAST)]
        probs = jnp.concatenate(parts, axis=0)
        probs = jnp.concatenate([probs, jnp.zeros((block, HD - LATE), F32)], axis=1)
        probs = jnp.where(held, probs, 0.0).astype(BF16)
        rows = [message_ref[:, (h * GROUP + g) * HD : (h * GROUP + g + 1) * HD] for g in range(GROUP)]
        sums = jnp.dot(probs, jnp.concatenate([*rows, pad], axis=0), preferred_element_type=F32)
        early = message_ref[:, SUMS + h * HD : SUMS + (h + 1) * HD].astype(F32)
        heads.append(sums + jnp.concatenate([early, jnp.zeros((block - LEAST, HD), F32)], axis=0))
    return jnp.concatenate(heads, axis=1).astype(BF16)


def attend_kernel(col_ref, row_ref, q_ref, k_ref, c_ref, out_ref):
    tok = q_ref.shape[0]
    query = jnp.concatenate([q_ref[:, g * HD : (g + 1) * HD] for g in range(GROUP)], axis=0)
    context = jnp.concatenate([c_ref[:, g * HD : (g + 1) * HD] for g in range(GROUP)], axis=0)
    allowed = (col_ref[...] == row_ref[...]) & (iota((tok, tok), 0) <= iota((tok, tok), 1))
    bias = jnp.where(allowed, 0.0, -jnp.inf)
    scores = lax.dot_general(k_ref[...], query, ON_COLUMNS, preferred_element_type=F32) * SCALE
    masked = scores + jnp.concatenate([bias] * GROUP, axis=1)
    exponent = jnp.exp(masked - jnp.max(masked, axis=0, keepdims=True))
    probs = (exponent * (1.0 / jnp.sum(exponent, axis=0, keepdims=True))).astype(BF16)
    out_ref[...] = jnp.dot(probs, context, preferred_element_type=F32).astype(BF16)


def attend(queries, key_rows, context_grad, segment):
    tok = segment.shape[0]
    wide = pl.BlockSpec((tok, GROUP * HD), lambda h: (0, h))
    thin = pl.BlockSpec((tok, HD), lambda h: (0, h))
    return pl.pallas_call(
        attend_kernel,
        grid=(KVH,),
        in_specs=[
            pl.BlockSpec((tok, 1), lambda h: (0, 0)),
            pl.BlockSpec((1, tok), lambda h: (0, 0)),
            wide,
            thin,
            wide,
        ],
        out_specs=thin,
        out_shape=jax.ShapeDtypeStruct((tok, WIDTH), BF16),
        name="attend",
    )(segment.reshape(tok, 1), segment.reshape(1, tok), queries, key_rows, context_grad)


def rows_kernel(block, slot_ref, main_ref, first_ref, second_ref, out_ref):
    slot = slot_ref[...]
    tok = slot.shape[0]
    parts = [sent_block(slot, ref, tok + s * block, block) for s, ref in enumerate((first_ref, second_ref))]
    held = jnp.concatenate([main_ref[...], *parts], axis=0)
    chosen = (slot == iota((tok, held.shape[0]), 1)).astype(F32).astype(BF16)
    out_ref[...] = jnp.dot(chosen, held, preferred_element_type=F32).astype(BF16)


def own_rows(send_slot, main, first, second, block):
    tok = main.shape[0]
    operands = (send_slot.reshape(tok, 1), main, first, second)
    return pl.pallas_call(
        functools.partial(rows_kernel, block),
        grid=(1,),
        in_specs=[pl.BlockSpec(x.shape, lambda i: (0, 0)) for x in operands],
        out_specs=pl.BlockSpec(main.shape, lambda i: (0, 0)),
        out_shape=jax.ShapeDtypeStruct(main.shape, BF16),
        compiler_params=pltpu.CompilerParams(vmem_limit_bytes=24 * 2**20),
        name="own_rows",
    )(*operands)


def gradient_kernel(core_ref, rows_ref, other_rows_ref, act_ref, other_act_ref, out_ref, whole):
    whole[...] = lax.dot_general(
        jnp.concatenate([act_ref[...], other_act_ref[...]], axis=0),
        jnp.concatenate([rows_ref[...], other_rows_ref[...]], axis=0),
        (((0,), (0,)), ((), ())),
        preferred_element_type=F32,
    )
    core = core_ref[0]
    quads = out_ref.shape[1] // 40
    shard = whole.shape[0] // (8 * quads)
    upper = iota((8, WIDTH), 0) < 4
    for quad in range(quads):
        for parity in range(2):

            def rows(later, start, size):
                at = (2 * (4 * quad + 2 * later + parity) + core) * shard + start
                return whole[pl.ds(pl.multiple_of(at, 8), size), :]

            for cut in range(CUTS):
                split = 16 * CUTS + 8 * (cut // 2)
                one, two = rows(0, split, 8), pltpu.roll(rows(1, split, 8), 4, 0)
                mixed = jnp.where(upper, one, two) if cut % 2 == 0 else jnp.where(upper, two, one)
                piece = jnp.concatenate([rows(0, 16 * cut, 16), rows(1, 16 * cut, 16), mixed], axis=0).astype(BF16)
                for k in range(CUTS):
                    target = 2 * (cut * CUTS + k) + parity
                    out_ref[target, 40 * quad : 40 * quad + 40, :] = piece[:, k * HD : (k + 1) * HD]


def gradient_pieces(core, rows, other_rows, activations, other_activations):
    tok, features = activations.shape
    steps = 2
    held = pl.BlockSpec((tok, WIDTH), lambda m, *_: (0, 0))
    columns = pl.BlockSpec((tok, features // steps), lambda m, *_: (0, m))
    return pl.pallas_call(
        gradient_kernel,
        grid_spec=pltpu.PrefetchScalarGridSpec(
            num_scalar_prefetch=1,
            grid=(steps,),
            in_specs=[held, held, columns, columns],
            out_specs=pl.BlockSpec((2 * PLANE, 10 * DEPTH // steps, HD), lambda m, *_: (0, m, 0)),
            scratch_shapes=[pltpu.VMEM((features // steps, WIDTH), F32)],
        ),
        out_shape=jax.ShapeDtypeStruct((2 * PLANE, 10 * DEPTH, HD), BF16),
        compiler_params=pltpu.CompilerParams(vmem_limit_bytes=24 * 2**20),
        name="gradient_pieces",
    )(core, rows, other_rows, activations, other_activations)


def plane_sum_kernel(parts_ref, out_ref):
    count = out_ref.shape[0] // 2
    for pair in range(count // 2):
        total = jnp.sum(parts_ref[:, 40 * pair : 40 * pair + 40, :].astype(F32), axis=0)
        for later in range(2):
            piece = jnp.concatenate([total[16 * later : 16 * later + 16], total[32:]], axis=0).astype(BF16)
            for half in range(2):
                out_ref[half * count + 2 * pair + later] = piece


def plane_sum(parts):
    _, rows, lanes = parts.shape
    out = (rows // 10, ROWS, lanes)
    return pl.pallas_call(
        plane_sum_kernel,
        grid=(1,),
        in_specs=[pl.BlockSpec(parts.shape, lambda i: (0, 0, 0))],
        out_specs=pl.BlockSpec(out, lambda i: (0, 0, 0)),
        out_shape=jax.ShapeDtypeStruct(out, BF16),
        compiler_params=pltpu.CompilerParams(vmem_limit_bytes=24 * 2**20),
        name="plane_sum",
    )(parts)


def join_kernel(later_ref, pieces_ref, out_ref):
    later = later_ref[0]
    upper = iota((8, HD), 0) < 4
    for k in range(CUTS):
        lanes = slice(k * HD, (k + 1) * HD)
        tiles = []
        for cut in range(CUTS):
            out_ref[16 * cut : 16 * cut + 16, lanes] = pieces_ref[cut * CUTS + k, :16, :]
            tiles.append(pieces_ref[cut * CUTS + k, 16:, :].astype(F32))
        last = []
        for low, high in ((tiles[0], tiles[1]), (tiles[2], tiles[3])):
            turned = pltpu.roll(jnp.where(upper, high, low), 4, 0)
            last.append(jnp.where(later == 1, turned, jnp.where(upper, low, high)))
        out_ref[16 * CUTS :, lanes] = jnp.concatenate(last, axis=0).astype(BF16)


def join(later, pieces, rows):
    return pl.pallas_call(
        join_kernel,
        grid_spec=pltpu.PrefetchScalarGridSpec(
            num_scalar_prefetch=1,
            grid=(1,),
            in_specs=[pl.BlockSpec(pieces.shape, lambda i, *_: (0, 0, 0))],
            out_specs=pl.BlockSpec((rows, WIDTH), lambda i, *_: (0, 0)),
        ),
        out_shape=jax.ShapeDtypeStruct((rows, WIDTH), BF16),
        name="join",
    )(later, pieces)


def cut_kernel(place_ref, rows_ref, tile_ref, out_ref):
    del place_ref
    for at in range(out_ref.shape[0]):
        out_ref[at, :16, :] = rows_ref[...]
        out_ref[at, 16:, :] = tile_ref[...]


def cut_out(shard, place):
    return pl.pallas_call(
        cut_kernel,
        grid_spec=pltpu.PrefetchScalarGridSpec(
            num_scalar_prefetch=1,
            grid=(1,),
            in_specs=[
                pl.BlockSpec((16, HD), lambda i, p: (p[0] // CUTS, p[0] % CUTS)),
                pl.BlockSpec((8, HD), lambda i, p: (2 * CUTS + p[0] // (2 * CUTS), p[0] % CUTS)),
            ],
            out_specs=pl.BlockSpec((DEPTH, ROWS, HD), lambda i, p: (0, 0, 0)),
        ),
        out_shape=jax.ShapeDtypeStruct((DEPTH, ROWS, HD), BF16),
        name="cut_out",
    )(place, shard, shard)


def spread_kernel(place_ref, pieces_ref, out_ref, paired):
    count = pieces_ref.shape[0]

    @pl.when(pl.program_id(0) == 0)
    def _():
        flip = place_ref[0] // CUTS % 2
        upper = iota((8, HD), 0) // 4 == flip
        for z in range(0, count, 2):
            even, odd = ((z + i + count // 2) % count for i in range(2))
            turned = pltpu.roll(pieces_ref[odd, 16:, :].astype(F32), 4, 0)
            mixed = jnp.where(upper, pieces_ref[even, 16:, :].astype(F32), turned)
            part = [pieces_ref[even, :16, :].astype(F32), pieces_ref[odd, :16, :].astype(F32), mixed]
            paired[20 * z : 20 * z + 40, :] = jnp.concatenate(part, axis=0)

    for at in range(out_ref.shape[0]):
        out_ref[at] = paired[...].astype(BF16)


def spread(place, pieces):
    steps = 4
    rows = pieces.shape[0] * 20
    return pl.pallas_call(
        spread_kernel,
        grid_spec=pltpu.PrefetchScalarGridSpec(
            num_scalar_prefetch=1,
            grid=(steps,),
            in_specs=[pl.BlockSpec(pieces.shape, lambda m, *_: (0, 0, 0))],
            out_specs=pl.BlockSpec((PLANE // steps, rows, HD), lambda m, *_: (m, 0, 0)),
            scratch_shapes=[pltpu.VMEM((rows, HD), F32)],
        ),
        out_shape=jax.ShapeDtypeStruct((PLANE, rows, HD), BF16),
        compiler_params=pltpu.CompilerParams(vmem_limit_bytes=24 * 2**20),
        name="spread",
    )(place, pieces)


def project_kernel(core_ref, rows_ref, own_ref, other_ref, out_ref, whole):
    core = core_ref[0]
    pairs = own_ref.shape[1] // 40
    shard = whole.shape[0] // (4 * pairs)
    upper = iota((8, HD), 0) < 4
    for source, parity in ((own_ref, core), (other_ref, 1 - core)):
        for pair in range(pairs):

            def put(odd, start, k, value):
                at = pl.multiple_of((4 * pair + 2 * odd + parity) * shard + start, 16)
                whole[pl.ds(at, 16), k * HD : (k + 1) * HD] = value

            for k in range(CUTS):
                tiles = []
                for cut in range(CUTS):
                    piece = source[cut * CUTS + k, 40 * pair : 40 * pair + 32, :]
                    put(0, 16 * cut, k, piece[:16])
                    put(1, 16 * cut, k, piece[16:])
                    tiles.append(source[cut * CUTS + k, 40 * pair + 32 : 40 * pair + 40, :].astype(F32))
                evens = [jnp.where(upper, tiles[i], tiles[i + 1]) for i in (0, 2)]
                odds = [pltpu.roll(jnp.where(upper, tiles[i + 1], tiles[i]), 4, 0) for i in (0, 2)]
                put(0, 16 * CUTS, k, jnp.concatenate(evens, axis=0).astype(BF16))
                put(1, 16 * CUTS, k, jnp.concatenate(odds, axis=0).astype(BF16))
    out_ref[...] = lax.dot_general(
        rows_ref[...], whole[...], ON_COLUMNS, preferred_element_type=F32
    ).astype(BF16)


def project_back(core, row_grads, own, other, features):
    tok, width = row_grads.shape
    steps = 4
    pieces = pl.BlockSpec((PLANE, own.shape[1] // steps, HD), lambda m, *_: (0, m, 0))
    return pl.pallas_call(
        project_kernel,
        grid_spec=pltpu.PrefetchScalarGridSpec(
            num_scalar_prefetch=1,
            grid=(steps,),
            in_specs=[pl.BlockSpec((tok, width), lambda m, *_: (0, 0)), pieces, pieces],
            out_specs=pl.BlockSpec((tok, features // steps), lambda m, *_: (0, m)),
            scratch_shapes=[pltpu.VMEM((features // steps, width), BF16)],
        ),
        out_shape=jax.ShapeDtypeStruct((tok, features), BF16),
        compiler_params=pltpu.CompilerParams(vmem_limit_bytes=24 * 2**20),
        name="project_back",
    )(core, row_grads, own, other)


def plane_exchange(pieces):
    groups = [list(range(half * PLANE, (half + 1) * PLANE)) for half in range(2)]
    return lax.all_to_all(pieces, "dp", 0, 0, axis_index_groups=groups)


def depth_gather(copies):
    groups = [[2 * ((z + DEPTH // 2) % DEPTH) + core for z in range(DEPTH)] for core in range(2)]
    return lax.all_to_all(copies, "fsdp", 0, 0, axis_index_groups=groups)


def planes_exchange(pieces):
    count = 2 * DEPTH
    groups = [
        [(half * PLANE + at) * count + 2 * (z + odd) + core for at in range(PLANE) for odd in range(2)]
        for half in range(2)
        for z in range(0, DEPTH, 2)
        for core in range(2)
    ]
    return lax.all_to_all(pieces, BOTH, 0, 0, axis_index_groups=groups)


def depth_exchange(pieces):
    count = 2 * DEPTH
    groups = [
        [(half * PLANE + at) * count + 2 * z + core for half in (1, 0) for z in range(odd, DEPTH, 2)]
        for at in range(PLANE)
        for odd in range(2)
        for core in range(2)
    ]
    return lax.all_to_all(pieces, BOTH, 0, 0, axis_index_groups=groups)


def local(activations, value_weight, queries, key_rows, context_grad, segment, send_slot):
    tok, features = activations.shape
    block = (queries.shape[0] - tok) // SECTIONS
    half = lax.axis_size("dp") // 2
    place = (lax.axis_index("dp") % PLANE).astype(jnp.int32).reshape(1)
    core = (lax.axis_index("fsdp") % 2).astype(jnp.int32).reshape(1)
    later = (lax.axis_index("fsdp") // 4 % 2).astype(jnp.int32).reshape(1)

    first, second = messages(queries, key_rows, context_grad, tok, block)
    first = swapped(first, "dp", half)
    second = swapped(second, "dp", half // 2)
    copies = spread(place, depth_gather(cut_out(value_weight, place)))

    def beside(held):
        copies, _, act = held
        return plane_exchange(copies), attend(queries, key_rows, context_grad, segment), swapped(act, "fsdp", 1)

    held = (copies, jnp.zeros((tok, WIDTH), BF16), activations)
    own_weight, main, other_act = lax.cond(
        lax.axis_index("dp") < lax.axis_size("dp"), beside, lambda held: held, held
    )
    main, own_weight = lax.optimization_barrier((main, own_weight))

    row_grads = own_rows(send_slot, main, first, second, block)
    other_rows = swapped(row_grads, "fsdp", 1)
    parts = planes_exchange(gradient_pieces(core, row_grads, other_rows, activations, other_act))
    other_weight = swapped(own_weight, "fsdp", 1)
    depth_parts = depth_exchange(plane_sum(parts))
    input_grad = project_back(core, row_grads, own_weight, other_weight, features)
    depth_parts, input_grad = lax.optimization_barrier((depth_parts, input_grad))
    finished = jnp.sum(depth_parts.astype(F32), axis=0).astype(BF16)
    finished = plane_exchange(jnp.broadcast_to(finished[None], (PLANE, *finished.shape)))
    weight_grad = join(later, finished, value_weight.shape[0])
    return (input_grad, weight_grad)


def solution(mesh):
    rows = P(("dp", "fsdp"), None)
    flat = P(("dp", "fsdp"))
    return jax.shard_map(
        local,
        mesh=mesh,
        in_specs=(rows, P("fsdp", None), rows, rows, rows, flat, flat),
        out_specs=(rows, P("fsdp", None)),
        check_vma=False,
    )
```

```python
import functools
import math

import jax
import jax.numpy as jnp
from jax import lax
from jax.experimental import pallas as pl
from jax.experimental.pallas import tpu as pltpu
from jax.sharding import PartitionSpec as P

KVH = 4
GROUP = 5
HD = 128
SECTIONS = 2
LEAST = 16
PLANE = 16
DEPTH = 16
CUTS = 4
ROWS = 24
BOTH = ("dp", "fsdp")
BF16 = jnp.bfloat16
F32 = jnp.float32
WIDTH = KVH * HD
FEATURES = KVH * GROUP * HD
LATE = GROUP * LEAST
SUMS = FEATURES
PROBS = SUMS + WIDTH
MESSAGE = PROBS + 2 * KVH * LATE
SCALE = 1.0 / math.sqrt(HD)
ON_COLUMNS = (((1,), (1,)), ((), ()))


def swapped(block, axis, distance):
    route = [(low, low ^ distance) for low in range(lax.axis_size(axis))]
    return lax.ppermute(block, axis, route)


def softmax_down(scores, allowed):
    masked = jnp.where(allowed, scores * SCALE, -jnp.inf)
    exponent = jnp.exp(masked - jnp.max(masked, axis=0, keepdims=True))
    return exponent * (1.0 / jnp.sum(exponent, axis=0, keepdims=True))


def iota(shape, dim):
    return lax.broadcasted_iota(jnp.int32, shape, dim)


def message_kernel(block, q_ref, k_ref, c_ref, *out_refs):
    for section, out_ref in enumerate(out_refs):
        low = section * block
        out_ref[:, :FEATURES] = c_ref[low + LEAST : low + block, :]
        pad = jnp.zeros((HD - LATE, HD), BF16)
        late = []
        for h in range(KVH):

            def stacked(ref, start):
                heads = [ref[start : start + LEAST, (h * GROUP + g) * HD : (h * GROUP + g + 1) * HD] for g in range(GROUP)]
                return jnp.concatenate([*heads, pad], axis=0)

            keys = k_ref[low : low + block, h * HD : (h + 1) * HD]
            scores = lax.dot_general(keys, stacked(q_ref, low + LEAST), ON_COLUMNS, preferred_element_type=F32)
            allowed = iota((block, HD), 0) <= iota((block, HD), 1) % LEAST + LEAST
            late.append(softmax_down(scores, allowed)[:, :LATE])

            scores = lax.dot_general(keys[:LEAST], stacked(q_ref, low), ON_COLUMNS, preferred_element_type=F32)
            allowed = iota((LEAST, HD), 0) <= iota((LEAST, HD), 1) % LEAST
            probs = softmax_down(scores, allowed).astype(BF16)
            sums = jnp.dot(probs, stacked(c_ref, low), preferred_element_type=F32)
            out_ref[:, SUMS + h * HD : SUMS + (h + 1) * HD] = sums.astype(BF16)
        late = [x[start : start + LEAST] for start in range(0, block, LEAST) for x in late]
        out_ref[:, PROBS:] = jnp.concatenate(late, axis=1).astype(BF16)


def messages(queries, key_rows, context_grad, tok, block):
    both = SECTIONS * block
    last = tok // both
    specs = [pl.BlockSpec((both, x.shape[1]), lambda i: (last, 0)) for x in (queries, key_rows, context_grad)]
    shape = (block - LEAST, MESSAGE)
    return pl.pallas_call(
        functools.partial(message_kernel, block),
        grid=(1,),
        in_specs=specs,
        out_specs=[pl.BlockSpec(shape, lambda i: (0, 0))] * SECTIONS,
        out_shape=[jax.ShapeDtypeStruct(shape, BF16)] * SECTIONS,
        compiler_params=pltpu.CompilerParams(vmem_limit_bytes=24 * 2**20),
        name="messages",
    )(queries, key_rows, context_grad)


def sent_block(slot, message_ref, low, block):
    inside = (slot >= low) & (slot < low + block)
    count = jnp.sum(inside.astype(jnp.int32), axis=0, keepdims=True)
    held = iota((block, HD), 1) % LEAST + LEAST < count
    pad = jnp.zeros((HD - LATE, HD), BF16)
    late = message_ref[:, PROBS:].astype(F32)
    heads = []
    for h in range(KVH):
        parts = [late[:, (half * KVH + h) * LATE : (half * KVH + h + 1) * LATE] for half in range(block // LEAST)]
        probs = jnp.concatenate(parts, axis=0)
        probs = jnp.concatenate([probs, jnp.zeros((block, HD - LATE), F32)], axis=1)
        probs = jnp.where(held, probs, 0.0).astype(BF16)
        rows = [message_ref[:, (h * GROUP + g) * HD : (h * GROUP + g + 1) * HD] for g in range(GROUP)]
        sums = jnp.dot(probs, jnp.concatenate([*rows, pad], axis=0), preferred_element_type=F32)
        early = message_ref[:, SUMS + h * HD : SUMS + (h + 1) * HD].astype(F32)
        heads.append(sums + jnp.concatenate([early, jnp.zeros((block - LEAST, HD), F32)], axis=0))
    return jnp.concatenate(heads, axis=1).astype(BF16)


def attend_kernel(col_ref, row_ref, q_ref, k_ref, c_ref, out_ref):
    tok = q_ref.shape[0]
    query = jnp.concatenate([q_ref[:, g * HD : (g + 1) * HD] for g in range(GROUP)], axis=0)
    context = jnp.concatenate([c_ref[:, g * HD : (g + 1) * HD] for g in range(GROUP)], axis=0)
    allowed = (col_ref[...] == row_ref[...]) & (iota((tok, tok), 0) <= iota((tok, tok), 1))
    bias = jnp.where(allowed, 0.0, -jnp.inf)
    scores = lax.dot_general(k_ref[...], query, ON_COLUMNS, preferred_element_type=F32) * SCALE
    masked = scores + jnp.concatenate([bias] * GROUP, axis=1)
    exponent = jnp.exp(masked - jnp.max(masked, axis=0, keepdims=True))
    probs = (exponent * (1.0 / jnp.sum(exponent, axis=0, keepdims=True))).astype(BF16)
    out_ref[...] = jnp.dot(probs, context, preferred_element_type=F32).astype(BF16)


def attend(queries, key_rows, context_grad, segment):
    tok = segment.shape[0]
    wide = pl.BlockSpec((tok, GROUP * HD), lambda h: (0, h))
    thin = pl.BlockSpec((tok, HD), lambda h: (0, h))
    return pl.pallas_call(
        attend_kernel,
        grid=(KVH,),
        in_specs=[
            pl.BlockSpec((tok, 1), lambda h: (0, 0)),
            pl.BlockSpec((1, tok), lambda h: (0, 0)),
            wide,
            thin,
            wide,
        ],
        out_specs=thin,
        out_shape=jax.ShapeDtypeStruct((tok, WIDTH), BF16),
        name="attend",
    )(segment.reshape(tok, 1), segment.reshape(1, tok), queries, key_rows, context_grad)


def rows_kernel(block, slot_ref, main_ref, second_ref, first_ref, out_ref):
    slot = slot_ref[...]
    tok = slot.shape[0]
    parts = [sent_block(slot, ref, tok + s * block, block) for s, ref in enumerate((first_ref, second_ref))]
    held = jnp.concatenate([main_ref[...], *parts], axis=0)
    chosen = (slot == iota((tok, held.shape[0]), 1)).astype(F32).astype(BF16)
    out_ref[...] = jnp.dot(chosen, held, preferred_element_type=F32).astype(BF16)


def own_rows(send_slot, main, first, second, block):
    tok = main.shape[0]
    operands = (send_slot.reshape(tok, 1), main, second, first)
    return pl.pallas_call(
        functools.partial(rows_kernel, block),
        grid=(1,),
        in_specs=[pl.BlockSpec(x.shape, lambda i: (0, 0)) for x in operands],
        out_specs=pl.BlockSpec(main.shape, lambda i: (0, 0)),
        out_shape=jax.ShapeDtypeStruct(main.shape, BF16),
        compiler_params=pltpu.CompilerParams(vmem_limit_bytes=24 * 2**20),
        name="own_rows",
    )(*operands)


def gradient_kernel(core_ref, rows_ref, other_rows_ref, act_ref, other_act_ref, out_ref, whole):
    whole[...] = lax.dot_general(
        jnp.concatenate([act_ref[...], other_act_ref[...]], axis=0),
        jnp.concatenate([rows_ref[...], other_rows_ref[...]], axis=0),
        (((0,), (0,)), ((), ())),
        preferred_element_type=F32,
    )
    core = core_ref[0]
    quads = out_ref.shape[1] // 40
    shard = whole.shape[0] // (8 * quads)
    upper = iota((8, WIDTH), 0) < 4
    for quad in range(quads):
        for parity in range(2):

            def rows(later, start, size):
                at = (2 * (4 * quad + 2 * later + parity) + core) * shard + start
                return whole[pl.ds(pl.multiple_of(at, 8), size), :]

            for cut in range(CUTS):
                split = 16 * CUTS + 8 * (cut // 2)
                one, two = rows(0, split, 8), pltpu.roll(rows(1, split, 8), 4, 0)
                mixed = jnp.where(upper, one, two) if cut % 2 == 0 else jnp.where(upper, two, one)
                piece = jnp.concatenate([rows(0, 16 * cut, 16), rows(1, 16 * cut, 16), mixed], axis=0).astype(BF16)
                for k in range(CUTS):
                    target = 2 * (cut * CUTS + k) + parity
                    out_ref[target, 40 * quad : 40 * quad + 40, :] = piece[:, k * HD : (k + 1) * HD]


def gradient_pieces(core, rows, other_rows, activations, other_activations):
    tok, features = activations.shape
    steps = 2
    held = pl.BlockSpec((tok, WIDTH), lambda m, *_: (0, 0))
    columns = pl.BlockSpec((tok, features // steps), lambda m, *_: (0, m))
    return pl.pallas_call(
        gradient_kernel,
        grid_spec=pltpu.PrefetchScalarGridSpec(
            num_scalar_prefetch=1,
            grid=(steps,),
            in_specs=[held, held, columns, columns],
            out_specs=pl.BlockSpec((2 * PLANE, 10 * DEPTH // steps, HD), lambda m, *_: (0, m, 0)),
            scratch_shapes=[pltpu.VMEM((features // steps, WIDTH), F32)],
        ),
        out_shape=jax.ShapeDtypeStruct((2 * PLANE, 10 * DEPTH, HD), BF16),
        compiler_params=pltpu.CompilerParams(vmem_limit_bytes=24 * 2**20),
        name="gradient_pieces",
    )(core, rows, other_rows, activations, other_activations)


def plane_sum_kernel(parts_ref, out_ref):
    count = out_ref.shape[0] // 2
    for pair in range(count // 2):
        total = jnp.sum(parts_ref[:, 40 * pair : 40 * pair + 40, :].astype(F32), axis=0)
        for later in range(2):
            piece = jnp.concatenate([total[16 * later : 16 * later + 16], total[32:]], axis=0).astype(BF16)
            for half in range(2):
                out_ref[half * count + 2 * pair + later] = piece


def plane_sum(parts):
    _, rows, lanes = parts.shape
    out = (rows // 10, ROWS, lanes)
    return pl.pallas_call(
        plane_sum_kernel,
        grid=(1,),
        in_specs=[pl.BlockSpec(parts.shape, lambda i: (0, 0, 0))],
        out_specs=pl.BlockSpec(out, lambda i: (0, 0, 0)),
        out_shape=jax.ShapeDtypeStruct(out, BF16),
        compiler_params=pltpu.CompilerParams(vmem_limit_bytes=24 * 2**20),
        name="plane_sum",
    )(parts)


def join_kernel(later_ref, pieces_ref, out_ref):
    later = later_ref[0]
    upper = iota((8, HD), 0) < 4
    for k in range(CUTS):
        lanes = slice(k * HD, (k + 1) * HD)
        tiles = []
        for cut in range(CUTS):
            out_ref[16 * cut : 16 * cut + 16, lanes] = pieces_ref[cut * CUTS + k, :16, :]
            tiles.append(pieces_ref[cut * CUTS + k, 16:, :].astype(F32))
        last = []
        for low, high in ((tiles[0], tiles[1]), (tiles[2], tiles[3])):
            turned = pltpu.roll(jnp.where(upper, high, low), 4, 0)
            last.append(jnp.where(later == 1, turned, jnp.where(upper, low, high)))
        out_ref[16 * CUTS :, lanes] = jnp.concatenate(last, axis=0).astype(BF16)


def join(later, pieces, rows):
    return pl.pallas_call(
        join_kernel,
        grid_spec=pltpu.PrefetchScalarGridSpec(
            num_scalar_prefetch=1,
            grid=(1,),
            in_specs=[pl.BlockSpec(pieces.shape, lambda i, *_: (0, 0, 0))],
            out_specs=pl.BlockSpec((rows, WIDTH), lambda i, *_: (0, 0)),
        ),
        out_shape=jax.ShapeDtypeStruct((rows, WIDTH), BF16),
        compiler_params=pltpu.CompilerParams(vmem_limit_bytes=24 * 2**20),
        name="join",
    )(later, pieces)


def cut_kernel(place_ref, rows_ref, tile_ref, out_ref):
    del place_ref
    for at in range(out_ref.shape[0]):
        out_ref[at, :16, :] = rows_ref[...]
        out_ref[at, 16:, :] = tile_ref[...]


def cut_out(shard, place):
    return pl.pallas_call(
        cut_kernel,
        grid_spec=pltpu.PrefetchScalarGridSpec(
            num_scalar_prefetch=1,
            grid=(1,),
            in_specs=[
                pl.BlockSpec((16, HD), lambda i, p: (p[0] // CUTS, p[0] % CUTS)),
                pl.BlockSpec((8, HD), lambda i, p: (2 * CUTS + p[0] // (2 * CUTS), p[0] % CUTS)),
            ],
            out_specs=pl.BlockSpec((DEPTH, ROWS, HD), lambda i, p: (0, 0, 0)),
        ),
        out_shape=jax.ShapeDtypeStruct((DEPTH, ROWS, HD), BF16),
        name="cut_out",
    )(place, shard, shard)


def spread_kernel(place_ref, pieces_ref, out_ref, paired):
    count = pieces_ref.shape[0]

    @pl.when(pl.program_id(0) == 0)
    def _():
        flip = place_ref[0] // CUTS % 2
        upper = iota((8, HD), 0) // 4 == flip
        for z in range(0, count, 2):
            even, odd = ((z + i + count // 2) % count for i in range(2))
            turned = pltpu.roll(pieces_ref[odd, 16:, :].astype(F32), 4, 0)
            mixed = jnp.where(upper, pieces_ref[even, 16:, :].astype(F32), turned)
            part = [pieces_ref[even, :16, :].astype(F32), pieces_ref[odd, :16, :].astype(F32), mixed]
            paired[20 * z : 20 * z + 40, :] = jnp.concatenate(part, axis=0)

    for at in range(out_ref.shape[0]):
        out_ref[at] = paired[...].astype(BF16)


def spread(place, pieces):
    steps = 4
    rows = pieces.shape[0] * 20
    return pl.pallas_call(
        spread_kernel,
        grid_spec=pltpu.PrefetchScalarGridSpec(
            num_scalar_prefetch=1,
            grid=(steps,),
            in_specs=[pl.BlockSpec(pieces.shape, lambda m, *_: (0, 0, 0))],
            out_specs=pl.BlockSpec((PLANE // steps, rows, HD), lambda m, *_: (m, 0, 0)),
            scratch_shapes=[pltpu.VMEM((rows, HD), F32)],
        ),
        out_shape=jax.ShapeDtypeStruct((PLANE, rows, HD), BF16),
        compiler_params=pltpu.CompilerParams(vmem_limit_bytes=24 * 2**20),
        name="spread",
    )(place, pieces)


def project_kernel(core_ref, rows_ref, own_ref, other_ref, out_ref, whole):
    core = core_ref[0]
    pairs = own_ref.shape[1] // 40
    shard = whole.shape[0] // (4 * pairs)
    upper = iota((8, HD), 0) < 4
    for source, parity in ((own_ref, core), (other_ref, 1 - core)):
        for pair in range(pairs):

            def put(odd, start, k, value):
                at = pl.multiple_of((4 * pair + 2 * odd + parity) * shard + start, 16)
                whole[pl.ds(at, 16), k * HD : (k + 1) * HD] = value

            for k in range(CUTS):
                tiles = []
                for cut in range(CUTS):
                    piece = source[cut * CUTS + k, 40 * pair : 40 * pair + 32, :]
                    put(0, 16 * cut, k, piece[:16])
                    put(1, 16 * cut, k, piece[16:])
                    tiles.append(source[cut * CUTS + k, 40 * pair + 32 : 40 * pair + 40, :].astype(F32))
                evens = [jnp.where(upper, tiles[i], tiles[i + 1]) for i in (0, 2)]
                odds = [pltpu.roll(jnp.where(upper, tiles[i + 1], tiles[i]), 4, 0) for i in (0, 2)]
                put(0, 16 * CUTS, k, jnp.concatenate(evens, axis=0).astype(BF16))
                put(1, 16 * CUTS, k, jnp.concatenate(odds, axis=0).astype(BF16))
    out_ref[...] = lax.dot_general(
        rows_ref[...], whole[...], ON_COLUMNS, preferred_element_type=F32
    ).astype(BF16)


def project_back(core, row_grads, own, other, features):
    tok, width = row_grads.shape
    steps = 4
    pieces = pl.BlockSpec((PLANE, own.shape[1] // steps, HD), lambda m, *_: (0, m, 0))
    return pl.pallas_call(
        project_kernel,
        grid_spec=pltpu.PrefetchScalarGridSpec(
            num_scalar_prefetch=1,
            grid=(steps,),
            in_specs=[pl.BlockSpec((tok, width), lambda m, *_: (0, 0)), pieces, pieces],
            out_specs=pl.BlockSpec((tok, features // steps), lambda m, *_: (0, m)),
            scratch_shapes=[pltpu.VMEM((features // steps, width), BF16)],
        ),
        out_shape=jax.ShapeDtypeStruct((tok, features), BF16),
        compiler_params=pltpu.CompilerParams(vmem_limit_bytes=24 * 2**20),
        name="project_back",
    )(core, row_grads, own, other)


def plane_exchange(pieces):
    groups = [list(range(half * PLANE, (half + 1) * PLANE)) for half in range(2)]
    return lax.all_to_all(pieces, "dp", 0, 0, axis_index_groups=groups)


def depth_gather(copies):
    groups = [[2 * ((z + DEPTH // 2) % DEPTH) + core for z in range(DEPTH)] for core in range(2)]
    return lax.all_to_all(copies, "fsdp", 0, 0, axis_index_groups=groups)


def planes_exchange(pieces):
    count = 2 * DEPTH
    groups = [
        [(half * PLANE + at) * count + 2 * (z + odd) + core for at in range(PLANE) for odd in range(2)]
        for half in range(2)
        for z in range(0, DEPTH, 2)
        for core in range(2)
    ]
    return lax.all_to_all(pieces, BOTH, 0, 0, axis_index_groups=groups)


def depth_exchange(pieces):
    count = 2 * DEPTH
    groups = [
        [(half * PLANE + at) * count + 2 * z + core for half in (1, 0) for z in range(odd, DEPTH, 2)]
        for at in range(PLANE)
        for odd in range(2)
        for core in range(2)
    ]
    return lax.all_to_all(pieces, BOTH, 0, 0, axis_index_groups=groups)


def local(activations, value_weight, queries, key_rows, context_grad, segment, send_slot):
    tok, features = activations.shape
    block = (queries.shape[0] - tok) // SECTIONS
    half = lax.axis_size("dp") // 2
    place = (lax.axis_index("dp") % PLANE).astype(jnp.int32).reshape(1)
    core = (lax.axis_index("fsdp") % 2).astype(jnp.int32).reshape(1)
    later = (lax.axis_index("fsdp") // 4 % 2).astype(jnp.int32).reshape(1)

    first, second = messages(queries, key_rows, context_grad, tok, block)
    second = swapped(second, "dp", half // 2)
    first = swapped(first, "dp", half)
    copies = spread(place, depth_gather(cut_out(value_weight, place)))

    def beside(held):
        copies, _, act = held
        return plane_exchange(copies), attend(queries, key_rows, context_grad, segment), swapped(act, "fsdp", 1)

    held = (copies, jnp.zeros((tok, WIDTH), BF16), activations)
    own_weight, main, other_act = lax.cond(
        lax.axis_index("dp") < lax.axis_size("dp"), beside, lambda held: held, held
    )
    main, own_weight = lax.optimization_barrier((main, own_weight))

    row_grads = own_rows(send_slot, main, first, second, block)
    other_rows = swapped(row_grads, "fsdp", 1)
    parts = planes_exchange(gradient_pieces(core, row_grads, other_rows, activations, other_act))
    other_weight = swapped(own_weight, "fsdp", 1)
    depth_parts = depth_exchange(plane_sum(parts))
    input_grad = project_back(core, row_grads, own_weight, other_weight, features)
    depth_parts, input_grad = lax.optimization_barrier((depth_parts, input_grad))
    finished = jnp.sum(depth_parts.astype(F32), axis=0).astype(BF16)
    finished = plane_exchange(jnp.broadcast_to(finished[None], (PLANE, *finished.shape)))
    weight_grad = join(later, finished, value_weight.shape[0])
    return (input_grad, weight_grad)


def solution(mesh):
    rows = P(("dp", "fsdp"), None)
    flat = P(("dp", "fsdp"))
    return jax.shard_map(
        local,
        mesh=mesh,
        in_specs=(rows, P("fsdp", None), rows, rows, rows, flat, flat),
        out_specs=(rows, P("fsdp", None)),
        check_vma=False,
    )
```

```python
import functools
import math

import jax
import jax.numpy as jnp
from jax import lax
from jax.experimental import pallas as pl
from jax.experimental.pallas import tpu as pltpu
from jax.sharding import PartitionSpec as P

KVH = 4
GROUP = 5
HD = 128
SECTIONS = 2
LEAST = 16
PLANE = 16
DEPTH = 16
CUTS = 4
ROWS = 24
BOTH = ("dp", "fsdp")
BF16 = jnp.bfloat16
F32 = jnp.float32
WIDTH = KVH * HD
FEATURES = KVH * GROUP * HD
LATE = GROUP * LEAST
SUMS = FEATURES
PROBS = SUMS + WIDTH
MESSAGE = PROBS + 2 * KVH * LATE
SCALE = 1.0 / math.sqrt(HD)
ON_COLUMNS = (((1,), (1,)), ((), ()))


def swapped(block, axis, distance):
    route = [(low, low ^ distance) for low in range(lax.axis_size(axis))]
    return lax.ppermute(block, axis, route)


def softmax_down(scores, allowed):
    masked = jnp.where(allowed, scores * SCALE, -jnp.inf)
    exponent = jnp.exp(masked - jnp.max(masked, axis=0, keepdims=True))
    return exponent * (1.0 / jnp.sum(exponent, axis=0, keepdims=True))


def iota(shape, dim):
    return lax.broadcasted_iota(jnp.int32, shape, dim)


def message_kernel(block, q_ref, k_ref, c_ref, *out_refs):
    for section, out_ref in enumerate(out_refs):
        low = section * block
        out_ref[:, :FEATURES] = c_ref[low + LEAST : low + block, :]
        pad = jnp.zeros((HD - LATE, HD), BF16)
        late = []
        for h in range(KVH):

            def stacked(ref, start):
                heads = [ref[start : start + LEAST, (h * GROUP + g) * HD : (h * GROUP + g + 1) * HD] for g in range(GROUP)]
                return jnp.concatenate([*heads, pad], axis=0)

            keys = k_ref[low : low + block, h * HD : (h + 1) * HD]
            scores = lax.dot_general(keys, stacked(q_ref, low + LEAST), ON_COLUMNS, preferred_element_type=F32)
            allowed = iota((block, HD), 0) <= iota((block, HD), 1) % LEAST + LEAST
            late.append(softmax_down(scores, allowed)[:, :LATE])

            scores = lax.dot_general(keys[:LEAST], stacked(q_ref, low), ON_COLUMNS, preferred_element_type=F32)
            allowed = iota((LEAST, HD), 0) <= iota((LEAST, HD), 1) % LEAST
            probs = softmax_down(scores, allowed).astype(BF16)
            sums = jnp.dot(probs, stacked(c_ref, low), preferred_element_type=F32)
            out_ref[:, SUMS + h * HD : SUMS + (h + 1) * HD] = sums.astype(BF16)
        late = [x[start : start + LEAST] for start in range(0, block, LEAST) for x in late]
        out_ref[:, PROBS:] = jnp.concatenate(late, axis=1).astype(BF16)


def messages(queries, key_rows, context_grad, tok, block):
    both = SECTIONS * block
    last = tok // both
    specs = [pl.BlockSpec((both, x.shape[1]), lambda i: (last, 0)) for x in (queries, key_rows, context_grad)]
    shape = (block - LEAST, MESSAGE)
    return pl.pallas_call(
        functools.partial(message_kernel, block),
        grid=(1,),
        in_specs=specs,
        out_specs=[pl.BlockSpec(shape, lambda i: (0, 0))] * SECTIONS,
        out_shape=[jax.ShapeDtypeStruct(shape, BF16)] * SECTIONS,
        compiler_params=pltpu.CompilerParams(vmem_limit_bytes=24 * 2**20),
        name="messages",
    )(queries, key_rows, context_grad)


def sent_block(slot, message_ref, low, block):
    inside = (slot >= low) & (slot < low + block)
    count = jnp.sum(inside.astype(jnp.int32), axis=0, keepdims=True)
    held = iota((block, HD), 1) % LEAST + LEAST < count
    pad = jnp.zeros((HD - LATE, HD), BF16)
    late = message_ref[:, PROBS:].astype(F32)
    heads = []
    for h in range(KVH):
        parts = [late[:, (half * KVH + h) * LATE : (half * KVH + h + 1) * LATE] for half in range(block // LEAST)]
        probs = jnp.concatenate(parts, axis=0)
        probs = jnp.concatenate([probs, jnp.zeros((block, HD - LATE), F32)], axis=1)
        probs = jnp.where(held, probs, 0.0).astype(BF16)
        rows = [message_ref[:, (h * GROUP + g) * HD : (h * GROUP + g + 1) * HD] for g in range(GROUP)]
        sums = jnp.dot(probs, jnp.concatenate([*rows, pad], axis=0), preferred_element_type=F32)
        early = message_ref[:, SUMS + h * HD : SUMS + (h + 1) * HD].astype(F32)
        heads.append(sums + jnp.concatenate([early, jnp.zeros((block - LEAST, HD), F32)], axis=0))
    return jnp.concatenate(heads, axis=1).astype(BF16)


def attend_kernel(col_ref, row_ref, q_ref, k_ref, c_ref, out_ref):
    tok = q_ref.shape[0]
    query = jnp.concatenate([q_ref[:, g * HD : (g + 1) * HD] for g in range(GROUP)], axis=0)
    context = jnp.concatenate([c_ref[:, g * HD : (g + 1) * HD] for g in range(GROUP)], axis=0)
    allowed = (col_ref[...] == row_ref[...]) & (iota((tok, tok), 0) <= iota((tok, tok), 1))
    bias = jnp.where(allowed, 0.0, -jnp.inf)
    scores = lax.dot_general(k_ref[...], query, ON_COLUMNS, preferred_element_type=F32) * SCALE
    masked = scores + jnp.concatenate([bias] * GROUP, axis=1)
    exponent = jnp.exp(masked - jnp.max(masked, axis=0, keepdims=True))
    probs = (exponent * (1.0 / jnp.sum(exponent, axis=0, keepdims=True))).astype(BF16)
    out_ref[...] = jnp.dot(probs, context, preferred_element_type=F32).astype(BF16)


def attend(queries, key_rows, context_grad, segment):
    tok = segment.shape[0]
    wide = pl.BlockSpec((tok, GROUP * HD), lambda h: (0, h))
    thin = pl.BlockSpec((tok, HD), lambda h: (0, h))
    return pl.pallas_call(
        attend_kernel,
        grid=(KVH,),
        in_specs=[
            pl.BlockSpec((tok, 1), lambda h: (0, 0)),
            pl.BlockSpec((1, tok), lambda h: (0, 0)),
            wide,
            thin,
            wide,
        ],
        out_specs=thin,
        out_shape=jax.ShapeDtypeStruct((tok, WIDTH), BF16),
        name="attend",
    )(segment.reshape(tok, 1), segment.reshape(1, tok), queries, key_rows, context_grad)


def rows_kernel(block, slot_ref, main_ref, second_ref, first_ref, out_ref):
    slot = slot_ref[...]
    tok = slot.shape[0]
    parts = [sent_block(slot, ref, tok + s * block, block) for s, ref in enumerate((first_ref, second_ref))]
    held = jnp.concatenate([main_ref[...], *parts], axis=0)
    chosen = (slot == iota((tok, held.shape[0]), 1)).astype(F32).astype(BF16)
    out_ref[...] = jnp.dot(chosen, held, preferred_element_type=F32).astype(BF16)


def own_rows(send_slot, main, first, second, block):
    tok = main.shape[0]
    operands = (send_slot.reshape(tok, 1), main, second, first)
    return pl.pallas_call(
        functools.partial(rows_kernel, block),
        grid=(1,),
        in_specs=[pl.BlockSpec(x.shape, lambda i: (0, 0)) for x in operands],
        out_specs=pl.BlockSpec(main.shape, lambda i: (0, 0)),
        out_shape=jax.ShapeDtypeStruct(main.shape, BF16),
        compiler_params=pltpu.CompilerParams(vmem_limit_bytes=24 * 2**20),
        name="own_rows",
    )(*operands)


def gradient_kernel(core_ref, rows_ref, other_rows_ref, act_ref, other_act_ref, out_ref, whole):
    whole[...] = lax.dot_general(
        jnp.concatenate([act_ref[...], other_act_ref[...]], axis=0),
        jnp.concatenate([rows_ref[...], other_rows_ref[...]], axis=0),
        (((0,), (0,)), ((), ())),
        preferred_element_type=F32,
    )
    core = core_ref[0]
    quads = out_ref.shape[1] // 40
    shard = whole.shape[0] // (8 * quads)
    upper = iota((8, WIDTH), 0) < 4
    for quad in range(quads):
        for parity in range(2):

            def rows(later, start, size):
                at = (2 * (4 * quad + 2 * later + parity) + core) * shard + start
                return whole[pl.ds(pl.multiple_of(at, 8), size), :]

            for cut in range(CUTS):
                split = 16 * CUTS + 8 * (cut // 2)
                one, two = rows(0, split, 8), pltpu.roll(rows(1, split, 8), 4, 0)
                mixed = jnp.where(upper, one, two) if cut % 2 == 0 else jnp.where(upper, two, one)
                piece = jnp.concatenate([rows(0, 16 * cut, 16), rows(1, 16 * cut, 16), mixed], axis=0).astype(BF16)
                for k in range(CUTS):
                    target = 2 * (cut * CUTS + k) + parity
                    out_ref[target, 40 * quad : 40 * quad + 40, :] = piece[:, k * HD : (k + 1) * HD]


def gradient_pieces(core, rows, other_rows, activations, other_activations):
    tok, features = activations.shape
    steps = 2
    held = pl.BlockSpec((tok, WIDTH), lambda m, *_: (0, 0))
    columns = pl.BlockSpec((tok, features // steps), lambda m, *_: (0, m))
    return pl.pallas_call(
        gradient_kernel,
        grid_spec=pltpu.PrefetchScalarGridSpec(
            num_scalar_prefetch=1,
            grid=(steps,),
            in_specs=[held, held, columns, columns],
            out_specs=pl.BlockSpec((2 * PLANE, 10 * DEPTH // steps, HD), lambda m, *_: (0, m, 0)),
            scratch_shapes=[pltpu.VMEM((features // steps, WIDTH), F32)],
        ),
        out_shape=jax.ShapeDtypeStruct((2 * PLANE, 10 * DEPTH, HD), BF16),
        compiler_params=pltpu.CompilerParams(vmem_limit_bytes=24 * 2**20),
        name="gradient_pieces",
    )(core, rows, other_rows, activations, other_activations)


def plane_sum_kernel(parts_ref, out_ref):
    count = out_ref.shape[0] // 2
    for pair in range(count // 2):
        total = jnp.sum(parts_ref[:, 40 * pair : 40 * pair + 40, :].astype(F32), axis=0)
        for later in range(2):
            piece = jnp.concatenate([total[16 * later : 16 * later + 16], total[32:]], axis=0).astype(BF16)
            for half in range(2):
                out_ref[half * count + 2 * pair + later] = piece


def plane_sum(parts):
    _, rows, lanes = parts.shape
    out = (rows // 10, ROWS, lanes)
    return pl.pallas_call(
        plane_sum_kernel,
        grid=(1,),
        in_specs=[pl.BlockSpec(parts.shape, lambda i: (0, 0, 0))],
        out_specs=pl.BlockSpec(out, lambda i: (0, 0, 0)),
        out_shape=jax.ShapeDtypeStruct(out, BF16),
        compiler_params=pltpu.CompilerParams(vmem_limit_bytes=24 * 2**20),
        name="plane_sum",
    )(parts)


def join_kernel(later_ref, pieces_ref, out_ref):
    later = later_ref[0]
    upper = iota((8, HD), 0) < 4
    for k in range(CUTS):
        lanes = slice(k * HD, (k + 1) * HD)
        tiles = []
        for cut in range(CUTS):
            out_ref[16 * cut : 16 * cut + 16, lanes] = pieces_ref[cut * CUTS + k, :16, :]
            tiles.append(pieces_ref[cut * CUTS + k, 16:, :].astype(F32))
        last = []
        for low, high in ((tiles[0], tiles[1]), (tiles[2], tiles[3])):
            turned = pltpu.roll(jnp.where(upper, high, low), 4, 0)
            last.append(jnp.where(later == 1, turned, jnp.where(upper, low, high)))
        out_ref[16 * CUTS :, lanes] = jnp.concatenate(last, axis=0).astype(BF16)


def join(later, pieces, rows):
    return pl.pallas_call(
        join_kernel,
        grid_spec=pltpu.PrefetchScalarGridSpec(
            num_scalar_prefetch=1,
            grid=(1,),
            in_specs=[pl.BlockSpec(pieces.shape, lambda i, *_: (0, 0, 0))],
            out_specs=pl.BlockSpec((rows, WIDTH), lambda i, *_: (0, 0)),
        ),
        out_shape=jax.ShapeDtypeStruct((rows, WIDTH), BF16),
        compiler_params=pltpu.CompilerParams(vmem_limit_bytes=24 * 2**20),
        name="join",
    )(later, pieces)


def cut_kernel(place_ref, rows_ref, tiles_ref, out_ref):
    tiles = tiles_ref[...].astype(F32)
    tile = jnp.where(place_ref[0] // (2 * CUTS) == 0, tiles[:8], tiles[8:]).astype(BF16)
    for at in range(out_ref.shape[0]):
        out_ref[at, :16, :] = rows_ref[...]
        out_ref[at, 16:, :] = tile


def cut_out(shard, place):
    return pl.pallas_call(
        cut_kernel,
        grid_spec=pltpu.PrefetchScalarGridSpec(
            num_scalar_prefetch=1,
            grid=(1,),
            in_specs=[
                pl.BlockSpec((16, HD), lambda i, p: (p[0] // CUTS, p[0] % CUTS)),
                pl.BlockSpec((16, HD), lambda i, p: (CUTS, p[0] % CUTS)),
            ],
            out_specs=pl.BlockSpec((DEPTH, ROWS, HD), lambda i, p: (0, 0, 0)),
        ),
        out_shape=jax.ShapeDtypeStruct((DEPTH, ROWS, HD), BF16),
        name="cut_out",
    )(place, shard, shard)


def spread_kernel(place_ref, pieces_ref, out_ref, paired):
    count = pieces_ref.shape[0]

    @pl.when(pl.program_id(0) == 0)
    def _():
        flip = place_ref[0] // CUTS % 2
        upper = iota((8, HD), 0) // 4 == flip
        for z in range(0, count, 2):
            even, odd = ((z + i + count // 2) % count for i in range(2))
            turned = pltpu.roll(pieces_ref[odd, 16:, :].astype(F32), 4, 0)
            mixed = jnp.where(upper, pieces_ref[even, 16:, :].astype(F32), turned)
            part = [pieces_ref[even, :16, :].astype(F32), pieces_ref[odd, :16, :].astype(F32), mixed]
            paired[20 * z : 20 * z + 40, :] = jnp.concatenate(part, axis=0)

    for at in range(out_ref.shape[0]):
        out_ref[at] = paired[...].astype(BF16)


def spread(place, pieces):
    steps = 4
    rows = pieces.shape[0] * 20
    return pl.pallas_call(
        spread_kernel,
        grid_spec=pltpu.PrefetchScalarGridSpec(
            num_scalar_prefetch=1,
            grid=(steps,),
            in_specs=[pl.BlockSpec(pieces.shape, lambda m, *_: (0, 0, 0))],
            out_specs=pl.BlockSpec((PLANE // steps, rows, HD), lambda m, *_: (m, 0, 0)),
            scratch_shapes=[pltpu.VMEM((rows, HD), F32)],
        ),
        out_shape=jax.ShapeDtypeStruct((PLANE, rows, HD), BF16),
        compiler_params=pltpu.CompilerParams(vmem_limit_bytes=24 * 2**20),
        name="spread",
    )(place, pieces)


def project_kernel(core_ref, rows_ref, own_ref, other_ref, out_ref, whole):
    core = core_ref[0]
    pairs = own_ref.shape[1] // 40
    shard = whole.shape[0] // (4 * pairs)
    upper = iota((8, HD), 0) < 4
    for source, parity in ((own_ref, core), (other_ref, 1 - core)):
        for pair in range(pairs):

            def put(odd, start, k, value):
                at = pl.multiple_of((4 * pair + 2 * odd + parity) * shard + start, 16)
                whole[pl.ds(at, 16), k * HD : (k + 1) * HD] = value

            for k in range(CUTS):
                tiles = []
                for cut in range(CUTS):
                    piece = source[cut * CUTS + k, 40 * pair : 40 * pair + 32, :]
                    put(0, 16 * cut, k, piece[:16])
                    put(1, 16 * cut, k, piece[16:])
                    tiles.append(source[cut * CUTS + k, 40 * pair + 32 : 40 * pair + 40, :].astype(F32))
                evens = [jnp.where(upper, tiles[i], tiles[i + 1]) for i in (0, 2)]
                odds = [pltpu.roll(jnp.where(upper, tiles[i + 1], tiles[i]), 4, 0) for i in (0, 2)]
                put(0, 16 * CUTS, k, jnp.concatenate(evens, axis=0).astype(BF16))
                put(1, 16 * CUTS, k, jnp.concatenate(odds, axis=0).astype(BF16))
    out_ref[...] = lax.dot_general(
        rows_ref[...], whole[...], ON_COLUMNS, preferred_element_type=F32
    ).astype(BF16)


def project_back(core, row_grads, own, other, features):
    tok, width = row_grads.shape
    steps = 4
    pieces = pl.BlockSpec((PLANE, own.shape[1] // steps, HD), lambda m, *_: (0, m, 0))
    return pl.pallas_call(
        project_kernel,
        grid_spec=pltpu.PrefetchScalarGridSpec(
            num_scalar_prefetch=1,
            grid=(steps,),
            in_specs=[pl.BlockSpec((tok, width), lambda m, *_: (0, 0)), pieces, pieces],
            out_specs=pl.BlockSpec((tok, features // steps), lambda m, *_: (0, m)),
            scratch_shapes=[pltpu.VMEM((features // steps, width), BF16)],
        ),
        out_shape=jax.ShapeDtypeStruct((tok, features), BF16),
        compiler_params=pltpu.CompilerParams(vmem_limit_bytes=24 * 2**20),
        name="project_back",
    )(core, row_grads, own, other)


def plane_exchange(pieces):
    groups = [list(range(half * PLANE, (half + 1) * PLANE)) for half in range(2)]
    return lax.all_to_all(pieces, "dp", 0, 0, axis_index_groups=groups)


def depth_gather(copies):
    groups = [[2 * ((z + DEPTH // 2) % DEPTH) + core for z in range(DEPTH)] for core in range(2)]
    return lax.all_to_all(copies, "fsdp", 0, 0, axis_index_groups=groups)


def planes_exchange(pieces):
    count = 2 * DEPTH
    groups = [
        [(half * PLANE + at) * count + 2 * (z + odd) + core for at in range(PLANE) for odd in range(2)]
        for half in range(2)
        for z in range(0, DEPTH, 2)
        for core in range(2)
    ]
    return lax.all_to_all(pieces, BOTH, 0, 0, axis_index_groups=groups)


def depth_exchange(pieces):
    count = 2 * DEPTH
    groups = [
        [(half * PLANE + at) * count + 2 * z + core for half in (1, 0) for z in range(odd, DEPTH, 2)]
        for at in range(PLANE)
        for odd in range(2)
        for core in range(2)
    ]
    return lax.all_to_all(pieces, BOTH, 0, 0, axis_index_groups=groups)


def local(activations, value_weight, queries, key_rows, context_grad, segment, send_slot):
    tok, features = activations.shape
    block = (queries.shape[0] - tok) // SECTIONS
    half = lax.axis_size("dp") // 2
    place = (lax.axis_index("dp") % PLANE).astype(jnp.int32).reshape(1)
    core = (lax.axis_index("fsdp") % 2).astype(jnp.int32).reshape(1)
    later = (lax.axis_index("fsdp") // 4 % 2).astype(jnp.int32).reshape(1)

    first, second = messages(queries, key_rows, context_grad, tok, block)
    second = swapped(second, "dp", half // 2)
    first = swapped(first, "dp", half)
    copies = spread(place, depth_gather(cut_out(value_weight, place)))

    def beside(held):
        copies, _, act = held
        return plane_exchange(copies), attend(queries, key_rows, context_grad, segment), swapped(act, "fsdp", 1)

    held = (copies, jnp.zeros((tok, WIDTH), BF16), activations)
    own_weight, main, other_act = lax.cond(
        lax.axis_index("dp") < lax.axis_size("dp"), beside, lambda held: held, held
    )
    main, own_weight = lax.optimization_barrier((main, own_weight))

    row_grads = own_rows(send_slot, main, first, second, block)
    other_rows = swapped(row_grads, "fsdp", 1)
    parts = planes_exchange(gradient_pieces(core, row_grads, other_rows, activations, other_act))
    other_weight = swapped(own_weight, "fsdp", 1)
    depth_parts = depth_exchange(plane_sum(parts))
    input_grad = project_back(core, row_grads, own_weight, other_weight, features)
    depth_parts, input_grad = lax.optimization_barrier((depth_parts, input_grad))
    finished = jnp.sum(depth_parts.astype(F32), axis=0).astype(BF16)
    finished = plane_exchange(jnp.broadcast_to(finished[None], (PLANE, *finished.shape)))
    weight_grad = join(later, finished, value_weight.shape[0])
    return (input_grad, weight_grad)


def solution(mesh):
    rows = P(("dp", "fsdp"), None)
    flat = P(("dp", "fsdp"))
    return jax.shard_map(
        local,
        mesh=mesh,
        in_specs=(rows, P("fsdp", None), rows, rows, rows, flat, flat),
        out_specs=(rows, P("fsdp", None)),
        check_vma=False,
    )
```
